256 devices in a mesh: md: 32 (over z, y_lo, core), cd: 8 (over x, y_hi).
Axes of the slice: x: 4, y: 4 (y_hi: 2, y_lo: 2; y = y_hi * 2 + y_lo), z: 8, core: 2. Of those that a mesh axis runs over, the one named last changes fastest.
Arguments:
- orientation: float32 [5, 16, 128, 8192], P(None, None, 'cd', 'md'), may hold values from 0.05 to 0.35
- velocity: float32 [3, 16, 128, 8192], P(None, None, 'cd', 'md'), may hold values from -3 to 3
- velocity_grad: float32 [9, 16, 128, 8192], P(None, None, 'cd', 'md'), may hold values from -3 to 3
- rotary: float32 [16, 128, 8192], P(None, 'cd', 'md'), may hold values from 0.05 to 0.5
- target: float32 [5, 16, 128, 8192], P(None, None, 'cd', 'md'), may hold values from 0 to 0.4
- needle_params: float32 [4096, 8, 16], P('md', 'cd'), may hold values from 0 to 0.2
- foot_start: int32 [4096, 8], P(None, 'cd'), may hold values from 0 to 8192, as said below
- foot_end: int32 [4096, 8], P(None, 'cd'), may hold values from 0 to 8192, as said below
- foot_column: int32 [4096, 8], P(None, 'cd'), may hold values from 0 to 15
Outputs:
- final_orientation: float32 [5, 16, 128, 8192], P(None, None, 'cd', 'md')
- initial_sensitivity: float32 [5, 16, 128, 8192], P(None, None, 'cd', 'md')
- needle_gradient: float32 [4096, 8, 16], P('md', 'cd')
The draws below stay inside these ranges and needn't reach their ends.
Inputs may be any that keep to these rules, and one draw needn't show every extreme that they name: foot_start[r, c] <= foot_end[r, c], and 2 r - 256 <= foot_start[r, c]. foot_end[r, c] <= 2 r + 256. Needle (r, c) lies in cross-direction cell c * 16 + foot_column[r, c].
All inputs are finite; a program needn't handle non-finite values.
Results may differ from the reference program's by a relative error of at most 0.0003.
Values sent between devices are 32-bit elements; how exact they have to be, the bound alone decides.
No kernel may reach another device: no remote copies, remote signals or barrier semaphores. Data moves between devices by JAX's collectives and lax.ppermute only.
A program may use at most 128 MiB of HBM per device.

```python
import math
import jax
import jax.numpy as jnp
from jax import lax

CX = 256
STRIPE = 16
NZ = 16
COLS = 8
STEPS = 2
NX = 8192
NY = 128
ROWS = 4096


def footprint_ends(key):
    key = jax.random.fold_in(key, 11)
    first_key, second_key = jax.random.split(key)
    centre = 2 * jnp.arange(ROWS, dtype=jnp.int32)[:, None]
    first = jax.random.randint(first_key, (ROWS, COLS), -CX, CX, dtype=jnp.int32) + centre
    second = jax.random.randint(second_key, (ROWS, COLS), -CX, CX, dtype=jnp.int32) + centre
    starts = jnp.clip(jnp.minimum(first, second), 0, NX)
    finish = jnp.clip(jnp.maximum(first, second) + 1, 0, NX)
    return (starts, finish)


def draw_foot_start(key, part):
    return footprint_ends(key)[0]


def draw_foot_end(key, part):
    return footprint_ends(key)[1]


def touch_ends(drawn, own_key, smallest, high):
    index_at = [jax.random.randint(jax.random.fold_in(own_key, axis), (), 0, length) for axis, length in enumerate(drawn.shape)]
    widest = drawn.shape.index(max(drawn.shape))
    neighbour = index_at[:widest] + [(index_at[widest] + 1) % drawn.shape[widest]] + index_at[widest + 1:]
    return drawn.at[tuple(index_at)].set(smallest).at[tuple(neighbour)].set(high)


def block_scale(own_key, dims, shards, smallest, high):
    def one(axis_at, parts):
        steps = jax.random.uniform(jax.random.fold_in(jax.random.fold_in(own_key, 6), axis_at), (parts,), jnp.float32, smallest / len(shards), high / len(shards))
        return jnp.repeat(jnp.exp(steps), dims[axis_at] // parts).reshape((-1,) + (1,) * (len(dims) - axis_at - 1))

    level = one(*shards[0])
    for cut in shards[1:]:
        level = level * one(*cut)
    return level


def scatter_about(key, shape, scale, reach, cuts=(), kind=jnp.bfloat16):
    loudness = block_scale(key, shape, cuts, -0.22, 0.18) if cuts else 1.0
    drawn = jax.random.normal(key, shape, jnp.float32) * scale * loudness
    return jnp.minimum(jnp.maximum(drawn, -reach), reach).astype(kind)


def setup_inputs(seed: int = 0) -> dict:
    key_list = jax.random.split(jax.random.key(seed), 10)
    return {
        "orientation": jnp.clip(0.05 + 0.29999999 * jax.random.uniform(key_list[0], (5, NZ, NY, NX), jnp.float32) ** block_scale(key_list[0], (5, NZ, NY, NX), ((2, 8), (3, 32)), -0.2, 0.2), 0.05, 0.35),
        "velocity": scatter_about(key_list[1], (3, NZ, NY, NX), 1.0, 3.0, ((2, 8), (3, 32)), jnp.float32),
        "velocity_grad": scatter_about(key_list[2], (9, NZ, NY, NX), 0.5, 3.0, ((2, 8), (3, 32)), jnp.float32),
        "rotary": jnp.clip(jnp.exp(math.log(0.5) - 2.3025851 * jax.random.uniform(key_list[3], (NZ, NY, NX), jnp.float32) ** block_scale(key_list[3], (NZ, NY, NX), ((1, 8), (2, 32)), -0.2, 0.2)), 0.05, 0.5),
        "target": jnp.clip(0.4 * jax.random.uniform(key_list[4], (5, NZ, NY, NX), jnp.float32) ** block_scale(key_list[4], (5, NZ, NY, NX), ((2, 8), (3, 32)), -0.2, 0.2), 0.0, 0.4),
        "needle_params": jnp.clip(0.2 * jax.random.uniform(key_list[5], (ROWS, COLS, NZ), jnp.float32) ** block_scale(key_list[5], (ROWS, COLS, NZ), ((0, 32), (1, 8)), -0.2, 0.2), 0.0, 0.2),
        "foot_start": draw_foot_start(jax.random.fold_in(key_list[9], 71), 0),
        "foot_end": draw_foot_end(jax.random.fold_in(key_list[9], 71), 0),
        "foot_column": touch_ends(jax.random.randint(key_list[8], (ROWS, COLS), 0, STRIPE), jax.random.fold_in(key_list[8], 1), 0, STRIPE - 1).astype(jnp.int32),
    }


XI = 0.95
STEP = 0.1
HIGH = lax.Precision.HIGHEST
OFFSETS = ((0, 0, 1), (0, 1, 0), (1, 0, 0))

def reaction(fields, velocity_grad, rotary):
    diag_one = fields[0]
    diag_two = fields[1]
    off_xy = fields[2]
    off_xz = fields[3]
    off_yz = fields[4]
    diag_three = 1.0 - diag_one - diag_two
    tensor = [[diag_one, off_xy, off_xz], [off_xy, diag_two, off_yz], [off_xz, off_yz, diag_three]]
    strain = [[0.5 * (velocity_grad[3 * i + j] + velocity_grad[3 * j + i]) for j in range(3)] for i in range(3)]
    vortex = [[0.5 * (velocity_grad[3 * i + j] - velocity_grad[3 * j + i]) for j in range(3)] for i in range(3)]
    contracted = sum((tensor[i][j] * strain[i][j] for i in range(3) for j in range(3)))

    def entry(i, j):
        spin = sum((vortex[i][k] * tensor[k][j] - tensor[i][k] * vortex[k][j] for k in range(3)))
        stretch = sum((strain[i][k] * tensor[k][j] + tensor[i][k] * strain[k][j] for k in range(3)))
        identity_part = 1.0 if i == j else 0.0
        return spin + XI * (stretch - 2.0 * contracted * tensor[i][j]) + 2.0 * rotary * (identity_part - 3.0 * tensor[i][j])
    return jnp.stack([entry(0, 0), entry(1, 1), entry(0, 1), entry(0, 2), entry(1, 2)])

def interior(padded, shift_z, shift_y, shift_x):
    layers = padded.shape[-3] - 2
    height = padded.shape[-2] - 2
    length = padded.shape[-1] - 2
    return padded[..., 1 + shift_z:1 + shift_z + layers, 1 + shift_y:1 + shift_y + height, 1 + shift_x:1 + shift_x + length]

def advect(padded, velocity):
    centre = interior(padded, 0, 0, 0)
    summed = jnp.zeros_like(centre)
    for number, offset in enumerate(OFFSETS):
        front_cell = interior(padded, offset[0], offset[1], offset[2])
        behind = interior(padded, -offset[0], -offset[1], -offset[2])
        upward = jnp.maximum(velocity[number], 0.0)
        downward = jnp.minimum(velocity[number], 0.0)
        summed = summed - upward * (centre - behind) - downward * (front_cell - centre)
    return summed

def advect_back(adjoint_pad, velocity_pad):
    centre = interior(adjoint_pad, 0, 0, 0)
    summed = jnp.zeros_like(centre)
    for number, offset in enumerate(OFFSETS):
        upward = jnp.maximum(velocity_pad[number], 0.0)
        downward = jnp.minimum(velocity_pad[number], 0.0)
        summed = summed + (interior(downward, 0, 0, 0) - interior(upward, 0, 0, 0)) * centre
        summed = summed + interior(upward * adjoint_pad, offset[0], offset[1], offset[2])
        summed = summed - interior(downward * adjoint_pad, -offset[0], -offset[1], -offset[2])
    return summed

def pad_cells(fields):
    return jnp.pad(fields, ((0, 0), (1, 1), (1, 1), (1, 1)))

def reference(orientation, velocity, velocity_grad, rotary, target, needle_params, foot_start, foot_end, foot_column):
    cells_x = jnp.arange(NX, dtype=jnp.int32)
    picker_range = jnp.arange(STRIPE, dtype=jnp.int32)

    def covered(starts, ends):
        return ((cells_x[None, :] >= starts[:, None]) & (cells_x[None, :] < ends[:, None])).astype(jnp.float32)

    def column_source(items):
        rates, starts, ends, chosen = items
        picked = (chosen[:, None] == picker_range[None, :]).astype(jnp.float32)
        spread = (rates[:, :, None] * picked[:, None, :]).reshape(ROWS, NZ * STRIPE)
        return jnp.dot(spread.T, covered(starts, ends), precision=HIGH, preferred_element_type=jnp.float32)
    per_column = lax.map(column_source, (jnp.transpose(needle_params, (1, 0, 2)), foot_start.T, foot_end.T, foot_column.T))
    source = jnp.transpose(per_column.reshape(COLS, NZ, STRIPE, NX), (1, 0, 2, 3)).reshape(NZ, NY, NX)
    velocity_pad = pad_cells(velocity)
    history = [orientation]
    for step_number in range(STEPS):
        current = history[-1]
        history.append(current + STEP * (advect(pad_cells(current), velocity) + reaction(current, velocity_grad, rotary) - source * current))
    adjoint = history[2] - target
    sensitivity = jnp.zeros_like(rotary)
    for fields in (history[1], history[0]):
        sensitivity = sensitivity - STEP * lax.optimization_barrier(jnp.sum(adjoint * fields, axis=0))
        pulled = jax.vjp(lambda values: reaction(values, velocity_grad, rotary), fields)[1](adjoint)[0]
        adjoint = adjoint + STEP * (advect_back(pad_cells(adjoint), velocity_pad) + pulled - source * adjoint)
    sens_grid = sensitivity.reshape(NZ, COLS, STRIPE, NX)

    def column_gradient(items):
        sens_column, starts, ends, chosen = items
        picked = (chosen[:, None] == picker_range[None, :]).astype(jnp.float32)
        flat = jnp.transpose(sens_column, (2, 0, 1)).reshape(NX, NZ * STRIPE)
        intersection = jnp.dot(covered(starts, ends), flat, precision=HIGH, preferred_element_type=jnp.float32)
        return lax.optimization_barrier(jnp.sum(intersection.reshape(ROWS, NZ, STRIPE) * picked[:, None, :], axis=2))
    gradient = lax.map(column_gradient, (jnp.transpose(sens_grid, (1, 0, 2, 3)), foot_start.T, foot_end.T, foot_column.T))
    return (history[2], adjoint, jnp.transpose(gradient, (1, 0, 2)))
```

```python
import functools

import jax
import jax.numpy as jnp
from jax import lax
from jax.experimental import pallas as pl
from jax.experimental.pallas import tpu as pltpu
from jax.sharding import PartitionSpec as P

XI = 0.95
DT = 0.1
LANES = 128
TILES = 3
HALO = 4
S0, VEL, GRAD, ROT, TGT, PLANES = 0, 5, 8, 17, 18, 23
F32 = jnp.float32


def lane_iota(shape):
    return lax.broadcasted_iota(jnp.int32, shape, len(shape) - 1)


def row_iota(shape):
    return lax.broadcasted_iota(jnp.int32, shape, len(shape) - 2)


def span(tile):
    return slice(tile * LANES, (tile + 1) * LANES)


def joined(native, halo, base):
    def read(number, z, tile):
        if tile < 2:
            return native[number, z, :, span(tile)]
        return halo[base + number, z]

    return read


def whole(ref):
    return lambda number, z, tile: ref[number, z, :, span(tile)]


def x_behind(read, number, z, tile):
    cur, prev = read(number, z, tile), read(number, z, (tile - 1) % TILES)
    return pltpu.roll(jnp.where(lane_iota(cur.shape) == LANES - 1, prev, cur), 1, 1)


def x_front(read, number, z, tile):
    cur, after = read(number, z, tile), read(number, z, (tile + 1) % TILES)
    return pltpu.roll(jnp.where(lane_iota(cur.shape) == 0, after, cur), LANES - 1, 1)


def y_behind(cur, halo):
    last = cur.shape[0] - 1
    return pltpu.roll(jnp.where(row_iota(cur.shape) == last, halo, cur), 1, 0)


def y_front(cur, halo):
    last = cur.shape[0] - 1
    return pltpu.roll(jnp.where(row_iota(cur.shape) == 0, halo, cur), last, 0)


def scaled_gradient(grad, z, tile):
    g = [grad(i, z, tile) for i in range(9)]
    low = 0.5 * (XI - 1.0) * DT
    m = {}
    for i, j in ((0, 1), (0, 2), (1, 2)):
        a, b = g[3 * i + j], g[3 * j + i]
        both = low * (a + b)
        m[i, j] = DT * a + both
        m[j, i] = DT * b + both
    m[0, 0] = (XI * DT) * (g[0] - g[8])
    m[1, 1] = (XI * DT) * (g[4] - g[8])
    return m


def speeds(vel, z, tile):
    out = []
    for d in range(3):
        u = DT * vel(d, z, tile)
        out.append((jnp.maximum(u, 0.0), jnp.minimum(u, 0.0)))
    return out


def damping(rot, src, wind, z, tile):
    total = (6.0 * DT) * rot(0, z, tile) + DT * src(0, z, tile)
    for up, down in wind:
        total = total + (up - down)
    return total


def forward(a, m, base, spread, wind, shifted):
    a11, a22, a12, a13, a23 = a
    n00 = m[0, 0] * a11 + m[0, 1] * a12 + m[0, 2] * a13
    n01 = m[0, 0] * a12 + m[0, 1] * a22 + m[0, 2] * a23
    a33 = 1.0 - a11 - a22
    n02 = m[0, 0] * a13 + m[0, 1] * a23 + m[0, 2] * a33
    n10 = m[1, 0] * a11 + m[1, 1] * a12 + m[1, 2] * a13
    n11 = m[1, 0] * a12 + m[1, 1] * a22 + m[1, 2] * a23
    n12 = m[1, 0] * a13 + m[1, 1] * a23 + m[1, 2] * a33
    n20 = m[2, 0] * a11 + m[2, 1] * a12
    n21 = m[2, 0] * a12 + m[2, 1] * a22
    n22 = m[2, 0] * a13 + m[2, 1] * a23
    keep = 1.0 - (base + 2.0 * (n00 + n11 + n22))
    gain = (
        2.0 * n00 + spread,
        2.0 * n11 + spread,
        n01 + n10,
        n02 + n20,
        n12 + n21,
    )
    out = []
    for c in range(5):
        total = gain[c] + keep * a[c]
        for (up, down), (behind, front) in zip(wind, shifted(c)):
            total = total + (up * behind - down * front)
        out.append(total)
    return out


def pulled(adj, a, m, base):
    b1, b2, b3, b4, b5 = adj
    a11, a22, a12, a13, a23 = a
    g = -2.0 * (b1 * a11 + b2 * a22 + b3 * a12 + b4 * a13 + b5 * a23)
    trace = (
        m[0, 0] * a11
        + m[1, 1] * a22
        + (m[0, 1] + m[1, 0]) * a12
        + (m[0, 2] + m[2, 0]) * a13
        + (m[1, 2] + m[2, 1]) * a23
    )
    s00, s11, s22 = 2.0 * b1 + g, 2.0 * b2 + g, g
    h00 = m[0, 0] * s00 + m[1, 0] * b3 + m[2, 0] * b4
    h01 = m[0, 0] * b3 + m[1, 0] * s11 + m[2, 0] * b5
    h02 = m[0, 0] * b4 + m[1, 0] * b5 + m[2, 0] * s22
    h10 = m[0, 1] * s00 + m[1, 1] * b3 + m[2, 1] * b4
    h11 = m[0, 1] * b3 + m[1, 1] * s11 + m[2, 1] * b5
    h12 = m[0, 1] * b4 + m[1, 1] * b5 + m[2, 1] * s22
    h20 = m[0, 2] * s00 + m[1, 2] * b3
    h21 = m[0, 2] * b3 + m[1, 2] * s11
    h22 = m[0, 2] * b4 + m[1, 2] * b5
    keep = 1.0 - (base + 2.0 * trace)
    return [
        keep * b1 + (h00 - h22),
        keep * b2 + (h11 - h22),
        keep * b3 + (h01 + h10),
        keep * b4 + (h02 + h20),
        keep * b5 + (h12 + h21),
    ]


def transposed_wind(vel, adj, z, tile, wind, layers):
    row = row_iota(wind[0][0].shape)
    lane = lane_iota(row.shape)
    after, prev = (tile + 1) % TILES, (tile - 1) % TILES
    u_front = jnp.maximum(DT * jnp.where(lane == 0, vel(0, z, after), vel(0, z, tile)), 0.0)
    u_back = jnp.minimum(
        DT * jnp.where(lane == LANES - 1, vel(0, z, prev), vel(0, z, tile)), 0.0
    )
    y_up = jnp.where(row == 0, 0.0, wind[1][0])
    y_down = jnp.where(row == row.shape[0] - 1, 0.0, wind[1][1])
    last = layers - 1
    z_next, z_prev = jnp.minimum(z + 1, last), jnp.maximum(z - 1, 0)
    z_up = jnp.where(z < last, DT, 0.0) * jnp.maximum(vel(2, z_next, tile), 0.0)
    z_down = jnp.where(z > 0, DT, 0.0) * jnp.minimum(vel(2, z_prev, tile), 0.0)

    def handed(c):
        cur = adj(c, z, tile)
        fx = u_front * jnp.where(lane == 0, adj(c, z, after), cur)
        bx = u_back * jnp.where(lane == LANES - 1, adj(c, z, prev), cur)
        total = pltpu.roll(fx, LANES - 1, 1) - pltpu.roll(bx, 1, 1)
        total = total + pltpu.roll(y_up * cur, row.shape[0] - 1, 0)
        total = total - pltpu.roll(y_down * cur, 1, 0)
        return total + (z_up * adj(c, z_next, tile) - z_down * adj(c, z_prev, tile))

    return handed


class Rows:
    def __init__(self, message, side, planes):
        self.message, self.side, self.planes = message, side, planes

    def put(self, plane, z, tile, value):
        if tile < 2:
            at = tile * self.planes + plane
            self.message[z, at : at + 1] = value
        else:
            at = self.side.shape[1] - 1 - plane
            self.side[z, at : at + 1] = value

    def get(self, plane, z, tile):
        if tile < 2:
            at = tile * self.planes + plane
            return self.message[z, at : at + 1]
        return self.side[z, plane : plane + 1]

    def pack(self):
        shape = self.side.shape[1:]
        mine = lane_iota(shape) // 8 == row_iota(shape)
        mine = mine & (row_iota(shape) >= shape[0] - self.planes)
        at = 2 * self.planes

        def layer(z, carry):
            moved = pltpu.roll(self.side[z], HALO, 1, stride=8, stride_axis=0)
            line = jnp.sum(jnp.where(mine, moved, 0.0), axis=0, keepdims=True)
            self.message[z, at : at + 1] = line
            return carry

        lax.fori_loop(0, self.side.shape[0], layer, 0)

    def unpack(self, source, valid):
        shape = self.side.shape[1:]
        lane = lane_iota(shape)
        kept = ((lane < HALO) | (lane >= LANES - HALO)) & valid
        at = 2 * self.planes

        def layer(z, carry):
            self.message[z] = jnp.where(valid, source[z], 0.0)
            line = jnp.broadcast_to(source[z, at : at + 1], shape)
            moved = pltpu.roll(line, HALO, 1, stride=8, stride_axis=0)
            self.side[z] = jnp.where(kept, moved, 0.0)
            return carry

        lax.fori_loop(0, self.side.shape[0], layer, 0)


def pack_kernel(s0, vel, grad, rot, tgt, needle, to_left, to_right):
    layers = s0.shape[1]

    @pl.when(pl.program_id(0) == 0)
    def _():
        to_left[to_left.shape[0] - 1] = needle[...]
        to_right[to_right.shape[0] - 1] = needle[...]

    first = pl.program_id(0) * layers
    lane = lane_iota(to_left.shape[1:])

    def layer(z, carry):
        left = jnp.zeros(lane.shape, F32)
        right = jnp.zeros(lane.shape, F32)
        slot = 0
        for ref in (s0, vel, grad, rot, tgt):
            for c in range(ref.shape[0]):
                low = ref[c, z, :, span(0)]
                high = ref[c, z, :, span(1)]
                if slot:
                    low = pltpu.roll(low, HALO * slot, 1)
                high = pltpu.roll(high, HALO * (slot + 1), 1)
                mine = lane // HALO == slot
                left = jnp.where(mine, low, left)
                right = jnp.where(mine, high, right)
                slot += 1
        to_left[first + z] = left
        to_right[first + z] = right
        return carry

    lax.fori_loop(0, layers, layer, 0)


def split_three(value):
    parts = []
    for _ in range(3):
        part = value.astype(jnp.bfloat16).astype(F32)
        parts.append(part)
        value = value - part
    return parts


def feet_block(ref, block, count):
    place = jnp.clip(block, 0, count - 1) * LANES
    row = ref[:, pl.ds(pl.multiple_of(place, LANES), LANES)]
    return jnp.where((block >= 0) & (block < count), row, 0)


def first_kernel(
    axis_md,
    s0,
    vel,
    grad,
    rot,
    own_message,
    from_left,
    from_right,
    far_left,
    far_right,
    start,
    end,
    column,
    s1,
    src,
    halo,
    up,
    down,
    spread,
    cover,
    up_side,
    down_side,
):
    layers, height = s0.shape[1], s0.shape[2]
    up_rows, down_rows = Rows(up, up_side, 11), Rows(down, down_side, 11)
    md = lax.axis_index(axis_md)
    count = lax.axis_size(axis_md)

    lane = lane_iota((height, LANES))
    left_ok = (lane >= LANES - HALO) & (md > 0)
    right_ok = (lane < HALO) & (md < count - 1)

    def unpack(z, carry):
        left, right = from_left[z], from_right[z]
        for c in range(PLANES):
            low = pltpu.roll(right, (LANES - HALO * c) % LANES, 1) if c else right
            high = pltpu.roll(left, (2 * LANES - HALO * (c + 1)) % LANES, 1)
            halo[c, z] = jnp.where(right_ok, low, jnp.where(left_ok, high, 0.0))
        return carry

    lax.fori_loop(0, layers, unpack, 0)

    near = lane_iota((1, LANES)) < LANES // 2

    def feet(ref):
        far = jnp.where(near, feet_block(ref, md + 2, count), feet_block(ref, md - 2, count))
        blocks = [feet_block(ref, md + d, count) for d in (-1, 0, 1)]
        return jnp.concatenate(blocks + [far], axis=1)

    starts, ends, columns = feet(start), feet(end), feet(column)
    own = own_message.shape[0] - 1
    wide = lane_iota((layers, LANES)) < LANES // 2
    rates = jnp.concatenate(
        [
            from_left[own],
            own_message[own],
            from_right[own],
            jnp.where(wide, far_right[...], far_left[...]),
        ],
        axis=1,
    )
    needles = rates.shape[1]
    picked = jnp.where(row_iota((height, needles)) == columns, 1.0, 0.0)
    for part, value in enumerate(split_three(rates)):
        for z in range(layers):
            spread[part, z * height : (z + 1) * height] = (picked * value[z : z + 1]).astype(
                jnp.bfloat16
            )
    cells = row_iota((TILES * LANES, needles))
    length = 2 * LANES
    cells = jnp.where(cells < length + LANES // 2, cells, cells - TILES * LANES) + md * length
    cover[...] = jnp.where((cells >= starts) & (cells < ends), 1.0, 0.0).astype(jnp.bfloat16)
    product = jnp.zeros((layers * height, TILES * LANES), F32)
    for part in range(3):
        product = product + lax.dot_general(
            spread[part], cover[...], (((1,), (1,)), ((), ())), preferred_element_type=F32
        )
    src[...] = product.reshape(src.shape)

    field = joined(s0, halo, S0)
    wind_of = joined(vel, halo, VEL)
    grad_of = joined(grad, halo, GRAD)
    rot_of = joined(rot, halo, ROT)
    src_of = whole(src)
    last = layers - 1

    def layer(z, carry):
        z_next, z_prev = jnp.minimum(z + 1, last), jnp.maximum(z - 1, 0)
        above, below = jnp.where(z < last, 1.0, 0.0), jnp.where(z > 0, 1.0, 0.0)
        for tile in range(TILES):
            wind = speeds(wind_of, z, tile)
            m = scaled_gradient(grad_of, z, tile)
            base = damping(rot_of, src_of, wind, z, tile)
            up_z, down_z = wind[2]
            flow = [wind[0], wind[1], (up_z * below, down_z * above)]
            a = [field(c, z, tile) for c in range(5)]

            def shifted(c):
                return (
                    (x_behind(field, c, z, tile), x_front(field, c, z, tile)),
                    (y_behind(a[c], 0.0), y_front(a[c], 0.0)),
                    (field(c, z_prev, tile), field(c, z_next, tile)),
                )

            out = forward(a, m, base, (2.0 * DT) * rot_of(0, z, tile), flow, shifted)
            for c in range(5):
                s1[c, z, :, span(tile)] = out[c]
                up_rows.put(c, z, tile, a[c][height - 1 :])
                down_rows.put(c, z, tile, a[c][:1])
                up_rows.put(5 + c, z, tile, out[c][height - 1 :])
                down_rows.put(5 + c, z, tile, out[c][:1])
            up_rows.put(10, z, tile, -wind[1][1][height - 1 :])
            down_rows.put(10, z, tile, wind[1][0][:1])
        return carry

    lax.fori_loop(0, layers, layer, 0)
    up_rows.pack()
    down_rows.pack()


def cd_flags(axis_cd):
    cd = lax.axis_index(axis_cd)
    return cd > 0, cd < lax.axis_size(axis_cd) - 1


def second_kernel(
    axis_cd,
    s1_part,
    src,
    halo,
    vel,
    grad,
    rot,
    tgt,
    own_up,
    own_down,
    from_below,
    from_above,
    s2,
    adj1,
    dots,
    up,
    down,
    s1,
    adj2,
    low_copy,
    high_copy,
    low_side,
    high_side,
    own_low_side,
    own_high_side,
    own_low_copy,
    own_high_copy,
    up_side,
    down_side,
):
    layers, height = vel.shape[1], vel.shape[2]
    last, top = layers - 1, height - 1
    has_below, has_above = cd_flags(axis_cd)
    up_rows, down_rows = Rows(up, up_side, 10), Rows(down, down_side, 10)
    low, high = Rows(low_copy, low_side, 11), Rows(high_copy, high_side, 11)
    own_low, own_high = Rows(own_low_copy, own_low_side, 11), Rows(own_high_copy, own_high_side, 11)
    low.unpack(from_below, has_below)
    high.unpack(from_above, has_above)
    own_low.unpack(own_down, True)
    own_high.unpack(own_up, True)

    def outer(rows, mine, c, z, tile):
        return rows.get(5 + c, z, tile) + rows.get(10, z, tile) * mine.get(c, z, tile)

    wind_of = joined(vel, halo, VEL)
    grad_of = joined(grad, halo, GRAD)
    rot_of = joined(rot, halo, ROT)
    tgt_of = joined(tgt, halo, TGT)
    src_of, s1_of, adj2_of = whole(src), whole(s1), whole(adj2)

    def mend(z, carry):
        for tile in range(TILES):
            u = DT * wind_of(1, z, tile)
            row = row_iota(u.shape)
            from_low = jnp.where(row == 0, jnp.maximum(u, 0.0), 0.0)
            from_high = jnp.where(row == top, -jnp.minimum(u, 0.0), 0.0)
            for c in range(5):
                s1[c, z, :, span(tile)] = (
                    s1_part[c, z, :, span(tile)]
                    + from_low * low.get(c, z, tile)
                    + from_high * high.get(c, z, tile)
                )
        return carry

    lax.fori_loop(0, layers, mend, 0)

    def advance(z, carry):
        z_next, z_prev = jnp.minimum(z + 1, last), jnp.maximum(z - 1, 0)
        above, below = jnp.where(z < last, 1.0, 0.0), jnp.where(z > 0, 1.0, 0.0)
        for tile in range(TILES):
            wind = speeds(wind_of, z, tile)
            m = scaled_gradient(grad_of, z, tile)
            base = damping(rot_of, src_of, wind, z, tile)
            up_z, down_z = wind[2]
            flow = [wind[0], wind[1], (up_z * below, down_z * above)]
            a = [s1_of(c, z, tile) for c in range(5)]

            def shifted(c):
                return (
                    (x_behind(s1_of, c, z, tile), x_front(s1_of, c, z, tile)),
                    (
                        y_behind(a[c], outer(low, own_low, c, z, tile)),
                        y_front(a[c], outer(high, own_high, c, z, tile)),
                    ),
                    (s1_of(c, z_prev, tile), s1_of(c, z_next, tile)),
                )

            out = forward(a, m, base, (2.0 * DT) * rot_of(0, z, tile), flow, shifted)
            for c in range(5):
                adj2[c, z, :, span(tile)] = out[c] - tgt_of(c, z, tile)
                if tile < 2:
                    s2[c, z, :, span(tile)] = out[c]
        return carry

    lax.fori_loop(0, layers, advance, 0)

    def retreat(z, carry):
        for tile in range(TILES):
            wind = speeds(wind_of, z, tile)
            m = scaled_gradient(grad_of, z, tile)
            base = damping(rot_of, src_of, wind, z, tile)
            a = [s1_of(c, z, tile) for c in range(5)]
            b = [adj2_of(c, z, tile) for c in range(5)]
            out = pulled(b, a, m, base)
            handed = transposed_wind(wind_of, adj2_of, z, tile, wind, layers)
            to_high, to_low = -wind[1][1][top:], wind[1][0][:1]
            for c in range(5):
                total = out[c] + handed(c)
                adj1[c, z, :, span(tile)] = total
                up_rows.put(c, z, tile, to_high * b[c][top:])
                down_rows.put(c, z, tile, to_low * b[c][:1])
                up_rows.put(5 + c, z, tile, to_high * total[top:])
                down_rows.put(5 + c, z, tile, to_low * total[:1])
            if tile < 2:
                dots[z, :, span(tile)] = sum(x * y for x, y in zip(a, b))
        return carry

    lax.fori_loop(0, layers, retreat, 0)
    up_rows.pack()
    down_rows.pack()


def third_kernel(
    axis_md,
    axis_cd,
    adj1_part,
    dots,
    s0,
    from_below,
    from_above,
    start,
    end,
    column,
    adj1,
    to_left,
    kept,
    to_right,
    sens,
    low_copy,
    high_copy,
    low_side,
    high_side,
):
    layers, height = s0.shape[1], s0.shape[2]
    top = height - 1
    md = lax.axis_index(axis_md)
    count = lax.axis_size(axis_md)
    has_below, has_above = cd_flags(axis_cd)
    low, high = Rows(low_copy, low_side, 10), Rows(high_copy, high_side, 10)
    low.unpack(from_below, has_below)
    high.unpack(from_above, has_above)

    def mend(z, carry):
        for tile in range(TILES):
            total = dots[z, :, span(tile)] if tile < 2 else None
            row = row_iota((height, LANES))
            for c in range(5):
                value = adj1_part[c, z, :, span(tile)] + jnp.where(
                    row == 0,
                    low.get(c, z, tile),
                    jnp.where(row == top, high.get(c, z, tile), 0.0),
                )
                adj1[c, z, :, span(tile)] = value
                if tile < 2:
                    total = total + value * s0[c, z, :, span(tile)]
            if tile < 2:
                sens[z, :, span(tile)] = -DT * total
        return carry

    lax.fori_loop(0, layers, mend, 0)

    def feet(ref):
        return jnp.concatenate([feet_block(ref, md + d, count) for d in (-1, 0, 1)], axis=1)

    starts, ends, columns = feet(start), feet(end), feet(column)
    needles = starts.shape[1]
    length = 2 * LANES
    cells = row_iota((length, needles)) + md * length
    cover = jnp.where((cells >= starts) & (cells < ends), 1.0, 0.0).astype(jnp.bfloat16)
    product = jnp.zeros((layers * height, needles), F32)
    for part in split_three(sens[...].reshape(layers * height, length)):
        product = product + jnp.dot(
            part.astype(jnp.bfloat16), cover, preferred_element_type=F32
        )
    picked = jnp.where(row_iota((height, needles)) == columns, 1.0, 0.0)
    for z in range(layers):
        line = jnp.sum(
            product[z * height : (z + 1) * height] * picked, axis=0, keepdims=True
        )
        to_left[z : z + 1] = line[:, span(0)]
        kept[z : z + 1] = line[:, span(1)]
        to_right[z : z + 1] = line[:, span(2)]


def fourth_kernel(
    axis_cd,
    adj1,
    s0,
    src,
    halo,
    vel,
    grad,
    rot,
    weights_below,
    weights_above,
    own_up,
    own_down,
    from_below,
    from_above,
    adj0,
):
    layers, height = s0.shape[1], s0.shape[2]
    top = height - 1
    has_below, has_above = cd_flags(axis_cd)

    def brought(weights, message, mine, valid, c, z, tile):
        old, new = tile * 11 + 10, tile * 10 + 5 + c
        own = tile * 10 + c
        line = message[z, new : new + 1] + weights[z, old : old + 1] * mine[z, own : own + 1]
        return jnp.where(valid, line, 0.0)

    wind_of = joined(vel, halo, VEL)
    src_of, adj1_of = whole(src), whole(adj1)

    def retreat(z, carry):
        for tile in range(2):
            wind = speeds(wind_of, z, tile)
            m = scaled_gradient(whole(grad), z, tile)
            base = damping(whole(rot), src_of, wind, z, tile)
            a = [s0[c, z, :, span(tile)] for c in range(5)]
            b = [adj1_of(c, z, tile) for c in range(5)]
            out = pulled(b, a, m, base)
            handed = transposed_wind(wind_of, adj1_of, z, tile, wind, layers)
            row = row_iota((height, LANES))
            for c in range(5):
                low = brought(weights_below, from_below, own_down, has_below, c, z, tile)
                high = brought(weights_above, from_above, own_up, has_above, c, z, tile)
                edge = jnp.where(row == 0, low, jnp.where(row == top, high, 0.0))
                adj0[c, z, :, span(tile)] = out[c] + handed(c) + edge
        return carry

    lax.fori_loop(0, layers, retreat, 0)


def ring(value, axis, steps):
    count = lax.axis_size(axis)
    return lax.ppermute(value, axis, [(i, (i + steps) % count) for i in range(count)])


def shape_of(*dims, dtype=F32):
    return jax.ShapeDtypeStruct(dims, dtype)


def scratch(*dims, dtype=F32):
    return pltpu.VMEM(dims, dtype)


PARAMS = pltpu.CompilerParams(vmem_limit_bytes=48 * 1024 * 1024)


def local(orientation, velocity, velocity_grad, rotary, target, needle_params, *feet):
    _, layers, height, length = orientation.shape
    rotary = rotary[None]
    rates = jnp.transpose(needle_params[:, 0, :])
    feet = [foot.reshape(1, -1) for foot in feet]
    wide = TILES * LANES
    cells = (layers, height, wide)

    blocks = 4
    deep = layers // blocks

    def chunk(count):
        return pl.BlockSpec((count, deep, height, length), lambda i: (0, i, 0, 0))

    message = shape_of(layers + 1, height, LANES)
    message_spec = pl.BlockSpec(message.shape, lambda i: (0, 0, 0))
    to_left, to_right = pl.pallas_call(
        pack_kernel,
        grid=(blocks,),
        in_specs=[chunk(5), chunk(3), chunk(9), chunk(1), chunk(5)]
        + [pl.BlockSpec(rates.shape, lambda i: (0, 0))],
        out_specs=[message_spec, message_spec],
        out_shape=[message, message],
        compiler_params=PARAMS,
    )(orientation, velocity, velocity_grad, rotary, target, rates)
    from_right = ring(to_left, "md", -1)
    from_left = ring(to_right, "md", 1)
    far_right = ring(rates, "md", -2)
    far_left = ring(rates, "md", 2)

    row_message = shape_of(layers, 24, LANES)
    copy, side = scratch(layers, 24, LANES), scratch(layers, 16, LANES)
    s1, src, halo, up, down = pl.pallas_call(
        functools.partial(first_kernel, "md"),
        out_shape=[
            shape_of(5, *cells),
            shape_of(1, *cells),
            shape_of(PLANES, layers, height, LANES),
            row_message,
            row_message,
        ],
        scratch_shapes=[
            scratch(3, layers * height, 4 * LANES, dtype=jnp.bfloat16),
            scratch(wide, 4 * LANES, dtype=jnp.bfloat16),
            side,
            side,
        ],
        compiler_params=PARAMS,
    )(
        orientation,
        velocity,
        velocity_grad,
        rotary,
        to_left,
        from_left,
        from_right,
        far_left,
        far_right,
        *feet,
    )
    below = ring(up, "cd", 1)
    above = ring(down, "cd", -1)

    s2, adj1, dots, back_up, back_down = pl.pallas_call(
        functools.partial(second_kernel, "cd"),
        out_shape=[
            shape_of(*orientation.shape),
            shape_of(5, *cells),
            shape_of(layers, height, length),
            row_message,
            row_message,
        ],
        scratch_shapes=[
            scratch(5, *cells),
            scratch(5, *cells),
            *([copy, copy] + [side] * 4 + [copy, copy] + [side] * 2),
        ],
        compiler_params=PARAMS,
    )(s1, src, halo, velocity, velocity_grad, rotary, target, up, down, below, above)
    back_below = ring(back_up, "cd", 1)
    back_above = ring(back_down, "cd", -1)

    part = shape_of(*rates.shape)
    adj1, part_left, part_own, part_right = pl.pallas_call(
        functools.partial(third_kernel, "md", "cd"),
        out_shape=[shape_of(5, *cells), part, part, part],
        scratch_shapes=[
            scratch(layers, height, length),
            copy,
            copy,
            side,
            side,
        ],
        compiler_params=PARAMS,
    )(adj1, dots, orientation, back_below, back_above, *feet)
    part_right = ring(part_right, "md", 1)
    part_left = ring(part_left, "md", -1)

    adj0 = pl.pallas_call(
        functools.partial(fourth_kernel, "cd"),
        out_shape=shape_of(*orientation.shape),
        compiler_params=PARAMS,
    )(
        adj1,
        orientation,
        src,
        halo,
        velocity,
        velocity_grad,
        rotary,
        below,
        above,
        back_up,
        back_down,
        back_below,
        back_above,
    )
    gradient = part_own + part_left + part_right
    return s2, adj0, jnp.transpose(gradient)[:, None, :]


def solution(mesh):
    field = P(None, None, "cd", "md")
    feet = P(None, "cd")
    needles = P("md", "cd", None)
    return jax.shard_map(
        local,
        mesh=mesh,
        in_specs=(field, field, field, P(None, "cd", "md"), field, needles, feet, feet, feet),
        out_specs=(field, field, needles),
        check_vma=False,
    )
```

```python
import functools

import jax
import jax.numpy as jnp
from jax import lax
from jax.experimental import pallas as pl
from jax.experimental.pallas import tpu as pltpu
from jax.sharding import PartitionSpec as P

XI = 0.95
DT = 0.1
LANES = 128
F32 = jnp.float32
HALO = 4
S0, VEL, GRAD, ROT, TGT, NEEDLES, PLANES = 0, 5, 8, 17, 18, 23, 24
PLACE = {(0, 0): 0, (1, 1): 1, (0, 1): 2, (1, 0): 3, (0, 2): 4, (2, 0): 5, (1, 2): 6, (2, 1): 7}
SPREAD, UX, UZ, COEFS = 8, 9, 10, 11
ROWS = 32
OWN, BEHIND, FRONT = slice(8, 24), slice(7, 23), slice(9, 25)


def lane_iota(shape):
    return lax.broadcasted_iota(jnp.int32, shape, len(shape) - 1)


def row_iota(shape):
    return lax.broadcasted_iota(jnp.int32, shape, len(shape) - 2)


def span(tile):
    return slice(tile * LANES, (tile + 1) * LANES)


def gradient_parts(read):
    g = [read(i) for i in range(9)]
    low = 0.5 * (XI - 1.0) * DT
    m = {}
    for i, j in ((0, 1), (0, 2), (1, 2)):
        a, b = g[3 * i + j], g[3 * j + i]
        both = low * (a + b)
        m[i, j] = DT * a + both
        m[j, i] = DT * b + both
    m[0, 0] = (XI * DT) * (g[0] - g[8])
    m[1, 1] = (XI * DT) * (g[4] - g[8])
    return m


def forward(a, m, base, spread, wind, around):
    a11, a22, a12, a13, a23 = a
    a33 = 1.0 - a11 - a22
    n00 = m[0, 0] * a11 + m[0, 1] * a12 + m[0, 2] * a13
    n01 = m[0, 0] * a12 + m[0, 1] * a22 + m[0, 2] * a23
    n02 = m[0, 0] * a13 + m[0, 1] * a23 + m[0, 2] * a33
    n10 = m[1, 0] * a11 + m[1, 1] * a12 + m[1, 2] * a13
    n11 = m[1, 0] * a12 + m[1, 1] * a22 + m[1, 2] * a23
    n12 = m[1, 0] * a13 + m[1, 1] * a23 + m[1, 2] * a33
    n20 = m[2, 0] * a11 + m[2, 1] * a12
    n21 = m[2, 0] * a12 + m[2, 1] * a22
    n22 = m[2, 0] * a13 + m[2, 1] * a23
    keep = 1.0 - (base + 2.0 * (n00 + n11 + n22))
    gain = (2.0 * n00 + spread, 2.0 * n11 + spread, n01 + n10, n02 + n20, n12 + n21)
    out = []
    for c in range(5):
        total = gain[c] + keep * a[c]
        for u, (behind, front) in zip(wind, around(c)):
            total = total + jnp.abs(u) * jnp.where(u > 0.0, behind, front)
        out.append(total)
    return out


def backward(b, a, m, base, wind, around):
    b1, b2, b3, b4, b5 = b
    a11, a22, a12, a13, a23 = a
    g = -2.0 * (b1 * a11 + b2 * a22 + b3 * a12 + b4 * a13 + b5 * a23)
    trace = (
        m[0, 0] * a11
        + m[1, 1] * a22
        + (m[0, 1] + m[1, 0]) * a12
        + (m[0, 2] + m[2, 0]) * a13
        + (m[1, 2] + m[2, 1]) * a23
    )
    s00, s11, s22 = 2.0 * b1 + g, 2.0 * b2 + g, g
    h00 = m[0, 0] * s00 + m[1, 0] * b3 + m[2, 0] * b4
    h01 = m[0, 0] * b3 + m[1, 0] * s11 + m[2, 0] * b5
    h02 = m[0, 0] * b4 + m[1, 0] * b5 + m[2, 0] * s22
    h10 = m[0, 1] * s00 + m[1, 1] * b3 + m[2, 1] * b4
    h11 = m[0, 1] * b3 + m[1, 1] * s11 + m[2, 1] * b5
    h12 = m[0, 1] * b4 + m[1, 1] * b5 + m[2, 1] * s22
    h20 = m[0, 2] * s00 + m[1, 2] * b3
    h21 = m[0, 2] * b3 + m[1, 2] * s11
    h22 = m[0, 2] * b4 + m[1, 2] * b5
    keep = 1.0 - (base + 2.0 * trace)
    gain = (h00 - h22, h11 - h22, h01 + h10, h02 + h20, h12 + h21)
    weights = [(jnp.minimum(w, 0.0), jnp.maximum(f, 0.0)) for w, f in wind]
    out = []
    for c in range(5):
        total = gain[c] + keep * b[c]
        for (low, high), (behind, front) in zip(weights, around(c)):
            total = total + (high * front - low * behind)
        out.append(total)
    return out


def merged(strips, c, rows):
    left, right = strips[c, 0, rows], strips[c, 1, rows]
    return jnp.where(lane_iota(left.shape) % 8 < HALO, left, right)


def edge_tile(joint, z):
    return pltpu.roll(joint, (2 * LANES - HALO - 8 * z) % LANES, 1)


def x_pair(tiles, tile, edge):
    cur = tiles[tile]
    prev, after = (edge, tiles[1]) if tile == 0 else (tiles[0], edge)
    lane = lane_iota(cur.shape)
    behind = pltpu.roll(jnp.where(lane == LANES - 1, prev, cur), 1, 1)
    front = pltpu.roll(jnp.where(lane == 0, after, cur), LANES - 1, 1)
    return behind, front


def strip_x(cur):
    return pltpu.roll(cur, 1, 1), pltpu.roll(cur, LANES - 1, 1)


def strip_z(cur):
    lane = lane_iota(cur.shape)
    behind = jnp.where(lane < 8, 0.0, pltpu.roll(cur, 8, 1))
    front = jnp.where(lane >= LANES - 8, 0.0, pltpu.roll(cur, LANES - 8, 1))
    return behind, front


def coefficients(coef, base, *at):
    m = {key: coef[(place,) + at] for key, place in PLACE.items()}
    return m, base[at]


class Field:
    def __init__(self, ref, strips, joint=None):
        self.ref, self.strips, self.joint = ref, strips, joint

    def join(self):
        for c in range(self.ref.shape[0]):
            self.joint[c] = merged(self.strips, c, OWN)

    def own(self, c, z, tile):
        return self.ref[c, z + 1, tile, OWN]

    def around(self, z, tile):
        def pairs(c):
            ref = self.ref
            tiles = [ref[c, z + 1, t, OWN] for t in range(2)]
            if self.joint is None:
                edge = jnp.zeros_like(tiles[0])
            else:
                edge = edge_tile(self.joint[c], z)
            return (
                x_pair(tiles, tile, edge),
                (ref[c, z + 1, tile, BEHIND], ref[c, z + 1, tile, FRONT]),
                (ref[c, z, tile, OWN], ref[c, z + 2, tile, OWN]),
            )

        return pairs

    def strip_around(self, side):
        def pairs(c):
            cur = self.strips[c, side, OWN]
            return (
                strip_x(cur),
                (self.strips[c, side, BEHIND], self.strips[c, side, FRONT]),
                strip_z(cur),
            )

        return pairs

    def clear(self):
        last = self.ref.shape[1] - 1
        zero = jnp.zeros((8, LANES), F32)
        clear_planes(self.ref)

        def layer(z, carry):
            for c in range(self.ref.shape[0]):
                for tile in range(2):
                    self.ref[c, z, tile, 0:8] = zero
                    self.ref[c, z, tile, 24:32] = zero
            return carry

        lax.fori_loop(1, last, layer, 0)

    def clear_strips(self):
        zero = jnp.zeros((8, LANES), F32)
        for c in range(self.strips.shape[0]):
            for side in range(2):
                self.strips[c, side, 0:8] = zero
                self.strips[c, side, 24:32] = zero


def clear_planes(ref, planes=None):
    last = ref.shape[1] - 1
    for c in planes or range(ref.shape[0]):
        for tile in range(2):
            for z in (0, last):
                ref[c, z, tile] = jnp.zeros(ref.shape[3:], F32)


def line(z, place, count, layers):
    if z is None:
        return slice(count * layers + place, count * layers + place + 1)
    return pl.ds(place * layers + z, 1)


def back_wind(coef, uy, edge_x, z, tile):
    tiles = [coef[UX, z + 1, t] for t in range(2)]
    return (
        x_pair(tiles, tile, edge_tile(edge_x, z)),
        (uy[z + 1, tile, BEHIND], uy[z + 1, tile, FRONT]),
        (coef[UZ, z, tile], coef[UZ, z + 2, tile]),
    )


def strip_back_wind(coef, uy, side):
    return (
        strip_x(coef[UX, side]),
        (uy[side, BEHIND], uy[side, FRONT]),
        strip_z(coef[UZ, side]),
    )


def pack_kernel(s0, vel, grad, rot, tgt, needle, out, stage, sems):
    layers = stage.shape[1]
    blocks = sems.shape[0]
    deep = layers // blocks
    sources = (s0, vel, grad, rot, tgt)

    def copies(block):
        slot, found = 0, []
        for number, ref in enumerate(sources):
            depth = pl.ds(block * deep, deep)
            target = stage.at[pl.ds(slot, ref.shape[0]), depth]
            found.append(
                pltpu.make_async_copy(ref.at[:, depth], target, sems.at[block, number])
            )
            slot += ref.shape[0]
        return found

    for block in range(blocks):
        for copy in copies(block):
            copy.start()
    out[NEEDLES] = needle[...]
    lane = lane_iota(out.shape[1:])

    def step(block, carry):
        for copy in copies(block):
            copy.wait()
        for c in range(NEEDLES):
            total = out[c]
            for k in range(deep):
                z = block * deep + k
                low, high = stage[c, z, :, span(0)], stage[c, z, :, span(1)]
                both = jnp.where(lane < HALO, low, high)
                moved = pltpu.roll(both, (8 * z + HALO) % LANES, 1)
                total = jnp.where(lane // 8 == z, moved, total)
            out[c] = total
        return carry

    lax.fori_loop(0, blocks, step, 0)


def bulk_kernel(s0, vel, grad, rot, field, coef, base, uy, s1):
    layers = s0.shape[1]
    state = Field(field, None)
    state.clear()
    clear_planes(coef, [UZ])

    def load(z, carry):
        zero = jnp.zeros((8, LANES), F32)
        for tile in range(2):
            for c in range(5):
                field[c, z + 1, tile, OWN] = s0[c, z, :, span(tile)]
            u = [DT * vel[d, z, :, span(tile)] for d in range(3)]
            turn = DT * rot[0, z, :, span(tile)]
            for key, value in gradient_parts(lambda i: grad[i, z, :, span(tile)]).items():
                coef[PLACE[key], z + 1, tile] = value
            coef[SPREAD, z + 1, tile] = 2.0 * turn
            coef[UX, z + 1, tile] = u[0]
            coef[UZ, z + 1, tile] = u[2]
            uy[z + 1, tile, 0:8] = zero
            uy[z + 1, tile, 24:32] = zero
            uy[z + 1, tile, OWN] = u[1]
            base[z + 1, tile] = 6.0 * turn + (jnp.abs(u[0]) + jnp.abs(u[1]) + jnp.abs(u[2]))
        return carry

    lax.fori_loop(0, layers, load, 0)

    def advance(z, carry):
        for tile in range(2):
            at = (z + 1, tile)
            m, damp = coefficients(coef, base, *at)
            wind = (coef[(UX,) + at], uy[at + (OWN,)], coef[(UZ,) + at])
            a = [state.own(c, z, tile) for c in range(5)]
            out = forward(a, m, damp, coef[(SPREAD,) + at], wind, state.around(z, tile))
            for c in range(5):
                s1[c, z + 1, tile, OWN] = out[c]
        return carry

    lax.fori_loop(0, layers, advance, 0)


def split_three(value):
    parts = []
    for _ in range(3):
        part = value.astype(jnp.bfloat16).astype(F32)
        parts.append(part)
        value = value - part
    return parts


def feet_block(ref, block, count):
    place = jnp.clip(block, 0, count - 1) * LANES
    row = ref[:, pl.ds(pl.multiple_of(place, LANES), LANES)]
    return jnp.where((block >= 0) & (block < count), row, 0)


def first_kernel(
    axis_md,
    axis_cd,
    own,
    near_first,
    near_second,
    far_first,
    far_second,
    start,
    end,
    column,
    field,
    coef,
    uy,
    base_in,
    s1_in,
    s1,
    base,
    strip_s0,
    strip_coef,
    strip_base,
    strip_uy,
    strip_s1,
    strip_tgt,
    up,
    down,
    spread,
    cover,
    source,
    joint,
):
    layers = field.shape[1] - 2
    height = own.shape[1]
    md = lax.axis_index(axis_md)
    count = lax.axis_size(axis_md)
    lane = lane_iota((height, LANES))
    outer = lane % 8 < HALO
    odd = lax.axis_index(axis_cd) % 2 == 1

    def from_left(c):
        return jnp.where(odd, near_second[c], near_first[c])

    def from_right(c):
        return jnp.where(odd, near_first[c], near_second[c])

    near = lane_iota((1, LANES)) < LANES // 2

    def feet(ref):
        far = jnp.where(near, feet_block(ref, md + 2, count), feet_block(ref, md - 2, count))
        blocks = [feet_block(ref, md + d, count) for d in (-1, 0, 1)]
        return jnp.concatenate(blocks + [far], axis=1)

    starts, ends, columns = feet(start), feet(end), feet(column)
    far = jnp.where((lane < LANES // 2) == odd, far_first[...], far_second[...])
    rates = jnp.concatenate(
        [from_left(NEEDLES), own[NEEDLES], from_right(NEEDLES), far], axis=1
    )
    needles = rates.shape[1]
    picked = jnp.where(row_iota((height, needles)) == columns, 1.0, 0.0)
    for part, value in enumerate(split_three(rates)):
        for z in range(layers):
            spread[part, z * height : (z + 1) * height] = (picked * value[z : z + 1]).astype(
                jnp.bfloat16
            )
    length = 2 * LANES
    cells = row_iota((length + LANES, needles))
    beyond = cells - length
    strip = jnp.where(beyond < 8, beyond - HALO, beyond - 8 + length - HALO)
    cells = jnp.where(cells < length, cells, strip) + md * length
    cover[...] = jnp.where((cells >= starts) & (cells < ends), 1.0, 0.0).astype(jnp.bfloat16)
    product = jnp.zeros((layers * height, length + LANES), F32)
    for part in range(3):
        product = product + lax.dot_general(
            spread[part], cover[...], (((1,), (1,)), ((), ())), preferred_element_type=F32
        )
    source[...] = (DT * product).reshape(source.shape)

    state = Field(field, strip_s0, joint)
    state.clear_strips()
    has_left, has_right = md > 0, md < count - 1
    for side in range(2):

        def raw(c):
            if side == 0:
                return jnp.where(outer, jnp.where(has_left, from_left(c), 0.0), own[c])
            return jnp.where(outer, own[c], jnp.where(has_right, from_right(c), 0.0))

        for c in range(5):
            strip_s0[c, side, OWN] = raw(S0 + c)
            strip_tgt[c, side] = raw(TGT + c)
        u = [DT * raw(VEL + d) for d in range(3)]
        turn = DT * raw(ROT)
        for key, value in gradient_parts(lambda i: raw(GRAD + i)).items():
            strip_coef[PLACE[key], side] = value
        strip_coef[SPREAD, side] = 2.0 * turn
        strip_coef[UX, side] = u[0]
        strip_coef[UZ, side] = u[2]
        strip_uy[side, 0:8] = jnp.zeros((8, LANES), F32)
        strip_uy[side, 24:32] = jnp.zeros((8, LANES), F32)
        strip_uy[side, OWN] = u[1]
        damp = 6.0 * turn + (jnp.abs(u[0]) + jnp.abs(u[1]) + jnp.abs(u[2]))
        taken = jnp.zeros((height, LANES), F32)
        for z in range(layers):
            moved = pltpu.roll(source[z, :, span(2)], (8 * z - 8 * side) % LANES, 1)
            taken = jnp.where(lane // 8 == z, moved, taken)
        strip_base[side] = damp + taken

    for side in range(2):
        m, damp = coefficients(strip_coef, strip_base, side)
        wind = (strip_coef[UX, side], strip_uy[side, OWN], strip_coef[UZ, side])
        a = [strip_s0[c, side, OWN] for c in range(5)]
        spin = strip_coef[SPREAD, side]
        out = forward(a, m, damp, spin, wind, state.strip_around(side))
        for c in range(5):
            strip_s1[c, side, OWN] = out[c]
    state.join()

    def put(z, tile, first, new, wind):
        def at(place):
            return line(z, tile * 11 + place, 22, layers)

        for c in range(5):
            up[at(c)] = first(c)[23:24]
            down[at(c)] = first(c)[8:9]
            up[at(5 + c)] = new(c)[23:24]
            down[at(5 + c)] = new(c)[8:9]
        up[at(10)] = -jnp.minimum(wind[23:24], 0.0)
        down[at(10)] = jnp.maximum(wind[8:9], 0.0)

    def mend(z, carry):
        for tile in range(2):
            gain = source[z, :, span(tile)]
            base[z + 1, tile] = base_in[z + 1, tile] + gain
            u = coef[UX, z + 1, tile]
            if tile == 0:
                weight, turn = jnp.where(lane == 0, jnp.maximum(u, 0.0), 0.0), 1
            else:
                weight, turn = jnp.where(lane == LANES - 1, -jnp.minimum(u, 0.0), 0.0), -1
            for c in range(5):
                edge = pltpu.roll(joint[c], (2 * LANES - HALO + turn - 8 * z) % LANES, 1)
                s1[c, z + 1, tile, OWN] = (
                    s1_in[c, z + 1, tile, OWN]
                    - gain * field[c, z + 1, tile, OWN]
                    + weight * edge
                )
            put(
                z,
                tile,
                lambda c: field.at[c, z + 1, tile],
                lambda c: s1.at[c, z + 1, tile],
                uy.at[z + 1, tile],
            )
        return carry

    clear_planes(s1)
    lax.fori_loop(0, layers, mend, 0)
    for side in range(2):
        put(
            None,
            side,
            lambda c: strip_s0.at[c, side],
            lambda c: strip_s1.at[c, side],
            strip_uy.at[side],
        )


def cd_flags(axis_cd):
    cd = lax.axis_index(axis_cd)
    return cd > 0, cd < lax.axis_size(axis_cd) - 1


def second_kernel(
    axis_cd,
    s1_in,
    strip_s1_in,
    coef,
    base,
    uy,
    tgt,
    strip_coef,
    strip_base,
    strip_uy,
    strip_tgt,
    own_up,
    own_down,
    from_below,
    from_above,
    s2,
    adj1,
    strip_adj1,
    dots,
    up,
    down,
    s1,
    strip_s1,
    adj2,
    strip_adj2,
    joint,
    joint2,
):
    layers = tgt.shape[1]
    has_below, has_above = cd_flags(axis_cd)

    def mend(target, wind, z, tile):
        def at(place):
            return line(z, tile * 11 + place, 22, layers)

        low_u, high_u = jnp.maximum(wind[8:9], 0.0), -jnp.minimum(wind[23:24], 0.0)
        low_n, high_n = from_below[at(10)], from_above[at(10)]
        for c in range(5):
            old, new = at(c), at(5 + c)
            ref = target(c)
            low = from_below[new] + low_n * own_down[old]
            high = from_above[new] + high_n * own_up[old]
            ref[7:8] = jnp.where(has_below, low, 0.0)
            ref[24:25] = jnp.where(has_above, high, 0.0)
            ref[8:9] = ref[8:9] + jnp.where(has_below, low_u * from_below[old], 0.0)
            ref[23:24] = ref[23:24] + jnp.where(has_above, high_u * from_above[old], 0.0)

    def mend_layer(z, carry):
        for tile in range(2):
            for c in range(5):
                s1[c, z + 1, tile, OWN] = s1_in[c, z + 1, tile, OWN]
            mend(lambda c: s1.at[c, z + 1, tile], uy.at[z + 1, tile], z, tile)
        return carry

    lax.fori_loop(0, layers, mend_layer, 0)
    clear_planes(s1)
    for side in range(2):
        for c in range(5):
            strip_s1[c, side, OWN] = strip_s1_in[c, side, OWN]
        mend(lambda c: strip_s1.at[c, side], strip_uy.at[side], None, side)

    state, delta = Field(s1, strip_s1, joint), Field(adj2, strip_adj2, joint2)
    state.join()
    delta.clear()
    delta.clear_strips()

    for side in range(2):
        m, damp = coefficients(strip_coef, strip_base, side)
        wind = (strip_coef[UX, side], strip_uy[side, OWN], strip_coef[UZ, side])
        a = [strip_s1[c, side, OWN] for c in range(5)]
        spin = strip_coef[SPREAD, side]
        out = forward(a, m, damp, spin, wind, state.strip_around(side))
        for c in range(5):
            strip_adj2[c, side, OWN] = out[c] - strip_tgt[c, side]
    delta.join()

    def advance(z, carry):
        for tile in range(2):
            at = (z + 1, tile)
            m, damp = coefficients(coef, base, *at)
            wind = (coef[(UX,) + at], uy[at + (OWN,)], coef[(UZ,) + at])
            a = [state.own(c, z, tile) for c in range(5)]
            out = forward(a, m, damp, coef[(SPREAD,) + at], wind, state.around(z, tile))
            total = 0.0
            for c in range(5):
                miss = out[c] - tgt[c, z, :, span(tile)]
                s2[c, z, :, span(tile)] = out[c]
                adj2[c, z + 1, tile, OWN] = miss
                total = total + miss * a[c]
            dots[z, :, span(tile)] = total
        return carry

    lax.fori_loop(0, layers, advance, 0)

    def put(z, tile, first, new, wind):
        def at(place):
            return line(z, tile * 10 + place, 20, layers)

        high, low = -jnp.minimum(wind[23:24], 0.0), jnp.maximum(wind[8:9], 0.0)
        for c in range(5):
            up[at(c)] = high * first(c)[23:24]
            down[at(c)] = low * first(c)[8:9]
            up[at(5 + c)] = high * new(c)[23:24]
            down[at(5 + c)] = low * new(c)[8:9]

    for side in range(2):
        m, damp = coefficients(strip_coef, strip_base, side)
        a = [strip_s1[c, side, OWN] for c in range(5)]
        b = [strip_adj2[c, side, OWN] for c in range(5)]
        wind = strip_back_wind(strip_coef, strip_uy, side)
        out = backward(b, a, m, damp, wind, delta.strip_around(side))
        for c in range(5):
            strip_adj1[c, side, OWN] = out[c]
        put(
            None,
            side,
            lambda c: strip_adj2.at[c, side],
            lambda c: strip_adj1.at[c, side],
            strip_uy.at[side],
        )
    edge_x = merged(strip_coef, UX, slice(None))

    def retreat(z, carry):
        for tile in range(2):
            at = (z + 1, tile)
            m, damp = coefficients(coef, base, *at)
            a = [state.own(c, z, tile) for c in range(5)]
            b = [delta.own(c, z, tile) for c in range(5)]
            wind = back_wind(coef, uy, edge_x, z, tile)
            out = backward(b, a, m, damp, wind, delta.around(z, tile))
            for c in range(5):
                adj1[c, z + 1, tile, OWN] = out[c]
            put(
                z,
                tile,
                lambda c: adj2.at[c, z + 1, tile],
                lambda c: adj1.at[c, z + 1, tile],
                uy.at[z + 1, tile],
            )
        return carry

    lax.fori_loop(0, layers, retreat, 0)


def third_kernel(
    axis_md,
    axis_cd,
    adj1_in,
    strip_adj1_in,
    dots,
    field,
    from_below,
    from_above,
    start,
    end,
    column,
    adj1,
    strip_adj1,
    first,
    kept,
    second,
    sens,
):
    layers, height, length = dots.shape
    md = lax.axis_index(axis_md)
    count = lax.axis_size(axis_md)
    has_below, has_above = cd_flags(axis_cd)
    odd = lax.axis_index(axis_cd) % 2 == 1

    row = row_iota((height, LANES))
    top = height - 1

    def mended(value, z, place):
        at = line(z, place, 20, layers)
        low = jnp.where(has_below, from_below[at], 0.0)
        high = jnp.where(has_above, from_above[at], 0.0)
        return value + jnp.where(row == 0, low, jnp.where(row == top, high, 0.0))

    for side in range(2):
        for c in range(5):
            value = strip_adj1_in[c, side, OWN]
            strip_adj1[c, side, OWN] = mended(value, None, side * 10 + c)
    Field(adj1, strip_adj1).clear()

    def weigh(z, carry):
        for tile in range(2):
            total = dots[z, :, span(tile)]
            for c in range(5):
                value = mended(adj1_in[c, z + 1, tile, OWN], z, tile * 10 + c)
                adj1[c, z + 1, tile, OWN] = value
                total = total + value * field[c, z + 1, tile, OWN]
            sens[z, :, span(tile)] = -DT * total
        return carry

    lax.fori_loop(0, layers, weigh, 0)

    def feet(ref):
        return jnp.concatenate([feet_block(ref, md + d, count) for d in (-1, 0, 1)], axis=1)

    starts, ends, columns = feet(start), feet(end), feet(column)
    needles = starts.shape[1]
    cells = row_iota((length, needles)) + md * length
    cover = jnp.where((cells >= starts) & (cells < ends), 1.0, 0.0).astype(jnp.bfloat16)
    product = jnp.zeros((layers * height, needles), F32)
    for part in split_three(sens[...].reshape(layers * height, length)):
        product = product + jnp.dot(
            part.astype(jnp.bfloat16), cover, preferred_element_type=F32
        )
    picked = jnp.where(row_iota((height, needles)) == columns, 1.0, 0.0)
    for z in range(layers):
        total = jnp.sum(
            product[z * height : (z + 1) * height] * picked, axis=0, keepdims=True
        )
        first[z : z + 1] = jnp.where(odd, total[:, span(0)], total[:, span(2)])
        kept[z : z + 1] = total[:, span(1)]
        second[z : z + 1] = jnp.where(odd, total[:, span(2)], total[:, span(0)])


def fourth_kernel(
    axis_cd,
    adj1,
    strip_adj1,
    field,
    coef,
    base,
    uy,
    strip_coef,
    weights_below,
    weights_above,
    own_up,
    own_down,
    from_below,
    from_above,
    adj0,
    joint,
):
    layers, height = adj0.shape[1], adj0.shape[2]
    top = height - 1
    has_below, has_above = cd_flags(axis_cd)
    delta = Field(adj1, strip_adj1, joint)
    delta.join()
    edge_x = merged(strip_coef, UX, slice(None))

    def retreat(z, carry):
        for tile in range(2):
            at = (z + 1, tile)
            m, damp = coefficients(coef, base, *at)
            a = [field[c, z + 1, tile, OWN] for c in range(5)]
            b = [delta.own(c, z, tile) for c in range(5)]
            wind = back_wind(coef, uy, edge_x, z, tile)
            out = backward(b, a, m, damp, wind, delta.around(z, tile))
            weight = line(z, tile * 11 + 10, 22, layers)
            low_n, high_n = weights_below[weight], weights_above[weight]
            lanes = span(tile)
            for c in range(5):
                old = line(z, tile * 10 + c, 20, layers)
                new = line(z, tile * 10 + 5 + c, 20, layers)
                low = from_below[new] + low_n * own_down[old]
                high = from_above[new] + high_n * own_up[old]
                low, high = jnp.where(has_below, low, 0.0), jnp.where(has_above, high, 0.0)
                adj0[c, z, :, lanes] = out[c]
                adj0[c, z, 0:1, lanes] = out[c][:1] + low
                adj0[c, z, top:, lanes] = out[c][top:] + high
        return carry

    lax.fori_loop(0, layers, retreat, 0)


def ring(value, axis, steps):
    count = lax.axis_size(axis)
    return lax.ppermute(value, axis, [(i, (i + steps) % count) for i in range(count)])


def winding(value, steps, turn):
    rows, columns = lax.axis_size("md"), lax.axis_size("cd")
    pairs = []
    for column in range(columns):
        for row in range(rows):
            target = row + (steps if column % 2 == turn else -steps)
            if 0 <= target < rows:
                pairs.append((row * columns + column, target * columns + column))
            else:
                pairs.append((row * columns + column, row * columns + (column ^ 1)))
    return lax.ppermute(value, ("md", "cd"), pairs)


def both_ways(value, steps):
    return winding(value, steps, 0), winding(value, steps, 1)


def shape_of(*dims, dtype=F32):
    return jax.ShapeDtypeStruct(dims, dtype)


def scratch(*dims, dtype=F32):
    return pltpu.VMEM(dims, dtype)


def cost(microseconds):
    return pl.CostEstimate(
        flops=int(microseconds * 1e6), bytes_accessed=int(microseconds * 3e6), transcendentals=0
    )


def params(mebibytes):
    return pltpu.CompilerParams(vmem_limit_bytes=mebibytes * 1024 * 1024)


def local(orientation, velocity, velocity_grad, rotary, target, needle_params, *feet):
    _, layers, height, length = orientation.shape
    rotary = rotary[None]
    rates = jnp.transpose(needle_params[:, 0, :])
    feet = [foot.reshape(1, -1) for foot in feet]
    padded = (layers + 2, 2, ROWS, LANES)
    plain = (layers + 2, 2, height, LANES)
    strip_padded, strip = (2, ROWS, LANES), (2, height, LANES)
    message, back_message = shape_of(22 * layers + 24, LANES), shape_of(20 * layers + 24, LANES)
    joint = scratch(5, height, LANES)

    hbm = pl.BlockSpec(memory_space=pltpu.HBM)
    blocks = 4
    packed = pl.pallas_call(
        pack_kernel,
        in_specs=[hbm] * 5 + [pl.BlockSpec(memory_space=pltpu.VMEM)],
        out_shape=shape_of(PLANES, height, LANES),
        scratch_shapes=[
            scratch(NEEDLES, layers, height, length),
            pltpu.SemaphoreType.DMA((blocks, 5)),
        ],
        compiler_params=params(62),
        cost_estimate=cost(4),
    )(orientation, velocity, velocity_grad, rotary, target, rates)
    far = both_ways(rates, 2)
    near = both_ways(packed, 1)

    field, coef, base, uy, s1 = pl.pallas_call(
        bulk_kernel,
        out_shape=[
            shape_of(5, *padded),
            shape_of(COEFS, *plain),
            shape_of(*plain),
            shape_of(*padded),
            shape_of(5, *padded),
        ],
        compiler_params=params(24),
        cost_estimate=cost(3),
    )(orientation, velocity, velocity_grad, rotary)

    s1, base, strip_s0, strip_coef, strip_base, strip_uy, strip_s1, strip_tgt, up, down = (
        pl.pallas_call(
            functools.partial(first_kernel, "md", "cd"),
            out_shape=[
                shape_of(5, *padded),
                shape_of(*plain),
                shape_of(5, *strip_padded),
                shape_of(COEFS, *strip),
                shape_of(*strip),
                shape_of(*strip_padded),
                shape_of(5, *strip_padded),
                shape_of(5, *strip),
                message,
                message,
            ],
            scratch_shapes=[
                scratch(3, layers * height, 4 * LANES, dtype=jnp.bfloat16),
                scratch(length + LANES, 4 * LANES, dtype=jnp.bfloat16),
                scratch(layers, height, length + LANES),
                joint,
            ],
            compiler_params=params(24),
        cost_estimate=cost(4),
        )(
            packed,
            *near,
            *far,
            *feet,
            field,
            coef,
            uy,
            base,
            s1,
        )
    )
    below = ring(up, "cd", 1)
    above = ring(down, "cd", -1)

    s2, adj1, strip_adj1, dots, back_up, back_down = pl.pallas_call(
        functools.partial(second_kernel, "cd"),
        out_shape=[
            shape_of(*orientation.shape),
            shape_of(5, *padded),
            shape_of(5, *strip_padded),
            shape_of(layers, height, length),
            back_message,
            back_message,
        ],
        scratch_shapes=[scratch(5, *padded), scratch(5, *strip_padded)] * 2 + [joint, joint],
        compiler_params=params(24),
        cost_estimate=cost(8),
    )(
        s1,
        strip_s1,
        coef,
        base,
        uy,
        target,
        strip_coef,
        strip_base,
        strip_uy,
        strip_tgt,
        up,
        down,
        below,
        above,
    )
    back_below = ring(back_up, "cd", 1)
    back_above = ring(back_down, "cd", -1)

    part = shape_of(*rates.shape)
    adj1, strip_adj1, part_first, part_own, part_second = pl.pallas_call(
        functools.partial(third_kernel, "md", "cd"),
        out_shape=[shape_of(5, *padded), shape_of(5, *strip_padded), part, part, part],
        scratch_shapes=[scratch(layers, height, length)],
        compiler_params=params(24),
        cost_estimate=cost(1),
    )(adj1, strip_adj1, dots, field, back_below, back_above, *feet)
    part_first = winding(part_first, 1, 0)
    part_second = winding(part_second, 1, 1)

    adj0 = pl.pallas_call(
        functools.partial(fourth_kernel, "cd"),
        out_shape=shape_of(*orientation.shape),
        scratch_shapes=[joint],
        compiler_params=params(24),
        cost_estimate=cost(4),
    )(
        adj1,
        strip_adj1,
        field,
        coef,
        base,
        uy,
        strip_coef,
        below,
        above,
        back_up,
        back_down,
        back_below,
        back_above,
    )
    gradient = part_own + part_first + part_second
    return s2, adj0, jnp.transpose(gradient)[:, None, :]


def solution(mesh):
    field = P(None, None, "cd", "md")
    feet = P(None, "cd")
    needles = P("md", "cd", None)
    return jax.shard_map(
        local,
        mesh=mesh,
        in_specs=(field, field, field, P(None, "cd", "md"), field, needles, feet, feet, feet),
        out_specs=(field, field, needles),
        check_vma=False,
    )
```

```python
import functools

import jax
import jax.numpy as jnp
from jax import lax
from jax.experimental import pallas as pl
from jax.experimental.pallas import tpu as pltpu
from jax.sharding import PartitionSpec as P

XI = 0.95
DT = 0.1
LANES = 128
F32 = jnp.float32
HALO = 4
S0, VEL, GRAD, ROT, TGT, NEEDLES, PLANES = 0, 5, 8, 17, 18, 23, 24
PLACE = {(0, 0): 0, (1, 1): 1, (0, 1): 2, (1, 0): 3, (0, 2): 4, (2, 0): 5, (1, 2): 6, (2, 1): 7}
SPREAD, UX, UZ, COEFS = 8, 9, 10, 11
ROWS = 32
OWN, BEHIND, FRONT = slice(8, 24), slice(7, 23), slice(9, 25)


def lane_iota(shape):
    return lax.broadcasted_iota(jnp.int32, shape, len(shape) - 1)


def row_iota(shape):
    return lax.broadcasted_iota(jnp.int32, shape, len(shape) - 2)


def span(tile):
    return slice(tile * LANES, (tile + 1) * LANES)


def gradient_parts(read):
    g = [read(i) for i in range(9)]
    low = 0.5 * (XI - 1.0) * DT
    m = {}
    for i, j in ((0, 1), (0, 2), (1, 2)):
        a, b = g[3 * i + j], g[3 * j + i]
        both = low * (a + b)
        m[i, j] = DT * a + both
        m[j, i] = DT * b + both
    m[0, 0] = (XI * DT) * (g[0] - g[8])
    m[1, 1] = (XI * DT) * (g[4] - g[8])
    return m


def forward(a, m, base, spread, wind, around):
    a11, a22, a12, a13, a23 = a
    a33 = 1.0 - a11 - a22
    n00 = m[0, 0] * a11 + m[0, 1] * a12 + m[0, 2] * a13
    n01 = m[0, 0] * a12 + m[0, 1] * a22 + m[0, 2] * a23
    n02 = m[0, 0] * a13 + m[0, 1] * a23 + m[0, 2] * a33
    n10 = m[1, 0] * a11 + m[1, 1] * a12 + m[1, 2] * a13
    n11 = m[1, 0] * a12 + m[1, 1] * a22 + m[1, 2] * a23
    n12 = m[1, 0] * a13 + m[1, 1] * a23 + m[1, 2] * a33
    n20 = m[2, 0] * a11 + m[2, 1] * a12
    n21 = m[2, 0] * a12 + m[2, 1] * a22
    n22 = m[2, 0] * a13 + m[2, 1] * a23
    keep = 1.0 - (base + 2.0 * (n00 + n11 + n22))
    gain = (2.0 * n00 + spread, 2.0 * n11 + spread, n01 + n10, n02 + n20, n12 + n21)
    out = []
    for c in range(5):
        total = gain[c] + keep * a[c]
        for u, (behind, front) in zip(wind, around(c)):
            total = total + jnp.abs(u) * jnp.where(u > 0.0, behind, front)
        out.append(total)
    return out


def backward(b, a, m, base, wind, around):
    b1, b2, b3, b4, b5 = b
    a11, a22, a12, a13, a23 = a
    g = -2.0 * (b1 * a11 + b2 * a22 + b3 * a12 + b4 * a13 + b5 * a23)
    trace = (
        m[0, 0] * a11
        + m[1, 1] * a22
        + (m[0, 1] + m[1, 0]) * a12
        + (m[0, 2] + m[2, 0]) * a13
        + (m[1, 2] + m[2, 1]) * a23
    )
    s00, s11, s22 = 2.0 * b1 + g, 2.0 * b2 + g, g
    h00 = m[0, 0] * s00 + m[1, 0] * b3 + m[2, 0] * b4
    h01 = m[0, 0] * b3 + m[1, 0] * s11 + m[2, 0] * b5
    h02 = m[0, 0] * b4 + m[1, 0] * b5 + m[2, 0] * s22
    h10 = m[0, 1] * s00 + m[1, 1] * b3 + m[2, 1] * b4
    h11 = m[0, 1] * b3 + m[1, 1] * s11 + m[2, 1] * b5
    h12 = m[0, 1] * b4 + m[1, 1] * b5 + m[2, 1] * s22
    h20 = m[0, 2] * s00 + m[1, 2] * b3
    h21 = m[0, 2] * b3 + m[1, 2] * s11
    h22 = m[0, 2] * b4 + m[1, 2] * b5
    keep = 1.0 - (base + 2.0 * trace)
    gain = (h00 - h22, h11 - h22, h01 + h10, h02 + h20, h12 + h21)
    weights = [(jnp.minimum(w, 0.0), jnp.maximum(f, 0.0)) for w, f in wind]
    out = []
    for c in range(5):
        total = gain[c] + keep * b[c]
        for (low, high), (behind, front) in zip(weights, around(c)):
            total = total + (high * front - low * behind)
        out.append(total)
    return out


def merged(strips, c, rows):
    left, right = strips[c, 0, rows], strips[c, 1, rows]
    return jnp.where(lane_iota(left.shape) % 8 < HALO, left, right)


def edge_tile(joint, z):
    return pltpu.roll(joint, (2 * LANES - HALO - 8 * z) % LANES, 1)


def x_pair(tiles, tile, edge):
    cur = tiles[tile]
    prev, after = (edge, tiles[1]) if tile == 0 else (tiles[0], edge)
    lane = lane_iota(cur.shape)
    behind = pltpu.roll(jnp.where(lane == LANES - 1, prev, cur), 1, 1)
    front = pltpu.roll(jnp.where(lane == 0, after, cur), LANES - 1, 1)
    return behind, front


def strip_x(cur):
    return pltpu.roll(cur, 1, 1), pltpu.roll(cur, LANES - 1, 1)


def strip_z(cur):
    lane = lane_iota(cur.shape)
    behind = jnp.where(lane < 8, 0.0, pltpu.roll(cur, 8, 1))
    front = jnp.where(lane >= LANES - 8, 0.0, pltpu.roll(cur, LANES - 8, 1))
    return behind, front


def coefficients(coef, base, *at):
    m = {key: coef[(place,) + at] for key, place in PLACE.items()}
    return m, base[at]


class Field:
    def __init__(self, ref, strips, joint=None):
        self.ref, self.strips, self.joint = ref, strips, joint

    def join(self):
        for c in range(self.ref.shape[0]):
            self.joint[c] = merged(self.strips, c, OWN)

    def own(self, c, z, tile):
        return self.ref[c, z + 1, tile, OWN]

    def around(self, z, tile):
        def pairs(c):
            ref = self.ref
            tiles = [ref[c, z + 1, t, OWN] for t in range(2)]
            if self.joint is None:
                edge = jnp.zeros_like(tiles[0])
            else:
                edge = edge_tile(self.joint[c], z)
            return (
                x_pair(tiles, tile, edge),
                (ref[c, z + 1, tile, BEHIND], ref[c, z + 1, tile, FRONT]),
                (ref[c, z, tile, OWN], ref[c, z + 2, tile, OWN]),
            )

        return pairs

    def strip_around(self, side):
        def pairs(c):
            cur = self.strips[c, side, OWN]
            return (
                strip_x(cur),
                (self.strips[c, side, BEHIND], self.strips[c, side, FRONT]),
                strip_z(cur),
            )

        return pairs

    def clear(self):
        last = self.ref.shape[1] - 1
        zero = jnp.zeros((8, LANES), F32)
        clear_planes(self.ref)

        def layer(z, carry):
            for c in range(self.ref.shape[0]):
                for tile in range(2):
                    self.ref[c, z, tile, 0:8] = zero
                    self.ref[c, z, tile, 24:32] = zero
            return carry

        lax.fori_loop(1, last, layer, 0)

    def clear_strips(self):
        zero = jnp.zeros((8, LANES), F32)
        for c in range(self.strips.shape[0]):
            for side in range(2):
                self.strips[c, side, 0:8] = zero
                self.strips[c, side, 24:32] = zero


def clear_planes(ref, planes=None):
    last = ref.shape[1] - 1
    for c in planes or range(ref.shape[0]):
        for tile in range(2):
            for z in (0, last):
                ref[c, z, tile] = jnp.zeros(ref.shape[3:], F32)


def line(z, place, count, layers):
    if z is None:
        return slice(count * layers + place, count * layers + place + 1)
    return pl.ds(place * layers + z, 1)


def planes(place, layers):
    return slice(place * layers, (place + 1) * layers)


def row_place(ref, c, tile, row):
    high, rows = ref.shape[-4], ref.shape[-2]
    total = 1
    for size in ref.shape[:-1]:
        total *= size
    at = ((c * high + 1) * 2 + tile) * rows + row
    return ref.reshape(total, LANES), pl.ds(at, high - 2, stride=2 * rows)


def row_of(ref, c, tile, row):
    flat, place = row_place(ref, c, tile, row)
    return flat[place, :]


def set_row(ref, c, tile, row, value):
    flat, place = row_place(ref, c, tile, row)
    flat[place, :] = value


def layer_pair(cur):
    row, last = row_iota(cur.shape), cur.shape[0] - 1
    behind = jnp.where(row == 0, 0.0, pltpu.roll(cur, 1, 0))
    front = jnp.where(row == last, 0.0, pltpu.roll(cur, last, 0))
    return behind, front


def edge_column(left, right, layers):
    shape = (layers, LANES)
    lane, layer = lane_iota(shape), row_iota(shape)
    low = jnp.sum(jnp.where(lane == 8 * layer + HALO - 1, left, 0.0), axis=1, keepdims=True)
    high = jnp.sum(jnp.where(lane == 8 * layer + HALO, right, 0.0), axis=1, keepdims=True)
    return jnp.where(lane == LANES - 1, low, jnp.where(lane == 0, high, 0.0))


def back_wind(coef, uy, edge_x, z, tile):
    tiles = [coef[UX, z + 1, t] for t in range(2)]
    return (
        x_pair(tiles, tile, edge_tile(edge_x, z)),
        (uy[z + 1, tile, BEHIND], uy[z + 1, tile, FRONT]),
        (coef[UZ, z, tile], coef[UZ, z + 2, tile]),
    )


def strip_back_wind(coef, uy, side):
    return (
        strip_x(coef[UX, side]),
        (uy[side, BEHIND], uy[side, FRONT]),
        strip_z(coef[UZ, side]),
    )


def pack_kernel(s0, vel, grad, rot, tgt, needle, out, stage, sems):
    layers = stage.shape[1]
    blocks = sems.shape[0]
    deep = layers // blocks
    sources = (s0, vel, grad, rot, tgt)

    def copies(block):
        slot, found = 0, []
        for number, ref in enumerate(sources):
            depth = pl.ds(block * deep, deep)
            target = stage.at[pl.ds(slot, ref.shape[0]), depth]
            found.append(
                pltpu.make_async_copy(ref.at[:, depth], target, sems.at[block, number])
            )
            slot += ref.shape[0]
        return found

    for block in range(blocks):
        for copy in copies(block):
            copy.start()
    out[NEEDLES] = needle[...]
    lane = lane_iota(out.shape[1:])

    def step(block, carry):
        for copy in copies(block):
            copy.wait()
        for c in range(NEEDLES):
            total = out[c]
            for k in range(deep):
                z = block * deep + k
                low, high = stage[c, z, :, span(0)], stage[c, z, :, span(1)]
                both = jnp.where(lane < HALO, low, high)
                moved = pltpu.roll(both, (8 * z + HALO) % LANES, 1)
                total = jnp.where(lane // 8 == z, moved, total)
            out[c] = total
        return carry

    lax.fori_loop(0, blocks, step, 0)


def bulk_kernel(s0, vel, grad, rot, field, coef, base, uy, s1):
    layers = s0.shape[1]
    state = Field(field, None)
    state.clear()
    clear_planes(coef, [UZ])

    def load(z, carry):
        zero = jnp.zeros((8, LANES), F32)
        for tile in range(2):
            for c in range(5):
                field[c, z + 1, tile, OWN] = s0[c, z, :, span(tile)]
            u = [DT * vel[d, z, :, span(tile)] for d in range(3)]
            turn = DT * rot[0, z, :, span(tile)]
            for key, value in gradient_parts(lambda i: grad[i, z, :, span(tile)]).items():
                coef[PLACE[key], z + 1, tile] = value
            coef[SPREAD, z + 1, tile] = 2.0 * turn
            coef[UX, z + 1, tile] = u[0]
            coef[UZ, z + 1, tile] = u[2]
            uy[z + 1, tile, 0:8] = zero
            uy[z + 1, tile, 24:32] = zero
            uy[z + 1, tile, OWN] = u[1]
            base[z + 1, tile] = 6.0 * turn + (jnp.abs(u[0]) + jnp.abs(u[1]) + jnp.abs(u[2]))
        return carry

    lax.fori_loop(0, layers, load, 0)

    def advance(z, carry):
        for tile in range(2):
            at = (z + 1, tile)
            m, damp = coefficients(coef, base, *at)
            wind = (coef[(UX,) + at], uy[at + (OWN,)], coef[(UZ,) + at])
            a = [state.own(c, z, tile) for c in range(5)]
            out = forward(a, m, damp, coef[(SPREAD,) + at], wind, state.around(z, tile))
            for c in range(5):
                s1[c, z + 1, tile, OWN] = out[c]
        return carry

    lax.fori_loop(0, layers, advance, 0)


def split_three(value):
    parts = []
    for _ in range(3):
        part = value.astype(jnp.bfloat16).astype(F32)
        parts.append(part)
        value = value - part
    return parts


def feet_block(ref, block, count):
    place = jnp.clip(block, 0, count - 1) * LANES
    row = ref[:, pl.ds(pl.multiple_of(place, LANES), LANES)]
    return jnp.where((block >= 0) & (block < count), row, 0)


def first_kernel(
    axis_md,
    axis_cd,
    own,
    near_first,
    near_second,
    far_first,
    far_second,
    start,
    end,
    column,
    field,
    coef,
    uy,
    base_in,
    s1_in,
    s1,
    base,
    strip_s0,
    strip_coef,
    strip_base,
    strip_uy,
    strip_s1,
    strip_tgt,
    up,
    down,
    spread,
    cover,
    source,
    joint,
):
    layers = field.shape[1] - 2
    height = own.shape[1]
    md = lax.axis_index(axis_md)
    count = lax.axis_size(axis_md)
    lane = lane_iota((height, LANES))
    outer = lane % 8 < HALO
    odd = lax.axis_index(axis_cd) % 2 == 1

    def from_left(c):
        return jnp.where(odd, near_second[c], near_first[c])

    def from_right(c):
        return jnp.where(odd, near_first[c], near_second[c])

    near = lane_iota((1, LANES)) < LANES // 2

    def feet(ref):
        far = jnp.where(near, feet_block(ref, md + 2, count), feet_block(ref, md - 2, count))
        blocks = [feet_block(ref, md + d, count) for d in (-1, 0, 1)]
        return jnp.concatenate(blocks + [far], axis=1)

    starts, ends, columns = feet(start), feet(end), feet(column)
    far = jnp.where((lane < LANES // 2) == odd, far_first[...], far_second[...])
    rates = jnp.concatenate(
        [from_left(NEEDLES), own[NEEDLES], from_right(NEEDLES), far], axis=1
    )
    needles = rates.shape[1]
    picked = jnp.where(row_iota((height, needles)) == columns, 1.0, 0.0)
    for part, value in enumerate(split_three(rates)):
        for z in range(layers):
            spread[part, z * height : (z + 1) * height] = (picked * value[z : z + 1]).astype(
                jnp.bfloat16
            )
    length = 2 * LANES
    cells = row_iota((length + LANES, needles))
    beyond = cells - length
    strip = jnp.where(beyond < 8, beyond - HALO, beyond - 8 + length - HALO)
    cells = jnp.where(cells < length, cells, strip) + md * length
    cover[...] = jnp.where((cells >= starts) & (cells < ends), 1.0, 0.0).astype(jnp.bfloat16)
    product = jnp.zeros((layers * height, length + LANES), F32)
    for part in range(3):
        product = product + lax.dot_general(
            spread[part], cover[...], (((1,), (1,)), ((), ())), preferred_element_type=F32
        )
    source[...] = (DT * product).reshape(source.shape)

    state = Field(field, strip_s0, joint)
    state.clear_strips()
    has_left, has_right = md > 0, md < count - 1
    for side in range(2):

        def raw(c):
            if side == 0:
                return jnp.where(outer, jnp.where(has_left, from_left(c), 0.0), own[c])
            return jnp.where(outer, own[c], jnp.where(has_right, from_right(c), 0.0))

        for c in range(5):
            strip_s0[c, side, OWN] = raw(S0 + c)
            strip_tgt[c, side] = raw(TGT + c)
        u = [DT * raw(VEL + d) for d in range(3)]
        turn = DT * raw(ROT)
        for key, value in gradient_parts(lambda i: raw(GRAD + i)).items():
            strip_coef[PLACE[key], side] = value
        strip_coef[SPREAD, side] = 2.0 * turn
        strip_coef[UX, side] = u[0]
        strip_coef[UZ, side] = u[2]
        strip_uy[side, 0:8] = jnp.zeros((8, LANES), F32)
        strip_uy[side, 24:32] = jnp.zeros((8, LANES), F32)
        strip_uy[side, OWN] = u[1]
        damp = 6.0 * turn + (jnp.abs(u[0]) + jnp.abs(u[1]) + jnp.abs(u[2]))
        taken = jnp.zeros((height, LANES), F32)
        for z in range(layers):
            moved = pltpu.roll(source[z, :, span(2)], (8 * z - 8 * side) % LANES, 1)
            taken = jnp.where(lane // 8 == z, moved, taken)
        strip_base[side] = damp + taken

    for side in range(2):
        m, damp = coefficients(strip_coef, strip_base, side)
        wind = (strip_coef[UX, side], strip_uy[side, OWN], strip_coef[UZ, side])
        a = [strip_s0[c, side, OWN] for c in range(5)]
        spin = strip_coef[SPREAD, side]
        out = forward(a, m, damp, spin, wind, state.strip_around(side))
        for c in range(5):
            strip_s1[c, side, OWN] = out[c]
    state.join()

    def put(side):
        def at(place):
            return line(None, side * 11 + place, 22, layers)

        for c in range(5):
            first, new = strip_s0.at[c, side], strip_s1.at[c, side]
            up[at(c)], down[at(c)] = first[23:24], first[8:9]
            up[at(5 + c)], down[at(5 + c)] = new[23:24], new[8:9]
        wind = strip_uy.at[side]
        up[at(10)] = -jnp.minimum(wind[23:24], 0.0)
        down[at(10)] = jnp.maximum(wind[8:9], 0.0)

    def mend(z, carry):
        for tile in range(2):
            gain = source[z, :, span(tile)]
            base[z + 1, tile] = base_in[z + 1, tile] + gain
            u = coef[UX, z + 1, tile]
            if tile == 0:
                weight, turn = jnp.where(lane == 0, jnp.maximum(u, 0.0), 0.0), 1
            else:
                weight, turn = jnp.where(lane == LANES - 1, -jnp.minimum(u, 0.0), 0.0), -1
            for c in range(5):
                edge = pltpu.roll(joint[c], (2 * LANES - HALO + turn - 8 * z) % LANES, 1)
                s1[c, z + 1, tile, OWN] = (
                    s1_in[c, z + 1, tile, OWN]
                    - gain * field[c, z + 1, tile, OWN]
                    + weight * edge
                )
        return carry

    clear_planes(s1)
    lax.fori_loop(0, layers, mend, 0)
    for tile in range(2):
        for message, row in ((up, 23), (down, 8)):
            for c in range(5):
                message[planes(tile * 11 + c, layers)] = row_of(field, c, tile, row)
                message[planes(tile * 11 + 5 + c, layers)] = row_of(s1, c, tile, row)
        out, into = row_of(uy, 0, tile, 23), row_of(uy, 0, tile, 8)
        up[planes(tile * 11 + 10, layers)] = -jnp.minimum(out, 0.0)
        down[planes(tile * 11 + 10, layers)] = jnp.maximum(into, 0.0)
    for side in range(2):
        put(side)


def cd_flags(axis_cd):
    cd = lax.axis_index(axis_cd)
    return cd > 0, cd < lax.axis_size(axis_cd) - 1


def advance_kernel(s1, strip_s1, coef, base, uy, tgt, s2, goal, joint):
    layers = tgt.shape[1]
    state = Field(s1, strip_s1, joint)
    state.join()

    def advance(z, carry):
        for tile in range(2):
            at = (z + 1, tile)
            m, damp = coefficients(coef, base, *at)
            wind = (coef[(UX,) + at], uy[at + (OWN,)], coef[(UZ,) + at])
            a = [state.own(c, z, tile) for c in range(5)]
            out = forward(a, m, damp, coef[(SPREAD,) + at], wind, state.around(z, tile))
            for c in range(5):
                s2[(c,) + at] = out[c]
                goal[(c,) + at] = tgt[c, z, :, span(tile)]
        return carry

    lax.fori_loop(0, layers, advance, 0)


def edge_kernel(
    axis_cd,
    s1,
    strip_s1_in,
    coef,
    base,
    uy,
    goal,
    strip_coef,
    strip_base,
    strip_uy,
    strip_tgt,
    own_up,
    own_down,
    from_below,
    from_above,
    s1_edge,
    s2_edge,
    strip_adj2,
    strip_adj1,
    up,
    down,
    strip_s1,
):
    layers = goal.shape[1] - 2
    has_below, has_above = cd_flags(axis_cd)

    state, delta = Field(s1, strip_s1), Field(s1, strip_adj2)
    delta.clear_strips()
    for side in range(2):

        def at(place):
            return line(None, side * 11 + place, 22, layers)

        wind = strip_uy.at[side]
        low_u, high_u = jnp.maximum(wind[8:9], 0.0), -jnp.minimum(wind[23:24], 0.0)
        low_n, high_n = from_below[at(10)], from_above[at(10)]
        for c in range(5):
            old, new = at(c), at(5 + c)
            ref = strip_s1.at[c, side]
            ref[OWN] = strip_s1_in[c, side, OWN]
            low = from_below[new] + low_n * own_down[old]
            high = from_above[new] + high_n * own_up[old]
            ref[7:8] = jnp.where(has_below, low, 0.0)
            ref[24:25] = jnp.where(has_above, high, 0.0)
            ref[8:9] = ref[8:9] + jnp.where(has_below, low_u * from_below[old], 0.0)
            ref[23:24] = ref[23:24] + jnp.where(has_above, high_u * from_above[old], 0.0)
    for side in range(2):
        m, damp = coefficients(strip_coef, strip_base, side)
        wind = (strip_coef[UX, side], strip_uy[side, OWN], strip_coef[UZ, side])
        a = [strip_s1[c, side, OWN] for c in range(5)]
        spin = strip_coef[SPREAD, side]
        out = forward(a, m, damp, spin, wind, state.strip_around(side))
        for c in range(5):
            strip_adj2[c, side, OWN] = out[c] - strip_tgt[c, side]
    for side in range(2):

        def at(place):
            return line(None, side * 10 + place, 20, layers)

        m, damp = coefficients(strip_coef, strip_base, side)
        a = [strip_s1[c, side, OWN] for c in range(5)]
        b = [strip_adj2[c, side, OWN] for c in range(5)]
        wind = strip_back_wind(strip_coef, strip_uy, side)
        out = backward(b, a, m, damp, wind, delta.strip_around(side))
        high = -jnp.minimum(strip_uy[side, 23:24], 0.0)
        low = jnp.maximum(strip_uy[side, 8:9], 0.0)
        for c in range(5):
            strip_adj1[c, side, OWN] = out[c]
            up[at(c)] = high * b[c][-1:]
            down[at(c)] = low * b[c][:1]
            up[at(5 + c)] = high * out[c][-1:]
            down[at(5 + c)] = low * out[c][:1]

    def constants(tile, row):
        m = {key: row_of(coef, place, tile, row) for key, place in PLACE.items()}
        return m, row_of(base, 0, tile, row)

    for number, (message, mine, valid, outgoing) in enumerate(
        ((from_below, own_down, has_below, down), (from_above, own_up, has_above, up))
    ):
        rows = (0, 1, 2) if number == 0 else (15, 14, 13)
        sides = (0, 1)

        def plane(ref, place, tile):
            return ref[planes(tile * 11 + place, layers)]

        lines = [{}, {}, {}, {}]
        for c in range(5):
            for tile in range(2):
                old, new = plane(message, c, tile), plane(message, 5 + c, tile)
                weight = plane(message, 10, tile)
                lines[0][c, tile] = jnp.where(
                    valid, new + weight * plane(mine, c, tile), 0.0
                )
                lines[1][c, tile] = plane(mine, 5 + c, tile) + jnp.where(
                    valid, plane(mine, 10, tile) * old, 0.0
                )
                s1_edge[c, number, tile] = lines[1][c, tile]
                for k in (1, 2):
                    lines[k + 1][c, tile] = row_of(s1, c, tile, 8 + rows[k])

        def strip_edge(ref, c, row):
            left, right = (ref[c, side, 8 + row : 9 + row] for side in sides)
            return edge_column(left, right, layers)

        def ordered(outer, inner):
            return (outer, inner) if number == 0 else (inner, outer)

        misses = [{}, {}]
        for k in range(2):
            row = rows[k]
            edges = [strip_edge(strip_s1, c, row) for c in range(5)]
            for tile in range(2):
                m, damp = constants(tile, row)
                wind = (
                    row_of(coef, UX, tile, row),
                    row_of(uy, 0, tile, 8 + row),
                    row_of(coef, UZ, tile, row),
                )
                a = [lines[k + 1][c, tile] for c in range(5)]

                def around(c):
                    tiles = [lines[k + 1][c, t] for t in range(2)]
                    return (
                        x_pair(tiles, tile, edges[c]),
                        ordered(lines[k][c, tile], lines[k + 2][c, tile]),
                        layer_pair(a[c]),
                    )

                out = forward(a, m, damp, row_of(coef, SPREAD, tile, row), wind, around)
                for c in range(5):
                    s2_edge[c, 2 * number + k, tile] = out[c]
                    misses[k][c, tile] = out[c] - row_of(goal, c, tile, row)

        row = rows[0]
        edges = [strip_edge(strip_adj2, c, row) for c in range(5)]
        left, right = (strip_coef[UX, side, row : row + 1] for side in sides)
        edge_x = edge_column(left, right, layers)
        for tile in range(2):
            m, damp = constants(tile, row)
            a = [lines[1][c, tile] for c in range(5)]
            b = [misses[0][c, tile] for c in range(5)]
            zero = jnp.zeros_like(b[0])
            wind = (
                x_pair([row_of(coef, UX, t, row) for t in range(2)], tile, edge_x),
                ordered(zero, row_of(uy, 0, tile, 8 + rows[1])),
                layer_pair(row_of(coef, UZ, tile, row)),
            )

            def around(c):
                tiles = [misses[0][c, t] for t in range(2)]
                return (
                    x_pair(tiles, tile, edges[c]),
                    ordered(zero, misses[1][c, tile]),
                    layer_pair(b[c]),
                )

            out = backward(b, a, m, damp, wind, around)
            weight = plane(mine, 10, tile)
            for c in range(5):
                outgoing[planes(tile * 10 + c, layers)] = weight * b[c]
                outgoing[planes(tile * 10 + 5 + c, layers)] = weight * out[c]


def second_kernel(
    s1_in,
    s2_in,
    goal,
    s1_edge,
    s2_edge,
    coef,
    base,
    uy,
    strip_coef,
    strip_adj2,
    s2_out,
    adj1,
    dots,
    s1,
    s2,
    adj2,
    joint,
):
    layers = goal.shape[1] - 2

    def gather(z, carry):
        for tile in range(2):
            for c in range(5):
                s1[c, z + 1, tile] = s1_in[c, z + 1, tile, OWN]
                s2[c, z + 1, tile] = s2_in[c, z + 1, tile]
        return carry

    lax.fori_loop(0, layers, gather, 0)
    for c in range(5):
        for tile in range(2):
            for number, row in enumerate((0, 15)):
                set_row(s1, c, tile, row, s1_edge[c, number, tile])
            for number, row in enumerate((0, 1, 15, 14)):
                set_row(s2, c, tile, row, s2_edge[c, number, tile])

    delta = Field(adj2, strip_adj2, joint)
    delta.clear()
    delta.join()

    def compare(z, carry):
        for tile in range(2):
            total = 0.0
            for c in range(5):
                value = s2[c, z + 1, tile]
                miss = value - goal[c, z + 1, tile]
                s2_out[c, z, :, span(tile)] = value
                adj2[c, z + 1, tile, OWN] = miss
                total = total + miss * s1[c, z + 1, tile]
            dots[z, :, span(tile)] = total
        return carry

    lax.fori_loop(0, layers, compare, 0)
    edge_x = merged(strip_coef, UX, slice(None))

    def retreat(z, carry):
        for tile in range(2):
            m, damp = coefficients(coef, base, z + 1, tile)
            a = [s1[c, z + 1, tile] for c in range(5)]
            b = [delta.own(c, z, tile) for c in range(5)]
            wind = back_wind(coef, uy, edge_x, z, tile)
            out = backward(b, a, m, damp, wind, delta.around(z, tile))
            for c in range(5):
                adj1[c, z + 1, tile, OWN] = out[c]
        return carry

    lax.fori_loop(0, layers, retreat, 0)


def third_kernel(
    axis_md,
    axis_cd,
    adj1_in,
    strip_adj1_in,
    dots,
    field,
    from_below,
    from_above,
    start,
    end,
    column,
    adj1,
    strip_adj1,
    first,
    kept,
    second,
    sens,
):
    layers, height, length = dots.shape
    md = lax.axis_index(axis_md)
    count = lax.axis_size(axis_md)
    has_below, has_above = cd_flags(axis_cd)
    odd = lax.axis_index(axis_cd) % 2 == 1

    row = row_iota((height, LANES))
    top = height - 1

    def mended(value, z, place):
        at = line(z, place, 20, layers)
        low = jnp.where(has_below, from_below[at], 0.0)
        high = jnp.where(has_above, from_above[at], 0.0)
        return value + jnp.where(row == 0, low, jnp.where(row == top, high, 0.0))

    for side in range(2):
        for c in range(5):
            value = strip_adj1_in[c, side, OWN]
            strip_adj1[c, side, OWN] = mended(value, None, side * 10 + c)
    Field(adj1, strip_adj1).clear()

    def weigh(z, carry):
        for tile in range(2):
            total = dots[z, :, span(tile)]
            for c in range(5):
                value = mended(adj1_in[c, z + 1, tile, OWN], z, tile * 10 + c)
                adj1[c, z + 1, tile, OWN] = value
                total = total + value * field[c, z + 1, tile, OWN]
            sens[z, :, span(tile)] = -DT * total
        return carry

    lax.fori_loop(0, layers, weigh, 0)

    def feet(ref):
        return jnp.concatenate([feet_block(ref, md + d, count) for d in (-1, 0, 1)], axis=1)

    starts, ends, columns = feet(start), feet(end), feet(column)
    needles = starts.shape[1]
    cells = row_iota((length, needles)) + md * length
    cover = jnp.where((cells >= starts) & (cells < ends), 1.0, 0.0).astype(jnp.bfloat16)
    product = jnp.zeros((layers * height, needles), F32)
    for part in split_three(sens[...].reshape(layers * height, length)):
        product = product + jnp.dot(
            part.astype(jnp.bfloat16), cover, preferred_element_type=F32
        )
    picked = jnp.where(row_iota((height, needles)) == columns, 1.0, 0.0)
    for z in range(layers):
        total = jnp.sum(
            product[z * height : (z + 1) * height] * picked, axis=0, keepdims=True
        )
        first[z : z + 1] = jnp.where(odd, total[:, span(0)], total[:, span(2)])
        kept[z : z + 1] = total[:, span(1)]
        second[z : z + 1] = jnp.where(odd, total[:, span(2)], total[:, span(0)])


def fourth_kernel(
    axis_cd,
    adj1,
    strip_adj1,
    field,
    coef,
    base,
    uy,
    strip_coef,
    weights_below,
    weights_above,
    own_up,
    own_down,
    from_below,
    from_above,
    adj0,
    joint,
):
    layers, height = adj0.shape[1], adj0.shape[2]
    top = height - 1
    has_below, has_above = cd_flags(axis_cd)
    delta = Field(adj1, strip_adj1, joint)
    delta.join()
    edge_x = merged(strip_coef, UX, slice(None))

    def retreat(z, carry):
        for tile in range(2):
            at = (z + 1, tile)
            m, damp = coefficients(coef, base, *at)
            a = [field[c, z + 1, tile, OWN] for c in range(5)]
            b = [delta.own(c, z, tile) for c in range(5)]
            wind = back_wind(coef, uy, edge_x, z, tile)
            out = backward(b, a, m, damp, wind, delta.around(z, tile))
            weight = line(z, tile * 11 + 10, 22, layers)
            low_n, high_n = weights_below[weight], weights_above[weight]
            lanes = span(tile)
            for c in range(5):
                old = line(z, tile * 10 + c, 20, layers)
                new = line(z, tile * 10 + 5 + c, 20, layers)
                low = from_below[new] + low_n * own_down[old]
                high = from_above[new] + high_n * own_up[old]
                low, high = jnp.where(has_below, low, 0.0), jnp.where(has_above, high, 0.0)
                adj0[c, z, :, lanes] = out[c]
                adj0[c, z, 0:1, lanes] = out[c][:1] + low
                adj0[c, z, top:, lanes] = out[c][top:] + high
        return carry

    lax.fori_loop(0, layers, retreat, 0)


def ring(value, axis, steps):
    count = lax.axis_size(axis)
    return lax.ppermute(value, axis, [(i, (i + steps) % count) for i in range(count)])


def winding(value, steps, turn):
    rows, columns = lax.axis_size("md"), lax.axis_size("cd")
    pairs = []
    for column in range(columns):
        for row in range(rows):
            target = row + (steps if column % 2 == turn else -steps)
            if 0 <= target < rows:
                pairs.append((row * columns + column, target * columns + column))
            else:
                pairs.append((row * columns + column, row * columns + (column ^ 1)))
    return lax.ppermute(value, ("md", "cd"), pairs)


def both_ways(value, steps):
    return winding(value, steps, 0), winding(value, steps, 1)


def shape_of(*dims, dtype=F32):
    return jax.ShapeDtypeStruct(dims, dtype)


def scratch(*dims, dtype=F32):
    return pltpu.VMEM(dims, dtype)


def cost(microseconds):
    return pl.CostEstimate(
        flops=int(microseconds * 1e6), bytes_accessed=int(microseconds * 3e6), transcendentals=0
    )


def params(mebibytes):
    return pltpu.CompilerParams(vmem_limit_bytes=mebibytes * 1024 * 1024)


def local(orientation, velocity, velocity_grad, rotary, target, needle_params, *feet):
    _, layers, height, length = orientation.shape
    rotary = rotary[None]
    rates = jnp.transpose(needle_params[:, 0, :])
    feet = [foot.reshape(1, -1) for foot in feet]
    padded = (layers + 2, 2, ROWS, LANES)
    plain = (layers + 2, 2, height, LANES)
    strip_padded, strip = (2, ROWS, LANES), (2, height, LANES)
    message, back_message = shape_of(22 * layers + 24, LANES), shape_of(20 * layers + 24, LANES)
    joint = scratch(5, height, LANES)

    hbm = pl.BlockSpec(memory_space=pltpu.HBM)
    blocks = 4
    packed = pl.pallas_call(
        pack_kernel,
        in_specs=[hbm] * 5 + [pl.BlockSpec(memory_space=pltpu.VMEM)],
        out_shape=shape_of(PLANES, height, LANES),
        scratch_shapes=[
            scratch(NEEDLES, layers, height, length),
            pltpu.SemaphoreType.DMA((blocks, 5)),
        ],
        compiler_params=params(62),
        cost_estimate=cost(4),
    )(orientation, velocity, velocity_grad, rotary, target, rates)
    far = both_ways(rates, 2)
    near = both_ways(packed, 1)

    field, coef, base, uy, s1 = pl.pallas_call(
        bulk_kernel,
        out_shape=[
            shape_of(5, *padded),
            shape_of(COEFS, *plain),
            shape_of(*plain),
            shape_of(*padded),
            shape_of(5, *padded),
        ],
        compiler_params=params(24),
        cost_estimate=cost(3),
    )(orientation, velocity, velocity_grad, rotary)

    s1, base, strip_s0, strip_coef, strip_base, strip_uy, strip_s1, strip_tgt, up, down = (
        pl.pallas_call(
            functools.partial(first_kernel, "md", "cd"),
            out_shape=[
                shape_of(5, *padded),
                shape_of(*plain),
                shape_of(5, *strip_padded),
                shape_of(COEFS, *strip),
                shape_of(*strip),
                shape_of(*strip_padded),
                shape_of(5, *strip_padded),
                shape_of(5, *strip),
                message,
                message,
            ],
            scratch_shapes=[
                scratch(3, layers * height, 4 * LANES, dtype=jnp.bfloat16),
                scratch(length + LANES, 4 * LANES, dtype=jnp.bfloat16),
                scratch(layers, height, length + LANES),
                joint,
            ],
            compiler_params=params(24),
        cost_estimate=cost(4),
        )(
            packed,
            *near,
            *far,
            *feet,
            field,
            coef,
            uy,
            base,
            s1,
        )
    )
    below = ring(up, "cd", 1)
    above = ring(down, "cd", -1)

    s2_part, goal = pl.pallas_call(
        advance_kernel,
        out_shape=[shape_of(5, *plain), shape_of(5, *plain)],
        scratch_shapes=[joint],
        compiler_params=params(16),
        cost_estimate=cost(4),
    )(s1, strip_s1, coef, base, uy, target)
    s1_edge, s2_edge, strip_adj2, strip_adj1, back_up, back_down = pl.pallas_call(
        functools.partial(edge_kernel, "cd"),
        out_shape=[
            shape_of(5, 2, 2, layers, LANES),
            shape_of(5, 4, 2, layers, LANES),
            shape_of(5, *strip_padded),
            shape_of(5, *strip_padded),
            back_message,
            back_message,
        ],
        scratch_shapes=[scratch(5, *strip_padded)],
        compiler_params=params(16),
        cost_estimate=cost(2),
    )(
        s1,
        strip_s1,
        coef,
        base,
        uy,
        goal,
        strip_coef,
        strip_base,
        strip_uy,
        strip_tgt,
        up,
        down,
        below,
        above,
    )
    back_below = ring(back_up, "cd", 1)
    back_above = ring(back_down, "cd", -1)

    s2, adj1, dots = pl.pallas_call(
        second_kernel,
        out_shape=[
            shape_of(*orientation.shape),
            shape_of(5, *padded),
            shape_of(layers, height, length),
        ],
        scratch_shapes=[
            scratch(5, *plain),
            scratch(5, *plain),
            scratch(5, *padded),
            joint,
        ],
        compiler_params=params(24),
        cost_estimate=cost(6),
    )(
        s1,
        s2_part,
        goal,
        s1_edge,
        s2_edge,
        coef,
        base,
        uy,
        strip_coef,
        strip_adj2,
    )

    part = shape_of(*rates.shape)
    adj1, strip_adj1, part_first, part_own, part_second = pl.pallas_call(
        functools.partial(third_kernel, "md", "cd"),
        out_shape=[shape_of(5, *padded), shape_of(5, *strip_padded), part, part, part],
        scratch_shapes=[scratch(layers, height, length)],
        compiler_params=params(24),
        cost_estimate=cost(1),
    )(adj1, strip_adj1, dots, field, back_below, back_above, *feet)
    part_first = winding(part_first, 1, 0)
    part_second = winding(part_second, 1, 1)

    adj0 = pl.pallas_call(
        functools.partial(fourth_kernel, "cd"),
        out_shape=shape_of(*orientation.shape),
        scratch_shapes=[joint],
        compiler_params=params(24),
        cost_estimate=cost(4),
    )(
        adj1,
        strip_adj1,
        field,
        coef,
        base,
        uy,
        strip_coef,
        below,
        above,
        back_up,
        back_down,
        back_below,
        back_above,
    )
    gradient = part_own + part_first + part_second
    return s2, adj0, jnp.transpose(gradient)[:, None, :]


def solution(mesh):
    field = P(None, None, "cd", "md")
    feet = P(None, "cd")
    needles = P("md", "cd", None)
    return jax.shard_map(
        local,
        mesh=mesh,
        in_specs=(field, field, field, P(None, "cd", "md"), field, needles, feet, feet, feet),
        out_specs=(field, field, needles),
        check_vma=False,
    )
```

```python
import functools

import jax
import jax.numpy as jnp
from jax import lax
from jax.experimental import pallas as pl
from jax.experimental.pallas import tpu as pltpu
from jax.sharding import PartitionSpec as P

XI = 0.95
DT = 0.1
LANES = 128
F32 = jnp.float32
HALO = 4
S0, VEL, GRAD, ROT, TGT, NEEDLES = 0, 5, 8, 17, 18, 23
PAIRS = 12
PLACE = {(0, 0): 0, (1, 1): 1, (0, 1): 2, (1, 0): 3, (0, 2): 4, (2, 0): 5, (1, 2): 6, (2, 1): 7}
SPREAD, UX, UZ, COEFS = 8, 9, 10, 11
ROWS = 32
OWN, BEHIND, FRONT = slice(8, 24), slice(7, 23), slice(9, 25)


def lane_iota(shape):
    return lax.broadcasted_iota(jnp.int32, shape, len(shape) - 1)


def row_iota(shape):
    return lax.broadcasted_iota(jnp.int32, shape, len(shape) - 2)


def span(tile):
    return slice(tile * LANES, (tile + 1) * LANES)


def gradient_parts(read):
    g = [read(i) for i in range(9)]
    low = 0.5 * (XI - 1.0) * DT
    m = {}
    for i, j in ((0, 1), (0, 2), (1, 2)):
        a, b = g[3 * i + j], g[3 * j + i]
        both = low * (a + b)
        m[i, j] = DT * a + both
        m[j, i] = DT * b + both
    m[0, 0] = (XI * DT) * (g[0] - g[8])
    m[1, 1] = (XI * DT) * (g[4] - g[8])
    return m


def forward(a, m, base, spread, wind, around):
    a11, a22, a12, a13, a23 = a
    a33 = 1.0 - a11 - a22
    n00 = m[0, 0] * a11 + m[0, 1] * a12 + m[0, 2] * a13
    n01 = m[0, 0] * a12 + m[0, 1] * a22 + m[0, 2] * a23
    n02 = m[0, 0] * a13 + m[0, 1] * a23 + m[0, 2] * a33
    n10 = m[1, 0] * a11 + m[1, 1] * a12 + m[1, 2] * a13
    n11 = m[1, 0] * a12 + m[1, 1] * a22 + m[1, 2] * a23
    n12 = m[1, 0] * a13 + m[1, 1] * a23 + m[1, 2] * a33
    n20 = m[2, 0] * a11 + m[2, 1] * a12
    n21 = m[2, 0] * a12 + m[2, 1] * a22
    n22 = m[2, 0] * a13 + m[2, 1] * a23
    keep = 1.0 - (base + 2.0 * (n00 + n11 + n22))
    gain = (2.0 * n00 + spread, 2.0 * n11 + spread, n01 + n10, n02 + n20, n12 + n21)
    out = []
    for c in range(5):
        total = gain[c] + keep * a[c]
        for u, (behind, front) in zip(wind, around(c)):
            total = total + jnp.abs(u) * jnp.where(u > 0.0, behind, front)
        out.append(total)
    return out


def backward(b, a, m, base, wind, around):
    b1, b2, b3, b4, b5 = b
    a11, a22, a12, a13, a23 = a
    g = -2.0 * (b1 * a11 + b2 * a22 + b3 * a12 + b4 * a13 + b5 * a23)
    trace = (
        m[0, 0] * a11
        + m[1, 1] * a22
        + (m[0, 1] + m[1, 0]) * a12
        + (m[0, 2] + m[2, 0]) * a13
        + (m[1, 2] + m[2, 1]) * a23
    )
    s00, s11, s22 = 2.0 * b1 + g, 2.0 * b2 + g, g
    h00 = m[0, 0] * s00 + m[1, 0] * b3 + m[2, 0] * b4
    h01 = m[0, 0] * b3 + m[1, 0] * s11 + m[2, 0] * b5
    h02 = m[0, 0] * b4 + m[1, 0] * b5 + m[2, 0] * s22
    h10 = m[0, 1] * s00 + m[1, 1] * b3 + m[2, 1] * b4
    h11 = m[0, 1] * b3 + m[1, 1] * s11 + m[2, 1] * b5
    h12 = m[0, 1] * b4 + m[1, 1] * b5 + m[2, 1] * s22
    h20 = m[0, 2] * s00 + m[1, 2] * b3
    h21 = m[0, 2] * b3 + m[1, 2] * s11
    h22 = m[0, 2] * b4 + m[1, 2] * b5
    keep = 1.0 - (base + 2.0 * trace)
    gain = (h00 - h22, h11 - h22, h01 + h10, h02 + h20, h12 + h21)
    weights = [(jnp.minimum(w, 0.0), jnp.maximum(f, 0.0)) for w, f in wind]
    out = []
    for c in range(5):
        total = gain[c] + keep * b[c]
        for (low, high), (behind, front) in zip(weights, around(c)):
            total = total + (high * front - low * behind)
        out.append(total)
    return out


def merged(strips, c, rows):
    left, right = strips[c, 0, rows], strips[c, 1, rows]
    return jnp.where(lane_iota(left.shape) % 8 < HALO, left, right)


def edge_tile(joint, z):
    return pltpu.roll(joint, (2 * LANES - HALO - 8 * z) % LANES, 1)


def x_pair(tiles, tile, edge):
    cur = tiles[tile]
    prev, after = (edge, tiles[1]) if tile == 0 else (tiles[0], edge)
    lane = lane_iota(cur.shape)
    behind = pltpu.roll(jnp.where(lane == LANES - 1, prev, cur), 1, 1)
    front = pltpu.roll(jnp.where(lane == 0, after, cur), LANES - 1, 1)
    return behind, front


def strip_x(cur):
    return pltpu.roll(cur, 1, 1), pltpu.roll(cur, LANES - 1, 1)


def strip_z(cur):
    lane = lane_iota(cur.shape)
    behind = jnp.where(lane < 8, 0.0, pltpu.roll(cur, 8, 1))
    front = jnp.where(lane >= LANES - 8, 0.0, pltpu.roll(cur, LANES - 8, 1))
    return behind, front


def coefficients(coef, base, *at):
    m = {key: coef[(place,) + at] for key, place in PLACE.items()}
    return m, base[at]


class Field:
    def __init__(self, ref, strips, joint=None):
        self.ref, self.strips, self.joint = ref, strips, joint

    def join(self):
        for c in range(self.ref.shape[0]):
            self.joint[c] = merged(self.strips, c, OWN)

    def own(self, c, z, tile):
        return self.ref[c, z + 1, tile, OWN]

    def around(self, z, tile):
        def pairs(c):
            ref = self.ref
            tiles = [ref[c, z + 1, t, OWN] for t in range(2)]
            if self.joint is None:
                edge = jnp.zeros_like(tiles[0])
            else:
                edge = edge_tile(self.joint[c], z)
            return (
                x_pair(tiles, tile, edge),
                (ref[c, z + 1, tile, BEHIND], ref[c, z + 1, tile, FRONT]),
                (ref[c, z, tile, OWN], ref[c, z + 2, tile, OWN]),
            )

        return pairs

    def strip_around(self, side):
        def pairs(c):
            cur = self.strips[c, side, OWN]
            return (
                strip_x(cur),
                (self.strips[c, side, BEHIND], self.strips[c, side, FRONT]),
                strip_z(cur),
            )

        return pairs

    def clear(self):
        last = self.ref.shape[1] - 1
        zero = jnp.zeros((8, LANES), F32)
        clear_planes(self.ref)

        def layer(z, carry):
            for c in range(self.ref.shape[0]):
                for tile in range(2):
                    self.ref[c, z, tile, 0:8] = zero
                    self.ref[c, z, tile, 24:32] = zero
            return carry

        lax.fori_loop(1, last, layer, 0)

    def clear_strips(self):
        zero = jnp.zeros((8, LANES), F32)
        for c in range(self.strips.shape[0]):
            for side in range(2):
                self.strips[c, side, 0:8] = zero
                self.strips[c, side, 24:32] = zero


def clear_planes(ref, planes=None):
    last = ref.shape[1] - 1
    for c in planes or range(ref.shape[0]):
        for tile in range(2):
            for z in (0, last):
                ref[c, z, tile] = jnp.zeros(ref.shape[3:], F32)


def line(z, place, count, layers):
    if z is None:
        return slice(count * layers + place, count * layers + place + 1)
    return pl.ds(place * layers + z, 1)


def planes(place, layers):
    return slice(place * layers, (place + 1) * layers)


def row_place(ref, c, tile, row):
    high, rows = ref.shape[-4], ref.shape[-2]
    total = 1
    for size in ref.shape[:-1]:
        total *= size
    at = ((c * high + 1) * 2 + tile) * rows + row
    return ref.reshape(total, LANES), pl.ds(at, high - 2, stride=2 * rows)


def row_of(ref, c, tile, row):
    flat, place = row_place(ref, c, tile, row)
    return flat[place, :]


def set_row(ref, c, tile, row, value):
    flat, place = row_place(ref, c, tile, row)
    flat[place, :] = value


def layer_pair(cur):
    row, last = row_iota(cur.shape), cur.shape[0] - 1
    behind = jnp.where(row == 0, 0.0, pltpu.roll(cur, 1, 0))
    front = jnp.where(row == last, 0.0, pltpu.roll(cur, last, 0))
    return behind, front


def edge_column(left, right, layers):
    shape = (layers, LANES)
    lane, layer = lane_iota(shape), row_iota(shape)
    low = jnp.sum(jnp.where(lane == 8 * layer + HALO - 1, left, 0.0), axis=1, keepdims=True)
    high = jnp.sum(jnp.where(lane == 8 * layer + HALO, right, 0.0), axis=1, keepdims=True)
    return jnp.where(lane == LANES - 1, low, jnp.where(lane == 0, high, 0.0))


def back_wind(coef, uy, edge_x, z, tile):
    tiles = [coef[UX, z + 1, t] for t in range(2)]
    return (
        x_pair(tiles, tile, edge_tile(edge_x, z)),
        (uy[z + 1, tile, BEHIND], uy[z + 1, tile, FRONT]),
        (coef[UZ, z, tile], coef[UZ, z + 2, tile]),
    )


def strip_back_wind(coef, uy, side):
    return (
        strip_x(coef[UX, side]),
        (uy[side, BEHIND], uy[side, FRONT]),
        strip_z(coef[UZ, side]),
    )


def pack_kernel(
    axis_cd,
    s0,
    vel,
    grad,
    rot,
    tgt,
    needle,
    out,
    first,
    second,
    field,
    coef,
    base,
    uy,
    stage,
    sems,
):
    layers = stage.shape[1]
    blocks = sems.shape[0]
    deep = layers // blocks
    sources = (s0, vel, grad, rot, tgt)

    def copies(block):
        slot, found = 0, []
        for number, ref in enumerate(sources):
            depth = pl.ds(block * deep, deep)
            target = stage.at[pl.ds(slot, ref.shape[0]), depth]
            found.append(
                pltpu.make_async_copy(ref.at[:, depth], target, sems.at[block, number])
            )
            slot += ref.shape[0]
        return found

    for block in range(blocks):
        for copy in copies(block):
            copy.start()
    lane = lane_iota(out.shape[1:])
    Field(field, None).clear()
    clear_planes(coef, [UZ])

    def load(z, carry):
        zero = jnp.zeros((8, LANES), F32)
        for tile in range(2):
            for c in range(5):
                field[c, z + 1, tile, OWN] = stage[c, z, :, span(tile)]
            u = [DT * stage[VEL + d, z, :, span(tile)] for d in range(3)]
            turn = DT * stage[ROT, z, :, span(tile)]
            parts = gradient_parts(lambda i: stage[GRAD + i, z, :, span(tile)])
            for key, value in parts.items():
                coef[PLACE[key], z + 1, tile] = value
            coef[SPREAD, z + 1, tile] = 2.0 * turn
            coef[UX, z + 1, tile] = u[0]
            coef[UZ, z + 1, tile] = u[2]
            uy[z + 1, tile, 0:8] = zero
            uy[z + 1, tile, 24:32] = zero
            uy[z + 1, tile, OWN] = u[1]
            base[z + 1, tile] = 6.0 * turn + (jnp.abs(u[0]) + jnp.abs(u[1]) + jnp.abs(u[2]))
        return carry


    def step(block, carry):
        for copy in copies(block):
            copy.wait()
        for c in range(NEEDLES):
            total = out[c]
            for k in range(deep):
                z = block * deep + k
                low, high = stage[c, z, :, span(0)], stage[c, z, :, span(1)]
                both = jnp.where(lane < HALO, low, high)
                moved = pltpu.roll(both, (8 * z + HALO) % LANES, 1)
                total = jnp.where(lane // 8 == z, moved, total)
            out[c] = total
        lax.fori_loop(block * deep, (block + 1) * deep, load, 0)
        return carry

    lax.fori_loop(0, blocks, step, 0)

    odd = lax.axis_index(axis_cd) % 2 == 1
    outer = lane % 8 < HALO
    first[PAIRS] = needle[...]
    second[PAIRS] = needle[...]
    for c in range(PAIRS):
        here, other = out[c], out[min(c + PAIRS, NEEDLES - 1)]
        to_right = jnp.where(outer, here, pltpu.roll(other, HALO, 1))
        to_left = jnp.where(outer, pltpu.roll(other, LANES - HALO, 1), here)
        first[c] = jnp.where(odd, to_left, to_right)
        second[c] = jnp.where(odd, to_right, to_left)


def bulk_kernel(field, coef, base, uy, s1):
    layers = field.shape[1] - 2
    state = Field(field, None)

    def advance(z, carry):
        for tile in range(2):
            at = (z + 1, tile)
            m, damp = coefficients(coef, base, *at)
            wind = (coef[(UX,) + at], uy[at + (OWN,)], coef[(UZ,) + at])
            a = [state.own(c, z, tile) for c in range(5)]
            out = forward(a, m, damp, coef[(SPREAD,) + at], wind, state.around(z, tile))
            for c in range(5):
                s1[c, z + 1, tile, OWN] = out[c]
        return carry

    lax.fori_loop(0, layers, advance, 0)


def split_three(value):
    parts = []
    for _ in range(3):
        part = value.astype(jnp.bfloat16).astype(F32)
        parts.append(part)
        value = value - part
    return parts


def feet_block(ref, block, count):
    place = jnp.clip(block, 0, count - 1) * LANES
    row = ref[:, pl.ds(pl.multiple_of(place, LANES), LANES)]
    return jnp.where((block >= 0) & (block < count), row, 0)


def first_kernel(
    axis_md,
    axis_cd,
    own,
    needle,
    near_first,
    near_second,
    far_first,
    far_second,
    start,
    end,
    column,
    field,
    coef,
    uy,
    base_in,
    s1_in,
    s1,
    base,
    strip_s0,
    strip_coef,
    strip_base,
    strip_uy,
    strip_s1,
    strip_tgt,
    up,
    down,
    spread,
    cover,
    source,
    joint,
):
    layers = field.shape[1] - 2
    height = own.shape[1]
    md = lax.axis_index(axis_md)
    count = lax.axis_size(axis_md)
    lane = lane_iota((height, LANES))
    outer = lane % 8 < HALO
    odd = lax.axis_index(axis_cd) % 2 == 1

    def from_left(c):
        return jnp.where(odd, near_second[c], near_first[c])

    def from_right(c):
        return jnp.where(odd, near_first[c], near_second[c])

    def half(take, c, turn):
        return take(c) if c < PAIRS else pltpu.roll(take(c - PAIRS), turn, 1)

    near = lane_iota((1, LANES)) < LANES // 2

    def feet(ref):
        far = jnp.where(near, feet_block(ref, md + 2, count), feet_block(ref, md - 2, count))
        blocks = [feet_block(ref, md + d, count) for d in (-1, 0, 1)]
        return jnp.concatenate(blocks + [far], axis=1)

    starts, ends, columns = feet(start), feet(end), feet(column)
    far = jnp.where((lane < LANES // 2) == odd, far_first[...], far_second[...])
    rates = jnp.concatenate(
        [from_left(PAIRS), needle[...], from_right(PAIRS), far], axis=1
    )
    needles = rates.shape[1]
    picked = jnp.where(row_iota((height, needles)) == columns, 1.0, 0.0)
    for part, value in enumerate(split_three(rates)):
        for z in range(layers):
            spread[part, z * height : (z + 1) * height] = (picked * value[z : z + 1]).astype(
                jnp.bfloat16
            )
    length = 2 * LANES
    cells = row_iota((length + LANES, needles))
    beyond = cells - length
    strip = jnp.where(beyond < 8, beyond - HALO, beyond - 8 + length - HALO)
    cells = jnp.where(cells < length, cells, strip) + md * length
    cover[...] = jnp.where((cells >= starts) & (cells < ends), 1.0, 0.0).astype(jnp.bfloat16)
    product = jnp.zeros((layers * height, length + LANES), F32)
    for part in range(3):
        product = product + lax.dot_general(
            spread[part], cover[...], (((1,), (1,)), ((), ())), preferred_element_type=F32
        )
    source[...] = (DT * product).reshape(source.shape)

    state = Field(field, strip_s0, joint)
    state.clear_strips()
    has_left, has_right = md > 0, md < count - 1
    for side in range(2):

        def raw(c):
            if side == 0:
                return jnp.where(outer, jnp.where(has_left, half(from_left, c, LANES - HALO), 0.0), own[c])
            return jnp.where(outer, own[c], jnp.where(has_right, half(from_right, c, HALO), 0.0))

        for c in range(5):
            strip_s0[c, side, OWN] = raw(S0 + c)
            strip_tgt[c, side] = raw(TGT + c)
        u = [DT * raw(VEL + d) for d in range(3)]
        turn = DT * raw(ROT)
        for key, value in gradient_parts(lambda i: raw(GRAD + i)).items():
            strip_coef[PLACE[key], side] = value
        strip_coef[SPREAD, side] = 2.0 * turn
        strip_coef[UX, side] = u[0]
        strip_coef[UZ, side] = u[2]
        strip_uy[side, 0:8] = jnp.zeros((8, LANES), F32)
        strip_uy[side, 24:32] = jnp.zeros((8, LANES), F32)
        strip_uy[side, OWN] = u[1]
        damp = 6.0 * turn + (jnp.abs(u[0]) + jnp.abs(u[1]) + jnp.abs(u[2]))
        taken = jnp.zeros((height, LANES), F32)
        for z in range(layers):
            moved = pltpu.roll(source[z, :, span(2)], (8 * z - 8 * side) % LANES, 1)
            taken = jnp.where(lane // 8 == z, moved, taken)
        strip_base[side] = damp + taken

    for side in range(2):
        m, damp = coefficients(strip_coef, strip_base, side)
        wind = (strip_coef[UX, side], strip_uy[side, OWN], strip_coef[UZ, side])
        a = [strip_s0[c, side, OWN] for c in range(5)]
        spin = strip_coef[SPREAD, side]
        out = forward(a, m, damp, spin, wind, state.strip_around(side))
        for c in range(5):
            strip_s1[c, side, OWN] = out[c]
    state.join()

    def put(side):
        def at(place):
            return line(None, side * 11 + place, 22, layers)

        for c in range(5):
            first, new = strip_s0.at[c, side], strip_s1.at[c, side]
            up[at(c)], down[at(c)] = first[23:24], first[8:9]
            up[at(5 + c)], down[at(5 + c)] = new[23:24], new[8:9]
        wind = strip_uy.at[side]
        up[at(10)] = -jnp.minimum(wind[23:24], 0.0)
        down[at(10)] = jnp.maximum(wind[8:9], 0.0)

    def mend(z, carry):
        for tile in range(2):
            gain = source[z, :, span(tile)]
            base[z + 1, tile] = base_in[z + 1, tile] + gain
            u = coef[UX, z + 1, tile]
            if tile == 0:
                weight, turn = jnp.where(lane == 0, jnp.maximum(u, 0.0), 0.0), 1
            else:
                weight, turn = jnp.where(lane == LANES - 1, -jnp.minimum(u, 0.0), 0.0), -1
            for c in range(5):
                edge = pltpu.roll(joint[c], (2 * LANES - HALO + turn - 8 * z) % LANES, 1)
                s1[c, z + 1, tile, OWN] = (
                    s1_in[c, z + 1, tile, OWN]
                    - gain * field[c, z + 1, tile, OWN]
                    + weight * edge
                )
        return carry

    clear_planes(s1)
    lax.fori_loop(0, layers, mend, 0)
    for tile in range(2):
        for message, row in ((up, 23), (down, 8)):
            for c in range(5):
                message[planes(tile * 11 + c, layers)] = row_of(field, c, tile, row)
                message[planes(tile * 11 + 5 + c, layers)] = row_of(s1, c, tile, row)
        out, into = row_of(uy, 0, tile, 23), row_of(uy, 0, tile, 8)
        up[planes(tile * 11 + 10, layers)] = -jnp.minimum(out, 0.0)
        down[planes(tile * 11 + 10, layers)] = jnp.maximum(into, 0.0)
    for side in range(2):
        put(side)


def cd_flags(axis_cd):
    cd = lax.axis_index(axis_cd)
    return cd > 0, cd < lax.axis_size(axis_cd) - 1


def advance_kernel(s1, strip_s1, coef, base, uy, tgt, s2, goal, joint):
    layers = tgt.shape[1]
    state = Field(s1, strip_s1, joint)
    state.join()

    def advance(z, carry):
        for tile in range(2):
            at = (z + 1, tile)
            m, damp = coefficients(coef, base, *at)
            wind = (coef[(UX,) + at], uy[at + (OWN,)], coef[(UZ,) + at])
            a = [state.own(c, z, tile) for c in range(5)]
            out = forward(a, m, damp, coef[(SPREAD,) + at], wind, state.around(z, tile))
            for c in range(5):
                s2[(c,) + at] = out[c]
                goal[(c,) + at] = tgt[c, z, :, span(tile)]
        return carry

    lax.fori_loop(0, layers, advance, 0)


def edge_kernel(
    axis_cd,
    s1,
    strip_s1_in,
    coef,
    base,
    uy,
    goal,
    strip_coef,
    strip_base,
    strip_uy,
    strip_tgt,
    own_up,
    own_down,
    from_below,
    from_above,
    s1_edge,
    s2_edge,
    strip_adj2,
    strip_adj1,
    up,
    down,
    strip_s1,
):
    layers = goal.shape[1] - 2
    has_below, has_above = cd_flags(axis_cd)

    state, delta = Field(s1, strip_s1), Field(s1, strip_adj2)
    delta.clear_strips()
    for side in range(2):

        def at(place):
            return line(None, side * 11 + place, 22, layers)

        wind = strip_uy.at[side]
        low_u, high_u = jnp.maximum(wind[8:9], 0.0), -jnp.minimum(wind[23:24], 0.0)
        low_n, high_n = from_below[at(10)], from_above[at(10)]
        for c in range(5):
            old, new = at(c), at(5 + c)
            ref = strip_s1.at[c, side]
            ref[OWN] = strip_s1_in[c, side, OWN]
            low = from_below[new] + low_n * own_down[old]
            high = from_above[new] + high_n * own_up[old]
            ref[7:8] = jnp.where(has_below, low, 0.0)
            ref[24:25] = jnp.where(has_above, high, 0.0)
            ref[8:9] = ref[8:9] + jnp.where(has_below, low_u * from_below[old], 0.0)
            ref[23:24] = ref[23:24] + jnp.where(has_above, high_u * from_above[old], 0.0)
    for side in range(2):
        m, damp = coefficients(strip_coef, strip_base, side)
        wind = (strip_coef[UX, side], strip_uy[side, OWN], strip_coef[UZ, side])
        a = [strip_s1[c, side, OWN] for c in range(5)]
        spin = strip_coef[SPREAD, side]
        out = forward(a, m, damp, spin, wind, state.strip_around(side))
        for c in range(5):
            strip_adj2[c, side, OWN] = out[c] - strip_tgt[c, side]
    for side in range(2):

        def at(place):
            return line(None, side * 10 + place, 20, layers)

        m, damp = coefficients(strip_coef, strip_base, side)
        a = [strip_s1[c, side, OWN] for c in range(5)]
        b = [strip_adj2[c, side, OWN] for c in range(5)]
        wind = strip_back_wind(strip_coef, strip_uy, side)
        out = backward(b, a, m, damp, wind, delta.strip_around(side))
        high = -jnp.minimum(strip_uy[side, 23:24], 0.0)
        low = jnp.maximum(strip_uy[side, 8:9], 0.0)
        for c in range(5):
            strip_adj1[c, side, OWN] = out[c]
            up[at(c)] = high * b[c][-1:]
            down[at(c)] = low * b[c][:1]
            up[at(5 + c)] = high * out[c][-1:]
            down[at(5 + c)] = low * out[c][:1]

    def constants(tile, row):
        m = {key: row_of(coef, place, tile, row) for key, place in PLACE.items()}
        return m, row_of(base, 0, tile, row)

    for number, (message, mine, valid, outgoing) in enumerate(
        ((from_below, own_down, has_below, down), (from_above, own_up, has_above, up))
    ):
        rows = (0, 1, 2) if number == 0 else (15, 14, 13)
        sides = (0, 1)

        def plane(ref, place, tile):
            return ref[planes(tile * 11 + place, layers)]

        lines = [{}, {}, {}, {}]
        for c in range(5):
            for tile in range(2):
                old, new = plane(message, c, tile), plane(message, 5 + c, tile)
                weight = plane(message, 10, tile)
                lines[0][c, tile] = jnp.where(
                    valid, new + weight * plane(mine, c, tile), 0.0
                )
                lines[1][c, tile] = plane(mine, 5 + c, tile) + jnp.where(
                    valid, plane(mine, 10, tile) * old, 0.0
                )
                s1_edge[c, number, tile] = lines[1][c, tile]
                for k in (1, 2):
                    lines[k + 1][c, tile] = row_of(s1, c, tile, 8 + rows[k])

        def strip_edge(ref, c, row):
            left, right = (ref[c, side, 8 + row : 9 + row] for side in sides)
            return edge_column(left, right, layers)

        def ordered(outer, inner):
            return (outer, inner) if number == 0 else (inner, outer)

        misses = [{}, {}]
        for k in range(2):
            row = rows[k]
            edges = [strip_edge(strip_s1, c, row) for c in range(5)]
            for tile in range(2):
                m, damp = constants(tile, row)
                wind = (
                    row_of(coef, UX, tile, row),
                    row_of(uy, 0, tile, 8 + row),
                    row_of(coef, UZ, tile, row),
                )
                a = [lines[k + 1][c, tile] for c in range(5)]

                def around(c):
                    tiles = [lines[k + 1][c, t] for t in range(2)]
                    return (
                        x_pair(tiles, tile, edges[c]),
                        ordered(lines[k][c, tile], lines[k + 2][c, tile]),
                        layer_pair(a[c]),
                    )

                out = forward(a, m, damp, row_of(coef, SPREAD, tile, row), wind, around)
                for c in range(5):
                    s2_edge[c, 2 * number + k, tile] = out[c]
                    misses[k][c, tile] = out[c] - row_of(goal, c, tile, row)

        row = rows[0]
        edges = [strip_edge(strip_adj2, c, row) for c in range(5)]
        left, right = (strip_coef[UX, side, row : row + 1] for side in sides)
        edge_x = edge_column(left, right, layers)
        for tile in range(2):
            m, damp = constants(tile, row)
            a = [lines[1][c, tile] for c in range(5)]
            b = [misses[0][c, tile] for c in range(5)]
            zero = jnp.zeros_like(b[0])
            wind = (
                x_pair([row_of(coef, UX, t, row) for t in range(2)], tile, edge_x),
                ordered(zero, row_of(uy, 0, tile, 8 + rows[1])),
                layer_pair(row_of(coef, UZ, tile, row)),
            )

            def around(c):
                tiles = [misses[0][c, t] for t in range(2)]
                return (
                    x_pair(tiles, tile, edges[c]),
                    ordered(zero, misses[1][c, tile]),
                    layer_pair(b[c]),
                )

            out = backward(b, a, m, damp, wind, around)
            weight = plane(mine, 10, tile)
            for c in range(5):
                outgoing[planes(tile * 10 + c, layers)] = weight * b[c]
                outgoing[planes(tile * 10 + 5 + c, layers)] = weight * out[c]


def second_kernel(
    s1_in,
    s2_in,
    goal,
    s1_edge,
    s2_edge,
    coef,
    base,
    uy,
    strip_coef,
    strip_adj2,
    s2_out,
    adj1,
    dots,
    s1,
    s2,
    adj2,
    joint,
):
    layers = goal.shape[1] - 2

    def gather(z, carry):
        for tile in range(2):
            for c in range(5):
                s1[c, z + 1, tile] = s1_in[c, z + 1, tile, OWN]
                s2[c, z + 1, tile] = s2_in[c, z + 1, tile]
        return carry

    lax.fori_loop(0, layers, gather, 0)
    for c in range(5):
        for tile in range(2):
            for number, row in enumerate((0, 15)):
                set_row(s1, c, tile, row, s1_edge[c, number, tile])
            for number, row in enumerate((0, 1, 15, 14)):
                set_row(s2, c, tile, row, s2_edge[c, number, tile])

    delta = Field(adj2, strip_adj2, joint)
    delta.clear()
    delta.join()

    def compare(z, carry):
        for tile in range(2):
            total = 0.0
            for c in range(5):
                value = s2[c, z + 1, tile]
                miss = value - goal[c, z + 1, tile]
                s2_out[c, z, :, span(tile)] = value
                adj2[c, z + 1, tile, OWN] = miss
                total = total + miss * s1[c, z + 1, tile]
            dots[z, :, span(tile)] = total
        return carry

    lax.fori_loop(0, layers, compare, 0)
    edge_x = merged(strip_coef, UX, slice(None))

    def retreat(z, carry):
        for tile in range(2):
            m, damp = coefficients(coef, base, z + 1, tile)
            a = [s1[c, z + 1, tile] for c in range(5)]
            b = [delta.own(c, z, tile) for c in range(5)]
            wind = back_wind(coef, uy, edge_x, z, tile)
            out = backward(b, a, m, damp, wind, delta.around(z, tile))
            for c in range(5):
                adj1[c, z + 1, tile, OWN] = out[c]
        return carry

    lax.fori_loop(0, layers, retreat, 0)


def third_kernel(
    axis_md,
    axis_cd,
    adj1_in,
    strip_adj1_in,
    dots,
    field,
    from_below,
    from_above,
    start,
    end,
    column,
    adj1,
    strip_adj1,
    first,
    kept,
    second,
    sens,
):
    layers, height, length = dots.shape
    md = lax.axis_index(axis_md)
    count = lax.axis_size(axis_md)
    has_below, has_above = cd_flags(axis_cd)
    odd = lax.axis_index(axis_cd) % 2 == 1

    row = row_iota((height, LANES))
    top = height - 1

    def mended(value, z, place):
        at = line(z, place, 20, layers)
        low = jnp.where(has_below, from_below[at], 0.0)
        high = jnp.where(has_above, from_above[at], 0.0)
        return value + jnp.where(row == 0, low, jnp.where(row == top, high, 0.0))

    for side in range(2):
        for c in range(5):
            value = strip_adj1_in[c, side, OWN]
            strip_adj1[c, side, OWN] = mended(value, None, side * 10 + c)
    Field(adj1, strip_adj1).clear()

    def weigh(z, carry):
        for tile in range(2):
            total = dots[z, :, span(tile)]
            for c in range(5):
                value = mended(adj1_in[c, z + 1, tile, OWN], z, tile * 10 + c)
                adj1[c, z + 1, tile, OWN] = value
                total = total + value * field[c, z + 1, tile, OWN]
            sens[z, :, span(tile)] = -DT * total
        return carry

    lax.fori_loop(0, layers, weigh, 0)

    def feet(ref):
        return jnp.concatenate([feet_block(ref, md + d, count) for d in (-1, 0, 1)], axis=1)

    starts, ends, columns = feet(start), feet(end), feet(column)
    needles = starts.shape[1]
    cells = row_iota((length, needles)) + md * length
    cover = jnp.where((cells >= starts) & (cells < ends), 1.0, 0.0).astype(jnp.bfloat16)
    product = jnp.zeros((layers * height, needles), F32)
    for part in split_three(sens[...].reshape(layers * height, length)):
        product = product + jnp.dot(
            part.astype(jnp.bfloat16), cover, preferred_element_type=F32
        )
    picked = jnp.where(row_iota((height, needles)) == columns, 1.0, 0.0)
    for z in range(layers):
        total = jnp.sum(
            product[z * height : (z + 1) * height] * picked, axis=0, keepdims=True
        )
        first[z : z + 1] = jnp.where(odd, total[:, span(0)], total[:, span(2)])
        kept[z : z + 1] = total[:, span(1)]
        second[z : z + 1] = jnp.where(odd, total[:, span(2)], total[:, span(0)])


def fourth_kernel(
    axis_cd,
    adj1,
    strip_adj1,
    field,
    coef,
    base,
    uy,
    strip_coef,
    weights_below,
    weights_above,
    own_up,
    own_down,
    from_below,
    from_above,
    adj0,
    joint,
):
    layers, height = adj0.shape[1], adj0.shape[2]
    top = height - 1
    has_below, has_above = cd_flags(axis_cd)
    delta = Field(adj1, strip_adj1, joint)
    delta.join()
    edge_x = merged(strip_coef, UX, slice(None))

    def retreat(z, carry):
        for tile in range(2):
            at = (z + 1, tile)
            m, damp = coefficients(coef, base, *at)
            a = [field[c, z + 1, tile, OWN] for c in range(5)]
            b = [delta.own(c, z, tile) for c in range(5)]
            wind = back_wind(coef, uy, edge_x, z, tile)
            out = backward(b, a, m, damp, wind, delta.around(z, tile))
            weight = line(z, tile * 11 + 10, 22, layers)
            low_n, high_n = weights_below[weight], weights_above[weight]
            lanes = span(tile)
            for c in range(5):
                old = line(z, tile * 10 + c, 20, layers)
                new = line(z, tile * 10 + 5 + c, 20, layers)
                low = from_below[new] + low_n * own_down[old]
                high = from_above[new] + high_n * own_up[old]
                low, high = jnp.where(has_below, low, 0.0), jnp.where(has_above, high, 0.0)
                adj0[c, z, :, lanes] = out[c]
                adj0[c, z, 0:1, lanes] = out[c][:1] + low
                adj0[c, z, top:, lanes] = out[c][top:] + high
        return carry

    lax.fori_loop(0, layers, retreat, 0)


def ring(value, axis, steps):
    count = lax.axis_size(axis)
    return lax.ppermute(value, axis, [(i, (i + steps) % count) for i in range(count)])


def winding(value, steps, turn):
    rows, columns = lax.axis_size("md"), lax.axis_size("cd")
    pairs = []
    for column in range(columns):
        for row in range(rows):
            target = row + (steps if column % 2 == turn else -steps)
            if 0 <= target < rows:
                pairs.append((row * columns + column, target * columns + column))
            else:
                pairs.append((row * columns + column, row * columns + (column ^ 1)))
    return lax.ppermute(value, ("md", "cd"), pairs)


def both_ways(value, steps):
    return winding(value, steps, 0), winding(value, steps, 1)


def shape_of(*dims, dtype=F32):
    return jax.ShapeDtypeStruct(dims, dtype)


def scratch(*dims, dtype=F32):
    return pltpu.VMEM(dims, dtype)


def cost(microseconds):
    return pl.CostEstimate(
        flops=int(microseconds * 1e6), bytes_accessed=int(microseconds * 3e6), transcendentals=0
    )


def params(mebibytes):
    return pltpu.CompilerParams(vmem_limit_bytes=mebibytes * 1024 * 1024)


def local(orientation, velocity, velocity_grad, rotary, target, needle_params, *feet):
    _, layers, height, length = orientation.shape
    rotary = rotary[None]
    rates = jnp.transpose(needle_params[:, 0, :])
    feet = [foot.reshape(1, -1) for foot in feet]
    padded = (layers + 2, 2, ROWS, LANES)
    plain = (layers + 2, 2, height, LANES)
    strip_padded, strip = (2, ROWS, LANES), (2, height, LANES)
    message, back_message = shape_of(22 * layers + 24, LANES), shape_of(20 * layers + 24, LANES)
    joint = scratch(5, height, LANES)

    hbm = pl.BlockSpec(memory_space=pltpu.HBM)
    blocks = 4
    packed, first, second, field, coef, base, uy = pl.pallas_call(
        functools.partial(pack_kernel, "cd"),
        in_specs=[hbm] * 5 + [pl.BlockSpec(memory_space=pltpu.VMEM)],
        out_shape=[
            shape_of(NEEDLES, height, LANES),
            shape_of(PAIRS + 1, height, LANES),
            shape_of(PAIRS + 1, height, LANES),
            shape_of(5, *padded),
            shape_of(COEFS, *plain),
            shape_of(*plain),
            shape_of(*padded),
        ],
        scratch_shapes=[
            scratch(NEEDLES, layers, height, length),
            pltpu.SemaphoreType.DMA((blocks, 5)),
        ],
        compiler_params=params(20),
        cost_estimate=cost(4),
    )(
        *(
            pltpu.with_memory_space_constraint(field, pltpu.HBM)
            for field in (orientation, velocity, velocity_grad, rotary, target)
        ),
        rates,
    )
    far = both_ways(rates, 2)
    near = winding(first, 1, 0), winding(second, 1, 1)

    s1 = pl.pallas_call(
        bulk_kernel,
        out_shape=shape_of(5, *padded),
        compiler_params=params(16),
        cost_estimate=cost(2),
    )(field, coef, base, uy)

    s1, base, strip_s0, strip_coef, strip_base, strip_uy, strip_s1, strip_tgt, up, down = (
        pl.pallas_call(
            functools.partial(first_kernel, "md", "cd"),
            out_shape=[
                shape_of(5, *padded),
                shape_of(*plain),
                shape_of(5, *strip_padded),
                shape_of(COEFS, *strip),
                shape_of(*strip),
                shape_of(*strip_padded),
                shape_of(5, *strip_padded),
                shape_of(5, *strip),
                message,
                message,
            ],
            scratch_shapes=[
                scratch(3, layers * height, 4 * LANES, dtype=jnp.bfloat16),
                scratch(length + LANES, 4 * LANES, dtype=jnp.bfloat16),
                scratch(layers, height, length + LANES),
                joint,
            ],
            compiler_params=params(24),
        cost_estimate=cost(4),
        )(
            packed,
            rates,
            *near,
            *far,
            *feet,
            field,
            coef,
            uy,
            base,
            s1,
        )
    )
    below = ring(up, "cd", 1)
    above = ring(down, "cd", -1)

    s2_part, goal = pl.pallas_call(
        advance_kernel,
        out_shape=[shape_of(5, *plain), shape_of(5, *plain)],
        scratch_shapes=[joint],
        compiler_params=params(16),
        cost_estimate=cost(4),
    )(s1, strip_s1, coef, base, uy, target)
    s1_edge, s2_edge, strip_adj2, strip_adj1, back_up, back_down = pl.pallas_call(
        functools.partial(edge_kernel, "cd"),
        out_shape=[
            shape_of(5, 2, 2, layers, LANES),
            shape_of(5, 4, 2, layers, LANES),
            shape_of(5, *strip_padded),
            shape_of(5, *strip_padded),
            back_message,
            back_message,
        ],
        scratch_shapes=[scratch(5, *strip_padded)],
        compiler_params=params(16),
        cost_estimate=cost(2),
    )(
        s1,
        strip_s1,
        coef,
        base,
        uy,
        goal,
        strip_coef,
        strip_base,
        strip_uy,
        strip_tgt,
        up,
        down,
        below,
        above,
    )
    back_below = ring(back_up, "cd", 1)
    back_above = ring(back_down, "cd", -1)

    s2, adj1, dots = pl.pallas_call(
        second_kernel,
        out_shape=[
            shape_of(*orientation.shape),
            shape_of(5, *padded),
            shape_of(layers, height, length),
        ],
        scratch_shapes=[
            scratch(5, *plain),
            scratch(5, *plain),
            scratch(5, *padded),
            joint,
        ],
        compiler_params=params(24),
        cost_estimate=cost(6),
    )(
        s1,
        s2_part,
        goal,
        s1_edge,
        s2_edge,
        coef,
        base,
        uy,
        strip_coef,
        strip_adj2,
    )

    part = shape_of(*rates.shape)
    adj1, strip_adj1, part_first, part_own, part_second = pl.pallas_call(
        functools.partial(third_kernel, "md", "cd"),
        out_shape=[shape_of(5, *padded), shape_of(5, *strip_padded), part, part, part],
        scratch_shapes=[scratch(layers, height, length)],
        compiler_params=params(24),
        cost_estimate=cost(1),
    )(adj1, strip_adj1, dots, field, back_below, back_above, *feet)
    part_first = winding(part_first, 1, 0)
    part_second = winding(part_second, 1, 1)

    adj0 = pl.pallas_call(
        functools.partial(fourth_kernel, "cd"),
        out_shape=shape_of(*orientation.shape),
        scratch_shapes=[joint],
        compiler_params=params(24),
        cost_estimate=cost(4),
    )(
        adj1,
        strip_adj1,
        field,
        coef,
        base,
        uy,
        strip_coef,
        below,
        above,
        back_up,
        back_down,
        back_below,
        back_above,
    )
    gradient = part_own + part_first + part_second
    return s2, adj0, jnp.transpose(gradient)[:, None, :]


def solution(mesh):
    field = P(None, None, "cd", "md")
    feet = P(None, "cd")
    needles = P("md", "cd", None)
    return jax.shard_map(
        local,
        mesh=mesh,
        in_specs=(field, field, field, P(None, "cd", "md"), field, needles, feet, feet, feet),
        out_specs=(field, field, needles),
        check_vma=False,
    )
```

```python
import functools

import jax
import jax.numpy as jnp
from jax import lax
from jax.experimental import pallas as pl
from jax.experimental.pallas import tpu as pltpu
from jax.sharding import PartitionSpec as P

XI = 0.95
DT = 0.1
LANES = 128
F32 = jnp.float32
HALO = 4
S0, VEL, GRAD, ROT, TGT, NEEDLES = 0, 5, 8, 17, 18, 23
PAIRS = 12
PLACE = {(0, 0): 0, (1, 1): 1, (0, 1): 2, (1, 0): 3, (0, 2): 4, (2, 0): 5, (1, 2): 6, (2, 1): 7}
SPREAD, UX, UZ, COEFS = 8, 9, 10, 11
ROWS = 32
OWN, BEHIND, FRONT = slice(8, 24), slice(7, 23), slice(9, 25)


def lane_iota(shape):
    return lax.broadcasted_iota(jnp.int32, shape, len(shape) - 1)


def row_iota(shape):
    return lax.broadcasted_iota(jnp.int32, shape, len(shape) - 2)


def span(tile):
    return slice(tile * LANES, (tile + 1) * LANES)


def gradient_parts(read):
    g = [read(i) for i in range(9)]
    low = 0.5 * (XI - 1.0) * DT
    m = {}
    for i, j in ((0, 1), (0, 2), (1, 2)):
        a, b = g[3 * i + j], g[3 * j + i]
        both = low * (a + b)
        m[i, j] = DT * a + both
        m[j, i] = DT * b + both
    m[0, 0] = (XI * DT) * (g[0] - g[8])
    m[1, 1] = (XI * DT) * (g[4] - g[8])
    return m


def forward(a, m, base, spread, wind, around):
    a11, a22, a12, a13, a23 = a
    a33 = 1.0 - a11 - a22
    n00 = m[0, 0] * a11 + m[0, 1] * a12 + m[0, 2] * a13
    n01 = m[0, 0] * a12 + m[0, 1] * a22 + m[0, 2] * a23
    n02 = m[0, 0] * a13 + m[0, 1] * a23 + m[0, 2] * a33
    n10 = m[1, 0] * a11 + m[1, 1] * a12 + m[1, 2] * a13
    n11 = m[1, 0] * a12 + m[1, 1] * a22 + m[1, 2] * a23
    n12 = m[1, 0] * a13 + m[1, 1] * a23 + m[1, 2] * a33
    n20 = m[2, 0] * a11 + m[2, 1] * a12
    n21 = m[2, 0] * a12 + m[2, 1] * a22
    n22 = m[2, 0] * a13 + m[2, 1] * a23
    keep = 1.0 - (base + 2.0 * (n00 + n11 + n22))
    gain = (2.0 * n00 + spread, 2.0 * n11 + spread, n01 + n10, n02 + n20, n12 + n21)
    out = []
    for c in range(5):
        total = gain[c] + keep * a[c]
        for u, (behind, front) in zip(wind, around(c)):
            total = total + jnp.abs(u) * jnp.where(u > 0.0, behind, front)
        out.append(total)
    return out


def backward(b, a, m, base, wind, around):
    b1, b2, b3, b4, b5 = b
    a11, a22, a12, a13, a23 = a
    g = -2.0 * (b1 * a11 + b2 * a22 + b3 * a12 + b4 * a13 + b5 * a23)
    trace = (
        m[0, 0] * a11
        + m[1, 1] * a22
        + (m[0, 1] + m[1, 0]) * a12
        + (m[0, 2] + m[2, 0]) * a13
        + (m[1, 2] + m[2, 1]) * a23
    )
    s00, s11, s22 = 2.0 * b1 + g, 2.0 * b2 + g, g
    h00 = m[0, 0] * s00 + m[1, 0] * b3 + m[2, 0] * b4
    h01 = m[0, 0] * b3 + m[1, 0] * s11 + m[2, 0] * b5
    h02 = m[0, 0] * b4 + m[1, 0] * b5 + m[2, 0] * s22
    h10 = m[0, 1] * s00 + m[1, 1] * b3 + m[2, 1] * b4
    h11 = m[0, 1] * b3 + m[1, 1] * s11 + m[2, 1] * b5
    h12 = m[0, 1] * b4 + m[1, 1] * b5 + m[2, 1] * s22
    h20 = m[0, 2] * s00 + m[1, 2] * b3
    h21 = m[0, 2] * b3 + m[1, 2] * s11
    h22 = m[0, 2] * b4 + m[1, 2] * b5
    keep = 1.0 - (base + 2.0 * trace)
    gain = (h00 - h22, h11 - h22, h01 + h10, h02 + h20, h12 + h21)
    weights = [(jnp.minimum(w, 0.0), jnp.maximum(f, 0.0)) for w, f in wind]
    out = []
    for c in range(5):
        total = gain[c] + keep * b[c]
        for (low, high), (behind, front) in zip(weights, around(c)):
            total = total + (high * front - low * behind)
        out.append(total)
    return out


def merged(strips, c, rows):
    left, right = strips[c, 0, rows], strips[c, 1, rows]
    return jnp.where(lane_iota(left.shape) % 8 < HALO, left, right)


def edge_tile(joint, z):
    return pltpu.roll(joint, (2 * LANES - HALO - 8 * z) % LANES, 1)


def x_pair(tiles, tile, edge):
    cur = tiles[tile]
    prev, after = (edge, tiles[1]) if tile == 0 else (tiles[0], edge)
    lane = lane_iota(cur.shape)
    behind = pltpu.roll(jnp.where(lane == LANES - 1, prev, cur), 1, 1)
    front = pltpu.roll(jnp.where(lane == 0, after, cur), LANES - 1, 1)
    return behind, front


def strip_x(cur):
    return pltpu.roll(cur, 1, 1), pltpu.roll(cur, LANES - 1, 1)


def strip_z(cur):
    lane = lane_iota(cur.shape)
    behind = jnp.where(lane < 8, 0.0, pltpu.roll(cur, 8, 1))
    front = jnp.where(lane >= LANES - 8, 0.0, pltpu.roll(cur, LANES - 8, 1))
    return behind, front


def coefficients(coef, base, *at):
    m = {key: coef[(place,) + at] for key, place in PLACE.items()}
    return m, base[at]


class Field:
    def __init__(self, ref, strips, joint=None):
        self.ref, self.strips, self.joint = ref, strips, joint

    def join(self):
        for c in range(self.ref.shape[0]):
            self.joint[c] = merged(self.strips, c, OWN)

    def own(self, c, z, tile):
        return self.ref[c, z + 1, tile, OWN]

    def around(self, z, tile):
        def pairs(c):
            ref = self.ref
            tiles = [ref[c, z + 1, t, OWN] for t in range(2)]
            if self.joint is None:
                edge = jnp.zeros_like(tiles[0])
            else:
                edge = edge_tile(self.joint[c], z)
            return (
                x_pair(tiles, tile, edge),
                (ref[c, z + 1, tile, BEHIND], ref[c, z + 1, tile, FRONT]),
                (ref[c, z, tile, OWN], ref[c, z + 2, tile, OWN]),
            )

        return pairs

    def strip_around(self, side):
        def pairs(c):
            cur = self.strips[c, side, OWN]
            return (
                strip_x(cur),
                (self.strips[c, side, BEHIND], self.strips[c, side, FRONT]),
                strip_z(cur),
            )

        return pairs

    def clear(self):
        last = self.ref.shape[1] - 1
        zero = jnp.zeros((8, LANES), F32)
        clear_planes(self.ref)

        def layer(z, carry):
            for c in range(self.ref.shape[0]):
                for tile in range(2):
                    self.ref[c, z, tile, 0:8] = zero
                    self.ref[c, z, tile, 24:32] = zero
            return carry

        lax.fori_loop(1, last, layer, 0)

    def clear_strips(self):
        zero = jnp.zeros((8, LANES), F32)
        for c in range(self.strips.shape[0]):
            for side in range(2):
                self.strips[c, side, 0:8] = zero
                self.strips[c, side, 24:32] = zero


def clear_planes(ref, planes=None):
    last = ref.shape[1] - 1
    for c in planes or range(ref.shape[0]):
        for tile in range(2):
            for z in (0, last):
                ref[c, z, tile] = jnp.zeros(ref.shape[3:], F32)


def line(z, place, count, layers):
    if z is None:
        return slice(count * layers + place, count * layers + place + 1)
    return pl.ds(place * layers + z, 1)


def planes(place, layers):
    return slice(place * layers, (place + 1) * layers)


def row_place(ref, c, tile, row):
    high, rows = ref.shape[-4], ref.shape[-2]
    total = 1
    for size in ref.shape[:-1]:
        total *= size
    at = ((c * high + 1) * 2 + tile) * rows + row
    return ref.reshape(total, LANES), pl.ds(at, high - 2, stride=2 * rows)


def row_of(ref, c, tile, row):
    flat, place = row_place(ref, c, tile, row)
    return flat[place, :]


def set_row(ref, c, tile, row, value):
    flat, place = row_place(ref, c, tile, row)
    flat[place, :] = value


def layer_pair(cur):
    row, last = row_iota(cur.shape), cur.shape[0] - 1
    behind = jnp.where(row == 0, 0.0, pltpu.roll(cur, 1, 0))
    front = jnp.where(row == last, 0.0, pltpu.roll(cur, last, 0))
    return behind, front


def edge_column(left, right, layers):
    shape = (layers, LANES)
    lane, layer = lane_iota(shape), row_iota(shape)
    low = jnp.sum(jnp.where(lane == 8 * layer + HALO - 1, left, 0.0), axis=1, keepdims=True)
    high = jnp.sum(jnp.where(lane == 8 * layer + HALO, right, 0.0), axis=1, keepdims=True)
    return jnp.where(lane == LANES - 1, low, jnp.where(lane == 0, high, 0.0))


def back_wind(coef, uy, edge_x, z, tile):
    tiles = [coef[UX, z + 1, t] for t in range(2)]
    return (
        x_pair(tiles, tile, edge_tile(edge_x, z)),
        (uy[z + 1, tile, BEHIND], uy[z + 1, tile, FRONT]),
        (coef[UZ, z, tile], coef[UZ, z + 2, tile]),
    )


def strip_back_wind(coef, uy, side):
    return (
        strip_x(coef[UX, side]),
        (uy[side, BEHIND], uy[side, FRONT]),
        strip_z(coef[UZ, side]),
    )


def pack_kernel(
    axis_cd,
    s0,
    vel,
    grad,
    rot,
    tgt,
    needle,
    out,
    first,
    second,
    field,
    coef,
    base,
    uy,
    stage,
    sems,
):
    layers = stage.shape[1]
    blocks = sems.shape[0]
    deep = layers // blocks
    sources = (s0, vel, grad, rot, tgt)

    def copies(block):
        slot, found = 0, []
        for number, ref in enumerate(sources):
            depth = pl.ds(block * deep, deep)
            target = stage.at[pl.ds(slot, ref.shape[0]), depth]
            found.append(
                pltpu.make_async_copy(ref.at[:, depth], target, sems.at[block, number])
            )
            slot += ref.shape[0]
        return found

    for block in range(blocks):
        for copy in copies(block):
            copy.start()
    lane = lane_iota(out.shape[1:])
    Field(field, None).clear()
    clear_planes(coef, [UZ])

    def load(z, carry):
        zero = jnp.zeros((8, LANES), F32)
        for tile in range(2):
            for c in range(5):
                field[c, z + 1, tile, OWN] = stage[c, z, :, span(tile)]
            u = [DT * stage[VEL + d, z, :, span(tile)] for d in range(3)]
            turn = DT * stage[ROT, z, :, span(tile)]
            parts = gradient_parts(lambda i: stage[GRAD + i, z, :, span(tile)])
            for key, value in parts.items():
                coef[PLACE[key], z + 1, tile] = value
            coef[SPREAD, z + 1, tile] = 2.0 * turn
            coef[UX, z + 1, tile] = u[0]
            coef[UZ, z + 1, tile] = u[2]
            uy[z + 1, tile, 0:8] = zero
            uy[z + 1, tile, 24:32] = zero
            uy[z + 1, tile, OWN] = u[1]
            base[z + 1, tile] = 6.0 * turn + (jnp.abs(u[0]) + jnp.abs(u[1]) + jnp.abs(u[2]))
        return carry


    def step(block, carry):
        for copy in copies(block):
            copy.wait()
        for c in range(NEEDLES):
            total = out[c]
            for k in range(deep):
                z = block * deep + k
                low, high = stage[c, z, :, span(0)], stage[c, z, :, span(1)]
                both = jnp.where(lane < HALO, low, high)
                moved = pltpu.roll(both, (8 * z + HALO) % LANES, 1)
                total = jnp.where(lane // 8 == z, moved, total)
            out[c] = total
        lax.fori_loop(block * deep, (block + 1) * deep, load, 0)
        return carry

    lax.fori_loop(0, blocks, step, 0)

    odd = lax.axis_index(axis_cd) % 2 == 1
    outer = lane % 8 < HALO
    first[PAIRS] = needle[...]
    second[PAIRS] = needle[...]
    for c in range(PAIRS):
        here, other = out[c], out[min(c + PAIRS, NEEDLES - 1)]
        to_right = jnp.where(outer, here, pltpu.roll(other, HALO, 1))
        to_left = jnp.where(outer, pltpu.roll(other, LANES - HALO, 1), here)
        first[c] = jnp.where(odd, to_left, to_right)
        second[c] = jnp.where(odd, to_right, to_left)


def bulk_kernel(field, coef, base, uy, s1):
    layers = field.shape[1] - 2
    state = Field(field, None)

    def advance(z, carry):
        for tile in range(2):
            at = (z + 1, tile)
            m, damp = coefficients(coef, base, *at)
            wind = (coef[(UX,) + at], uy[at + (OWN,)], coef[(UZ,) + at])
            a = [state.own(c, z, tile) for c in range(5)]
            out = forward(a, m, damp, coef[(SPREAD,) + at], wind, state.around(z, tile))
            for c in range(5):
                s1[c, z + 1, tile, OWN] = out[c]
        return carry

    lax.fori_loop(0, layers, advance, 0)


def split_three(value):
    parts = []
    for _ in range(3):
        part = value.astype(jnp.bfloat16).astype(F32)
        parts.append(part)
        value = value - part
    return parts


def feet_block(ref, block, count):
    place = jnp.clip(block, 0, count - 1) * LANES
    row = ref[:, pl.ds(pl.multiple_of(place, LANES), LANES)]
    return jnp.where((block >= 0) & (block < count), row, 0)


def first_kernel(
    axis_md,
    axis_cd,
    own,
    needle,
    near_first,
    near_second,
    far_first,
    far_second,
    start,
    end,
    column,
    field,
    coef,
    uy,
    base_in,
    s1_in,
    s1,
    base,
    strip_s0,
    strip_coef,
    strip_base,
    strip_uy,
    strip_s1,
    strip_tgt,
    up,
    down,
    spread,
    cover,
    source,
    joint,
):
    layers = field.shape[1] - 2
    height = own.shape[1]
    md = lax.axis_index(axis_md)
    count = lax.axis_size(axis_md)
    lane = lane_iota((height, LANES))
    outer = lane % 8 < HALO
    odd = lax.axis_index(axis_cd) % 2 == 1

    def from_left(c):
        return jnp.where(odd, near_second[c], near_first[c])

    def from_right(c):
        return jnp.where(odd, near_first[c], near_second[c])

    def half(take, c, turn):
        return take(c) if c < PAIRS else pltpu.roll(take(c - PAIRS), turn, 1)

    near = lane_iota((1, LANES)) < LANES // 2

    def feet(ref):
        far = jnp.where(near, feet_block(ref, md + 2, count), feet_block(ref, md - 2, count))
        blocks = [feet_block(ref, md + d, count) for d in (-1, 0, 1)]
        return jnp.concatenate(blocks + [far], axis=1)

    starts, ends, columns = feet(start), feet(end), feet(column)
    far = jnp.where((lane < LANES // 2) == odd, far_first[...], far_second[...])
    rates = jnp.concatenate(
        [from_left(PAIRS), needle[...], from_right(PAIRS), far], axis=1
    )
    needles = rates.shape[1]
    picked = jnp.where(row_iota((height, needles)) == columns, 1.0, 0.0)
    for part, value in enumerate(split_three(rates)):
        for z in range(layers):
            spread[part, z * height : (z + 1) * height] = (picked * value[z : z + 1]).astype(
                jnp.bfloat16
            )
    length = 2 * LANES
    cells = row_iota((length + LANES, needles))
    beyond = cells - length
    strip = jnp.where(beyond < 8, beyond - HALO, beyond - 8 + length - HALO)
    cells = jnp.where(cells < length, cells, strip) + md * length
    cover[...] = jnp.where((cells >= starts) & (cells < ends), 1.0, 0.0).astype(jnp.bfloat16)
    product = jnp.zeros((layers * height, length + LANES), F32)
    for part in range(3):
        product = product + lax.dot_general(
            spread[part], cover[...], (((1,), (1,)), ((), ())), preferred_element_type=F32
        )
    source[...] = (DT * product).reshape(source.shape)

    state = Field(field, strip_s0, joint)
    state.clear_strips()
    has_left, has_right = md > 0, md < count - 1
    for side in range(2):

        def raw(c):
            if side == 0:
                return jnp.where(outer, jnp.where(has_left, half(from_left, c, LANES - HALO), 0.0), own[c])
            return jnp.where(outer, own[c], jnp.where(has_right, half(from_right, c, HALO), 0.0))

        for c in range(5):
            strip_s0[c, side, OWN] = raw(S0 + c)
            strip_tgt[c, side] = raw(TGT + c)
        u = [DT * raw(VEL + d) for d in range(3)]
        turn = DT * raw(ROT)
        for key, value in gradient_parts(lambda i: raw(GRAD + i)).items():
            strip_coef[PLACE[key], side] = value
        strip_coef[SPREAD, side] = 2.0 * turn
        strip_coef[UX, side] = u[0]
        strip_coef[UZ, side] = u[2]
        strip_uy[side, 0:8] = jnp.zeros((8, LANES), F32)
        strip_uy[side, 24:32] = jnp.zeros((8, LANES), F32)
        strip_uy[side, OWN] = u[1]
        damp = 6.0 * turn + (jnp.abs(u[0]) + jnp.abs(u[1]) + jnp.abs(u[2]))
        taken = jnp.zeros((height, LANES), F32)
        for z in range(layers):
            moved = pltpu.roll(source[z, :, span(2)], (8 * z - 8 * side) % LANES, 1)
            taken = jnp.where(lane // 8 == z, moved, taken)
        strip_base[side] = damp + taken

    for side in range(2):
        m, damp = coefficients(strip_coef, strip_base, side)
        wind = (strip_coef[UX, side], strip_uy[side, OWN], strip_coef[UZ, side])
        a = [strip_s0[c, side, OWN] for c in range(5)]
        spin = strip_coef[SPREAD, side]
        out = forward(a, m, damp, spin, wind, state.strip_around(side))
        for c in range(5):
            strip_s1[c, side, OWN] = out[c]
    state.join()

    def put(side):
        def at(place):
            return line(None, side * 11 + place, 22, layers)

        for c in range(5):
            first, new = strip_s0.at[c, side], strip_s1.at[c, side]
            up[at(c)], down[at(c)] = first[23:24], first[8:9]
            up[at(5 + c)], down[at(5 + c)] = new[23:24], new[8:9]
        wind = strip_uy.at[side]
        up[at(10)] = -jnp.minimum(wind[23:24], 0.0)
        down[at(10)] = jnp.maximum(wind[8:9], 0.0)

    def mend(z, carry):
        for tile in range(2):
            gain = source[z, :, span(tile)]
            base[z + 1, tile] = base_in[z + 1, tile] + gain
            u = coef[UX, z + 1, tile]
            if tile == 0:
                weight, turn = jnp.where(lane == 0, jnp.maximum(u, 0.0), 0.0), 1
            else:
                weight, turn = jnp.where(lane == LANES - 1, -jnp.minimum(u, 0.0), 0.0), -1
            for c in range(5):
                edge = pltpu.roll(joint[c], (2 * LANES - HALO + turn - 8 * z) % LANES, 1)
                s1[c, z + 1, tile, OWN] = (
                    s1_in[c, z + 1, tile, OWN]
                    - gain * field[c, z + 1, tile, OWN]
                    + weight * edge
                )
        return carry

    clear_planes(s1)
    lax.fori_loop(0, layers, mend, 0)
    for tile in range(2):
        for message, row in ((up, 23), (down, 8)):
            for c in range(5):
                message[planes(tile * 11 + c, layers)] = row_of(field, c, tile, row)
                message[planes(tile * 11 + 5 + c, layers)] = row_of(s1, c, tile, row)
        out, into = row_of(uy, 0, tile, 23), row_of(uy, 0, tile, 8)
        up[planes(tile * 11 + 10, layers)] = -jnp.minimum(out, 0.0)
        down[planes(tile * 11 + 10, layers)] = jnp.maximum(into, 0.0)
    for side in range(2):
        put(side)


def cd_flags(axis_cd):
    cd = lax.axis_index(axis_cd)
    return cd > 0, cd < lax.axis_size(axis_cd) - 1


def advance_kernel(s1, strip_s1, coef, base, uy, tgt, s2, goal, joint):
    layers = tgt.shape[1]
    state = Field(s1, strip_s1, joint)
    state.join()

    def advance(z, carry):
        for tile in range(2):
            at = (z + 1, tile)
            m, damp = coefficients(coef, base, *at)
            wind = (coef[(UX,) + at], uy[at + (OWN,)], coef[(UZ,) + at])
            a = [state.own(c, z, tile) for c in range(5)]
            out = forward(a, m, damp, coef[(SPREAD,) + at], wind, state.around(z, tile))
            for c in range(5):
                s2[(c,) + at] = out[c]
                goal[(c,) + at] = tgt[c, z, :, span(tile)]
        return carry

    lax.fori_loop(0, layers, advance, 0)


def edge_kernel(
    axis_cd,
    s1,
    strip_s1_in,
    coef,
    base,
    uy,
    goal,
    strip_coef,
    strip_base,
    strip_uy,
    strip_tgt,
    own_up,
    own_down,
    from_below,
    from_above,
    s1_edge,
    s2_edge,
    strip_adj2,
    strip_adj1,
    up,
    down,
    strip_s1,
):
    layers = goal.shape[1] - 2
    has_below, has_above = cd_flags(axis_cd)

    state, delta = Field(s1, strip_s1), Field(s1, strip_adj2)
    delta.clear_strips()
    for side in range(2):

        def at(place):
            return line(None, side * 11 + place, 22, layers)

        wind = strip_uy.at[side]
        low_u, high_u = jnp.maximum(wind[8:9], 0.0), -jnp.minimum(wind[23:24], 0.0)
        low_n, high_n = from_below[at(10)], from_above[at(10)]
        for c in range(5):
            old, new = at(c), at(5 + c)
            ref = strip_s1.at[c, side]
            ref[OWN] = strip_s1_in[c, side, OWN]
            low = from_below[new] + low_n * own_down[old]
            high = from_above[new] + high_n * own_up[old]
            ref[7:8] = jnp.where(has_below, low, 0.0)
            ref[24:25] = jnp.where(has_above, high, 0.0)
            ref[8:9] = ref[8:9] + jnp.where(has_below, low_u * from_below[old], 0.0)
            ref[23:24] = ref[23:24] + jnp.where(has_above, high_u * from_above[old], 0.0)
    for side in range(2):
        m, damp = coefficients(strip_coef, strip_base, side)
        wind = (strip_coef[UX, side], strip_uy[side, OWN], strip_coef[UZ, side])
        a = [strip_s1[c, side, OWN] for c in range(5)]
        spin = strip_coef[SPREAD, side]
        out = forward(a, m, damp, spin, wind, state.strip_around(side))
        for c in range(5):
            strip_adj2[c, side, OWN] = out[c] - strip_tgt[c, side]
    for side in range(2):

        def at(place):
            return line(None, side * 10 + place, 20, layers)

        m, damp = coefficients(strip_coef, strip_base, side)
        a = [strip_s1[c, side, OWN] for c in range(5)]
        b = [strip_adj2[c, side, OWN] for c in range(5)]
        wind = strip_back_wind(strip_coef, strip_uy, side)
        out = backward(b, a, m, damp, wind, delta.strip_around(side))
        high = -jnp.minimum(strip_uy[side, 23:24], 0.0)
        low = jnp.maximum(strip_uy[side, 8:9], 0.0)
        for c in range(5):
            strip_adj1[c, side, OWN] = out[c]
            up[at(c)] = high * b[c][-1:]
            down[at(c)] = low * b[c][:1]
            up[at(5 + c)] = high * out[c][-1:]
            down[at(5 + c)] = low * out[c][:1]

    def constants(tile, row):
        m = {key: row_of(coef, place, tile, row) for key, place in PLACE.items()}
        return m, row_of(base, 0, tile, row)

    for number, (message, mine, valid, outgoing) in enumerate(
        ((from_below, own_down, has_below, down), (from_above, own_up, has_above, up))
    ):
        rows = (0, 1, 2) if number == 0 else (15, 14, 13)
        sides = (0, 1)

        def plane(ref, place, tile):
            return ref[planes(tile * 11 + place, layers)]

        lines = [{}, {}, {}, {}]
        for c in range(5):
            for tile in range(2):
                old, new = plane(message, c, tile), plane(message, 5 + c, tile)
                weight = plane(message, 10, tile)
                lines[0][c, tile] = jnp.where(
                    valid, new + weight * plane(mine, c, tile), 0.0
                )
                lines[1][c, tile] = plane(mine, 5 + c, tile) + jnp.where(
                    valid, plane(mine, 10, tile) * old, 0.0
                )
                s1_edge[c, number, tile] = lines[1][c, tile]
                for k in (1, 2):
                    lines[k + 1][c, tile] = row_of(s1, c, tile, 8 + rows[k])

        def strip_edge(ref, c, row):
            left, right = (ref[c, side, 8 + row : 9 + row] for side in sides)
            return edge_column(left, right, layers)

        def ordered(outer, inner):
            return (outer, inner) if number == 0 else (inner, outer)

        misses = [{}, {}]
        for k in range(2):
            row = rows[k]
            edges = [strip_edge(strip_s1, c, row) for c in range(5)]
            for tile in range(2):
                m, damp = constants(tile, row)
                wind = (
                    row_of(coef, UX, tile, row),
                    row_of(uy, 0, tile, 8 + row),
                    row_of(coef, UZ, tile, row),
                )
                a = [lines[k + 1][c, tile] for c in range(5)]

                def around(c):
                    tiles = [lines[k + 1][c, t] for t in range(2)]
                    return (
                        x_pair(tiles, tile, edges[c]),
                        ordered(lines[k][c, tile], lines[k + 2][c, tile]),
                        layer_pair(a[c]),
                    )

                out = forward(a, m, damp, row_of(coef, SPREAD, tile, row), wind, around)
                for c in range(5):
                    s2_edge[c, 2 * number + k, tile] = out[c]
                    misses[k][c, tile] = out[c] - row_of(goal, c, tile, row)

        row = rows[0]
        edges = [strip_edge(strip_adj2, c, row) for c in range(5)]
        left, right = (strip_coef[UX, side, row : row + 1] for side in sides)
        edge_x = edge_column(left, right, layers)
        for tile in range(2):
            m, damp = constants(tile, row)
            a = [lines[1][c, tile] for c in range(5)]
            b = [misses[0][c, tile] for c in range(5)]
            zero = jnp.zeros_like(b[0])
            wind = (
                x_pair([row_of(coef, UX, t, row) for t in range(2)], tile, edge_x),
                ordered(zero, row_of(uy, 0, tile, 8 + rows[1])),
                layer_pair(row_of(coef, UZ, tile, row)),
            )

            def around(c):
                tiles = [misses[0][c, t] for t in range(2)]
                return (
                    x_pair(tiles, tile, edges[c]),
                    ordered(zero, misses[1][c, tile]),
                    layer_pair(b[c]),
                )

            out = backward(b, a, m, damp, wind, around)
            weight = plane(mine, 10, tile)
            for c in range(5):
                outgoing[planes(tile * 10 + c, layers)] = weight * b[c]
                outgoing[planes(tile * 10 + 5 + c, layers)] = weight * out[c]


def needle_feet(ref, md, count):
    return jnp.concatenate([feet_block(ref, md + d, count) for d in (-1, 0, 1)], axis=1)


def own_cover(md, length, starts, ends):
    cells = row_iota((length, starts.shape[1])) + md * length
    return jnp.where((cells >= starts) & (cells < ends), 1.0, 0.0).astype(jnp.bfloat16)


def covered_sum(values, cover):
    product = jnp.zeros((values.shape[0], cover.shape[1]), F32)
    for part in split_three(values):
        product = product + jnp.dot(
            part.astype(jnp.bfloat16), cover, preferred_element_type=F32
        )
    return product


def second_kernel(
    axis_md,
    s1_in,
    s2_in,
    goal,
    s1_edge,
    s2_edge,
    field,
    coef,
    base,
    uy,
    strip_coef,
    strip_adj2,
    strip_adj1,
    start,
    end,
    column,
    s2_out,
    adj0,
    gained,
    adj1,
    dots,
    s1,
    s2,
    adj2,
    joint,
    joint1,
):
    layers, height = goal.shape[1] - 2, goal.shape[3]
    length = 2 * LANES
    md = lax.axis_index(axis_md)
    count = lax.axis_size(axis_md)

    def gather(z, carry):
        for tile in range(2):
            for c in range(5):
                s1[c, z + 1, tile] = s1_in[c, z + 1, tile, OWN]
                s2[c, z + 1, tile] = s2_in[c, z + 1, tile]
        return carry

    lax.fori_loop(0, layers, gather, 0)
    for c in range(5):
        for tile in range(2):
            for number, row in enumerate((0, 15)):
                set_row(s1, c, tile, row, s1_edge[c, number, tile])
            for number, row in enumerate((0, 1, 15, 14)):
                set_row(s2, c, tile, row, s2_edge[c, number, tile])

    delta = Field(adj2, strip_adj2, joint)
    delta.clear()
    delta.join()

    def compare(z, carry):
        for tile in range(2):
            total = 0.0
            for c in range(5):
                value = s2[c, z + 1, tile]
                miss = value - goal[c, z + 1, tile]
                s2_out[c, z, :, span(tile)] = value
                adj2[c, z + 1, tile, OWN] = miss
                total = total + miss * s1[c, z + 1, tile]
            dots[z, :, span(tile)] = total
        return carry

    lax.fori_loop(0, layers, compare, 0)
    edge_x = merged(strip_coef, UX, slice(None))

    def retreat(z, carry):
        for tile in range(2):
            m, damp = coefficients(coef, base, z + 1, tile)
            a = [s1[c, z + 1, tile] for c in range(5)]
            b = [delta.own(c, z, tile) for c in range(5)]
            wind = back_wind(coef, uy, edge_x, z, tile)
            out = backward(b, a, m, damp, wind, delta.around(z, tile))
            for c in range(5):
                adj1[c, z + 1, tile, OWN] = out[c]
        return carry

    last_delta = Field(adj1, strip_adj1, joint1)
    last_delta.clear()
    last_delta.join()
    lax.fori_loop(0, layers, retreat, 0)

    def finish(z, carry):
        for tile in range(2):
            m, damp = coefficients(coef, base, z + 1, tile)
            a = [field[c, z + 1, tile, OWN] for c in range(5)]
            b = [last_delta.own(c, z, tile) for c in range(5)]
            wind = back_wind(coef, uy, edge_x, z, tile)
            out = backward(b, a, m, damp, wind, last_delta.around(z, tile))
            total = dots[z, :, span(tile)]
            for c in range(5):
                adj0[c, z + 1, tile] = out[c]
                total = total + a[c] * b[c]
            dots[z, :, span(tile)] = -DT * total
        return carry

    lax.fori_loop(0, layers, finish, 0)
    starts, ends, columns = (needle_feet(ref, md, count) for ref in (start, end, column))
    cover = own_cover(md, length, starts, ends)
    product = covered_sum(dots[...].reshape(layers * height, length), cover)
    picked = jnp.where(row_iota((height, starts.shape[1])) == columns, 1.0, 0.0)
    for z in range(layers):
        gained[z : z + 1] = jnp.sum(
            product[z * height : (z + 1) * height] * picked, axis=0, keepdims=True
        )


def third_kernel(
    axis_md,
    axis_cd,
    gained,
    field,
    from_below,
    from_above,
    start,
    end,
    column,
    first,
    kept,
    second,
):
    layers = field.shape[1] - 2
    length = 2 * LANES
    md = lax.axis_index(axis_md)
    count = lax.axis_size(axis_md)
    odd = lax.axis_index(axis_cd) % 2 == 1
    lines = []
    for message, valid, row in zip((from_below, from_above), cd_flags(axis_cd), (8, 23)):
        parts = []
        for tile in range(2):
            total = 0.0
            for c in range(5):
                brought = message[planes(tile * 10 + c, layers)]
                total = total + brought * row_of(field, c, tile, row)
            parts.append(jnp.where(valid, -DT * total, 0.0))
        lines.append(jnp.concatenate(parts, axis=1))
    starts, ends, columns = (needle_feet(ref, md, count) for ref in (start, end, column))
    cover = own_cover(md, length, starts, ends)
    product = covered_sum(jnp.concatenate(lines, axis=0), cover)
    total = gained[...]
    for number, row in enumerate((0, 15)):
        here = product[number * layers : (number + 1) * layers]
        total = total + jnp.where(columns == row, here, 0.0)
    first[...] = jnp.where(odd, total[:, span(0)], total[:, span(2)])
    kept[...] = total[:, span(1)]
    second[...] = jnp.where(odd, total[:, span(2)], total[:, span(0)])


def fourth_kernel(
    axis_cd,
    adj0_in,
    field,
    coef,
    base,
    uy,
    strip_coef,
    weights_below,
    weights_above,
    own_up,
    own_down,
    from_below,
    from_above,
    out_field,
    adj0,
):
    layers = field.shape[1] - 2
    has_below, has_above = cd_flags(axis_cd)

    def gather(z, carry):
        for tile in range(2):
            for c in range(5):
                adj0[c, z + 1, tile] = adj0_in[c, z + 1, tile]
        return carry

    lax.fori_loop(0, layers, gather, 0)

    for number, (weights, message, mine, valid) in enumerate(
        (
            (weights_below, from_below, own_down, has_below),
            (weights_above, from_above, own_up, has_above),
        )
    ):
        row, inner = ((0, 1), (15, 14))[number]
        brought = {}
        for c in range(5):
            for tile in range(2):
                value = message[planes(tile * 10 + c, layers)]
                brought[c, tile] = jnp.where(valid, value, 0.0)
        edges = []
        for c in range(5):
            left, right = (message[line(None, side * 10 + c, 20, layers)] for side in (0, 1))
            edges.append(jnp.where(valid, edge_column(left, right, layers), 0.0))
        left, right = (strip_coef[UX, side, row : row + 1] for side in (0, 1))
        edge_x = edge_column(left, right, layers)
        for tile in range(2):
            m = {key: row_of(coef, place, tile, row) for key, place in PLACE.items()}
            damp = row_of(base, 0, tile, row)
            a = [row_of(field, c, tile, 8 + row) for c in range(5)]
            b = [brought[c, tile] for c in range(5)]
            wind = (
                x_pair([row_of(coef, UX, t, row) for t in range(2)], tile, edge_x),
                layer_pair(row_of(coef, UZ, tile, row)),
            )

            def around(c):
                tiles = [brought[c, t] for t in range(2)]
                return x_pair(tiles, tile, edges[c]), layer_pair(b[c])

            out = backward(b, a, m, damp, wind, around)
            speed = row_of(uy, 0, tile, 8 + row)
            inward = -jnp.minimum(speed, 0.0) if number == 0 else jnp.maximum(speed, 0.0)
            weight = weights[planes(tile * 11 + 10, layers)]
            for c in range(5):
                own = mine[planes(tile * 10 + c, layers)]
                far = message[planes(tile * 10 + 5 + c, layers)] + weight * own
                total = out[c] + jnp.where(valid, far, 0.0)
                set_row(adj0, c, tile, row, row_of(adj0, c, tile, row) + total)
                more = inward * b[c]
                set_row(adj0, c, tile, inner, row_of(adj0, c, tile, inner) + more)

    def scatter(z, carry):
        for tile in range(2):
            for c in range(5):
                out_field[c, z, :, span(tile)] = adj0[c, z + 1, tile]
        return carry

    lax.fori_loop(0, layers, scatter, 0)


def ring(value, axis, steps):
    count = lax.axis_size(axis)
    return lax.ppermute(value, axis, [(i, (i + steps) % count) for i in range(count)])


def winding(value, steps, turn):
    rows, columns = lax.axis_size("md"), lax.axis_size("cd")
    pairs = []
    for column in range(columns):
        for row in range(rows):
            target = row + (steps if column % 2 == turn else -steps)
            if 0 <= target < rows:
                pairs.append((row * columns + column, target * columns + column))
            else:
                pairs.append((row * columns + column, row * columns + (column ^ 1)))
    return lax.ppermute(value, ("md", "cd"), pairs)


def both_ways(value, steps):
    return winding(value, steps, 0), winding(value, steps, 1)


def shape_of(*dims, dtype=F32):
    return jax.ShapeDtypeStruct(dims, dtype)


def scratch(*dims, dtype=F32):
    return pltpu.VMEM(dims, dtype)


def cost(microseconds):
    return pl.CostEstimate(
        flops=int(microseconds * 1e6), bytes_accessed=int(microseconds * 3e6), transcendentals=0
    )


def params(mebibytes):
    return pltpu.CompilerParams(vmem_limit_bytes=mebibytes * 1024 * 1024)


def local(orientation, velocity, velocity_grad, rotary, target, needle_params, *feet):
    _, layers, height, length = orientation.shape
    rotary = rotary[None]
    rates = jnp.transpose(needle_params[:, 0, :])
    feet = [foot.reshape(1, -1) for foot in feet]
    padded = (layers + 2, 2, ROWS, LANES)
    plain = (layers + 2, 2, height, LANES)
    strip_padded, strip = (2, ROWS, LANES), (2, height, LANES)
    message, back_message = shape_of(22 * layers + 24, LANES), shape_of(20 * layers + 24, LANES)
    joint = scratch(5, height, LANES)

    hbm = pl.BlockSpec(memory_space=pltpu.HBM)
    blocks = 4
    packed, first, second, field, coef, base, uy = pl.pallas_call(
        functools.partial(pack_kernel, "cd"),
        in_specs=[hbm] * 5 + [pl.BlockSpec(memory_space=pltpu.VMEM)],
        out_shape=[
            shape_of(NEEDLES, height, LANES),
            shape_of(PAIRS + 1, height, LANES),
            shape_of(PAIRS + 1, height, LANES),
            shape_of(5, *padded),
            shape_of(COEFS, *plain),
            shape_of(*plain),
            shape_of(*padded),
        ],
        scratch_shapes=[
            scratch(NEEDLES, layers, height, length),
            pltpu.SemaphoreType.DMA((blocks, 5)),
        ],
        compiler_params=params(20),
        cost_estimate=cost(4),
    )(
        *(
            pltpu.with_memory_space_constraint(field, pltpu.HBM)
            for field in (orientation, velocity, velocity_grad, rotary, target)
        ),
        rates,
    )
    far = both_ways(rates, 2)
    near = winding(first, 1, 0), winding(second, 1, 1)

    s1 = pl.pallas_call(
        bulk_kernel,
        out_shape=shape_of(5, *padded),
        compiler_params=params(16),
        cost_estimate=cost(2),
    )(field, coef, base, uy)

    s1, base, strip_s0, strip_coef, strip_base, strip_uy, strip_s1, strip_tgt, up, down = (
        pl.pallas_call(
            functools.partial(first_kernel, "md", "cd"),
            out_shape=[
                shape_of(5, *padded),
                shape_of(*plain),
                shape_of(5, *strip_padded),
                shape_of(COEFS, *strip),
                shape_of(*strip),
                shape_of(*strip_padded),
                shape_of(5, *strip_padded),
                shape_of(5, *strip),
                message,
                message,
            ],
            scratch_shapes=[
                scratch(3, layers * height, 4 * LANES, dtype=jnp.bfloat16),
                scratch(length + LANES, 4 * LANES, dtype=jnp.bfloat16),
                scratch(layers, height, length + LANES),
                joint,
            ],
            compiler_params=params(24),
        cost_estimate=cost(4),
        )(
            packed,
            rates,
            *near,
            *far,
            *feet,
            field,
            coef,
            uy,
            base,
            s1,
        )
    )
    below = ring(up, "cd", 1)
    above = ring(down, "cd", -1)

    s2_part, goal = pl.pallas_call(
        advance_kernel,
        out_shape=[shape_of(5, *plain), shape_of(5, *plain)],
        scratch_shapes=[joint],
        compiler_params=params(16),
        cost_estimate=cost(4),
    )(s1, strip_s1, coef, base, uy, target)
    s1_edge, s2_edge, strip_adj2, strip_adj1, back_up, back_down = pl.pallas_call(
        functools.partial(edge_kernel, "cd"),
        out_shape=[
            shape_of(5, 2, 2, layers, LANES),
            shape_of(5, 4, 2, layers, LANES),
            shape_of(5, *strip_padded),
            shape_of(5, *strip_padded),
            back_message,
            back_message,
        ],
        scratch_shapes=[scratch(5, *strip_padded)],
        compiler_params=params(16),
        cost_estimate=cost(2),
    )(
        s1,
        strip_s1,
        coef,
        base,
        uy,
        goal,
        strip_coef,
        strip_base,
        strip_uy,
        strip_tgt,
        up,
        down,
        below,
        above,
    )
    back_below = ring(back_up, "cd", 1)
    back_above = ring(back_down, "cd", -1)

    part = shape_of(*rates.shape)
    s2, adj0_part, gained = pl.pallas_call(
        functools.partial(second_kernel, "md"),
        out_shape=[
            shape_of(*orientation.shape),
            shape_of(5, *plain),
            shape_of(layers, 3 * LANES),
        ],
        scratch_shapes=[
            scratch(5, *padded),
            scratch(layers, height, length),
            scratch(5, *plain),
            scratch(5, *plain),
            scratch(5, *padded),
            joint,
            joint,
        ],
        compiler_params=params(24),
        cost_estimate=cost(9),
    )(
        s1,
        s2_part,
        goal,
        s1_edge,
        s2_edge,
        field,
        coef,
        base,
        uy,
        strip_coef,
        strip_adj2,
        strip_adj1,
        *feet,
    )

    part_first, part_own, part_second = pl.pallas_call(
        functools.partial(third_kernel, "md", "cd"),
        out_shape=[part, part, part],
        compiler_params=params(16),
        cost_estimate=cost(1),
    )(gained, field, back_below, back_above, *feet)
    part_first = winding(part_first, 1, 0)
    part_second = winding(part_second, 1, 1)

    adj0 = pl.pallas_call(
        functools.partial(fourth_kernel, "cd"),
        out_shape=shape_of(*orientation.shape),
        scratch_shapes=[scratch(5, *plain)],
        compiler_params=params(16),
        cost_estimate=cost(2),
    )(
        adj0_part,
        field,
        coef,
        base,
        uy,
        strip_coef,
        below,
        above,
        back_up,
        back_down,
        back_below,
        back_above,
    )
    gradient = part_own + part_first + part_second
    return s2, adj0, jnp.transpose(gradient)[:, None, :]


def solution(mesh):
    field = P(None, None, "cd", "md")
    feet = P(None, "cd")
    needles = P("md", "cd", None)
    return jax.shard_map(
        local,
        mesh=mesh,
        in_specs=(field, field, field, P(None, "cd", "md"), field, needles, feet, feet, feet),
        out_specs=(field, field, needles),
        check_vma=False,
    )
```

```python
import functools

import jax
import jax.numpy as jnp
from jax import lax
from jax.experimental import pallas as pl
from jax.experimental.pallas import tpu as pltpu
from jax.sharding import PartitionSpec as P

XI = 0.95
DT = 0.1
LANES = 128
F32 = jnp.float32
HALO = 4
S0, VEL, GRAD, ROT, TGT, NEEDLES = 0, 5, 8, 17, 18, 23
PAIRS = 12
PLACE = {(0, 0): 0, (1, 1): 1, (0, 1): 2, (1, 0): 3, (0, 2): 4, (2, 0): 5, (1, 2): 6, (2, 1): 7}
SPREAD, UX, UZ, COEFS = 8, 9, 10, 11
ROWS = 32
OWN, BEHIND, FRONT = slice(8, 24), slice(7, 23), slice(9, 25)


def lane_iota(shape):
    return lax.broadcasted_iota(jnp.int32, shape, len(shape) - 1)


def row_iota(shape):
    return lax.broadcasted_iota(jnp.int32, shape, len(shape) - 2)


def span(tile):
    return slice(tile * LANES, (tile + 1) * LANES)


def gradient_parts(read):
    g = [read(i) for i in range(9)]
    low = 0.5 * (XI - 1.0) * DT
    m = {}
    for i, j in ((0, 1), (0, 2), (1, 2)):
        a, b = g[3 * i + j], g[3 * j + i]
        both = low * (a + b)
        m[i, j] = DT * a + both
        m[j, i] = DT * b + both
    m[0, 0] = (XI * DT) * (g[0] - g[8])
    m[1, 1] = (XI * DT) * (g[4] - g[8])
    return m


def forward(a, m, base, spread, wind, around):
    a11, a22, a12, a13, a23 = a
    a33 = 1.0 - a11 - a22
    n00 = m[0, 0] * a11 + m[0, 1] * a12 + m[0, 2] * a13
    n01 = m[0, 0] * a12 + m[0, 1] * a22 + m[0, 2] * a23
    n02 = m[0, 0] * a13 + m[0, 1] * a23 + m[0, 2] * a33
    n10 = m[1, 0] * a11 + m[1, 1] * a12 + m[1, 2] * a13
    n11 = m[1, 0] * a12 + m[1, 1] * a22 + m[1, 2] * a23
    n12 = m[1, 0] * a13 + m[1, 1] * a23 + m[1, 2] * a33
    n20 = m[2, 0] * a11 + m[2, 1] * a12
    n21 = m[2, 0] * a12 + m[2, 1] * a22
    n22 = m[2, 0] * a13 + m[2, 1] * a23
    keep = 1.0 - (base + 2.0 * (n00 + n11 + n22))
    gain = (2.0 * n00 + spread, 2.0 * n11 + spread, n01 + n10, n02 + n20, n12 + n21)
    out = []
    for c in range(5):
        total = gain[c] + keep * a[c]
        for u, (behind, front) in zip(wind, around(c)):
            total = total + jnp.abs(u) * jnp.where(u > 0.0, behind, front)
        out.append(total)
    return out


def backward(b, a, m, base, wind, around):
    b1, b2, b3, b4, b5 = b
    a11, a22, a12, a13, a23 = a
    g = -2.0 * (b1 * a11 + b2 * a22 + b3 * a12 + b4 * a13 + b5 * a23)
    trace = (
        m[0, 0] * a11
        + m[1, 1] * a22
        + (m[0, 1] + m[1, 0]) * a12
        + (m[0, 2] + m[2, 0]) * a13
        + (m[1, 2] + m[2, 1]) * a23
    )
    s00, s11, s22 = 2.0 * b1 + g, 2.0 * b2 + g, g
    h00 = m[0, 0] * s00 + m[1, 0] * b3 + m[2, 0] * b4
    h01 = m[0, 0] * b3 + m[1, 0] * s11 + m[2, 0] * b5
    h02 = m[0, 0] * b4 + m[1, 0] * b5 + m[2, 0] * s22
    h10 = m[0, 1] * s00 + m[1, 1] * b3 + m[2, 1] * b4
    h11 = m[0, 1] * b3 + m[1, 1] * s11 + m[2, 1] * b5
    h12 = m[0, 1] * b4 + m[1, 1] * b5 + m[2, 1] * s22
    h20 = m[0, 2] * s00 + m[1, 2] * b3
    h21 = m[0, 2] * b3 + m[1, 2] * s11
    h22 = m[0, 2] * b4 + m[1, 2] * b5
    keep = 1.0 - (base + 2.0 * trace)
    gain = (h00 - h22, h11 - h22, h01 + h10, h02 + h20, h12 + h21)
    weights = [(jnp.minimum(w, 0.0), jnp.maximum(f, 0.0)) for w, f in wind]
    out = []
    for c in range(5):
        total = gain[c] + keep * b[c]
        for (low, high), (behind, front) in zip(weights, around(c)):
            total = total + (high * front - low * behind)
        out.append(total)
    return out


def merged(strips, c, rows):
    left, right = strips[c, 0, rows], strips[c, 1, rows]
    return jnp.where(lane_iota(left.shape) % 8 < HALO, left, right)


def edge_tile(joint, z):
    return pltpu.roll(joint, (2 * LANES - HALO - 8 * z) % LANES, 1)


def x_pair(tiles, tile, edge):
    cur = tiles[tile]
    prev, after = (edge, tiles[1]) if tile == 0 else (tiles[0], edge)
    lane = lane_iota(cur.shape)
    behind = pltpu.roll(jnp.where(lane == LANES - 1, prev, cur), 1, 1)
    front = pltpu.roll(jnp.where(lane == 0, after, cur), LANES - 1, 1)
    return behind, front


def strip_x(cur):
    return pltpu.roll(cur, 1, 1), pltpu.roll(cur, LANES - 1, 1)


def strip_z(cur):
    lane = lane_iota(cur.shape)
    behind = jnp.where(lane < 8, 0.0, pltpu.roll(cur, 8, 1))
    front = jnp.where(lane >= LANES - 8, 0.0, pltpu.roll(cur, LANES - 8, 1))
    return behind, front


def coefficients(coef, base, *at):
    m = {key: coef[(place,) + at] for key, place in PLACE.items()}
    return m, base[at]


class Field:
    def __init__(self, ref, strips, joint=None):
        self.ref, self.strips, self.joint = ref, strips, joint

    def join(self):
        for c in range(self.ref.shape[0]):
            self.joint[c] = merged(self.strips, c, OWN)

    def own(self, c, z, tile):
        return self.ref[c, z + 1, tile, OWN]

    def around(self, z, tile):
        def pairs(c):
            ref = self.ref
            tiles = [ref[c, z + 1, t, OWN] for t in range(2)]
            if self.joint is None:
                edge = jnp.zeros_like(tiles[0])
            else:
                edge = edge_tile(self.joint[c], z)
            return (
                x_pair(tiles, tile, edge),
                (ref[c, z + 1, tile, BEHIND], ref[c, z + 1, tile, FRONT]),
                (ref[c, z, tile, OWN], ref[c, z + 2, tile, OWN]),
            )

        return pairs

    def strip_around(self, side):
        def pairs(c):
            cur = self.strips[c, side, OWN]
            return (
                strip_x(cur),
                (self.strips[c, side, BEHIND], self.strips[c, side, FRONT]),
                strip_z(cur),
            )

        return pairs

    def clear(self):
        last = self.ref.shape[1] - 1
        zero = jnp.zeros((8, LANES), F32)
        clear_planes(self.ref)

        def layer(z, carry):
            for c in range(self.ref.shape[0]):
                for tile in range(2):
                    self.ref[c, z, tile, 0:8] = zero
                    self.ref[c, z, tile, 24:32] = zero
            return carry

        lax.fori_loop(1, last, layer, 0)

    def clear_strips(self):
        zero = jnp.zeros((8, LANES), F32)
        for c in range(self.strips.shape[0]):
            for side in range(2):
                self.strips[c, side, 0:8] = zero
                self.strips[c, side, 24:32] = zero


def clear_planes(ref, planes=None):
    last = ref.shape[1] - 1
    for c in planes or range(ref.shape[0]):
        for tile in range(2):
            for z in (0, last):
                ref[c, z, tile] = jnp.zeros(ref.shape[3:], F32)


def line(z, place, count, layers):
    if z is None:
        return slice(count * layers + place, count * layers + place + 1)
    return pl.ds(place * layers + z, 1)


def planes(place, layers):
    return slice(place * layers, (place + 1) * layers)


def row_place(ref, c, tile, row):
    high, rows = ref.shape[-4], ref.shape[-2]
    total = 1
    for size in ref.shape[:-1]:
        total *= size
    at = ((c * high + 1) * 2 + tile) * rows + row
    return ref.reshape(total, LANES), pl.ds(at, high - 2, stride=2 * rows)


def row_of(ref, c, tile, row):
    flat, place = row_place(ref, c, tile, row)
    return flat[place, :]


def set_row(ref, c, tile, row, value):
    flat, place = row_place(ref, c, tile, row)
    flat[place, :] = value


def layer_pair(cur):
    row, last = row_iota(cur.shape), cur.shape[0] - 1
    behind = jnp.where(row == 0, 0.0, pltpu.roll(cur, 1, 0))
    front = jnp.where(row == last, 0.0, pltpu.roll(cur, last, 0))
    return behind, front


def edge_column(left, right, layers):
    shape = (layers, LANES)
    lane, layer = lane_iota(shape), row_iota(shape)
    low = jnp.sum(jnp.where(lane == 8 * layer + HALO - 1, left, 0.0), axis=1, keepdims=True)
    high = jnp.sum(jnp.where(lane == 8 * layer + HALO, right, 0.0), axis=1, keepdims=True)
    return jnp.where(lane == LANES - 1, low, jnp.where(lane == 0, high, 0.0))


def back_wind(coef, uy, edge_x, z, tile):
    tiles = [coef[UX, z + 1, t] for t in range(2)]
    return (
        x_pair(tiles, tile, edge_tile(edge_x, z)),
        (uy[z + 1, tile, BEHIND], uy[z + 1, tile, FRONT]),
        (coef[UZ, z, tile], coef[UZ, z + 2, tile]),
    )


def strip_back_wind(coef, uy, side):
    return (
        strip_x(coef[UX, side]),
        (uy[side, BEHIND], uy[side, FRONT]),
        strip_z(coef[UZ, side]),
    )


def pack_kernel(
    axis_cd,
    s0,
    vel,
    grad,
    rot,
    tgt,
    needle,
    out,
    first,
    second,
    field,
    coef,
    base,
    uy,
    stage,
    needle_stage,
    sems,
    needle_sem,
):
    layers = stage.shape[1]
    blocks = sems.shape[0]
    deep = layers // blocks
    sources = (s0, vel, grad, rot, tgt)

    def copies(block):
        slot, found = 0, []
        for number, ref in enumerate(sources):
            depth = pl.ds(block * deep, deep)
            target = stage.at[pl.ds(slot, ref.shape[0]), depth]
            found.append(
                pltpu.make_async_copy(ref.at[:, depth], target, sems.at[block, number])
            )
            slot += ref.shape[0]
        return found

    for block in range(blocks):
        for copy in copies(block):
            copy.start()
    needle_copy = pltpu.make_async_copy(needle, needle_stage, needle_sem)
    needle_copy.start()
    lane = lane_iota(out.shape[1:])
    Field(field, None).clear()
    clear_planes(coef, [UZ])

    def load(z, carry):
        zero = jnp.zeros((8, LANES), F32)
        for tile in range(2):
            for c in range(5):
                field[c, z + 1, tile, OWN] = stage[c, z, :, span(tile)]
            u = [DT * stage[VEL + d, z, :, span(tile)] for d in range(3)]
            turn = DT * stage[ROT, z, :, span(tile)]
            parts = gradient_parts(lambda i: stage[GRAD + i, z, :, span(tile)])
            for key, value in parts.items():
                coef[PLACE[key], z + 1, tile] = value
            coef[SPREAD, z + 1, tile] = 2.0 * turn
            coef[UX, z + 1, tile] = u[0]
            coef[UZ, z + 1, tile] = u[2]
            uy[z + 1, tile, 0:8] = zero
            uy[z + 1, tile, 24:32] = zero
            uy[z + 1, tile, OWN] = u[1]
            base[z + 1, tile] = 6.0 * turn + (jnp.abs(u[0]) + jnp.abs(u[1]) + jnp.abs(u[2]))
        return carry


    def step(block, carry):
        for copy in copies(block):
            copy.wait()
        for c in range(NEEDLES):
            total = out[c]
            for k in range(deep):
                z = block * deep + k
                low, high = stage[c, z, :, span(0)], stage[c, z, :, span(1)]
                both = jnp.where(lane < HALO, low, high)
                moved = pltpu.roll(both, (8 * z + HALO) % LANES, 1)
                total = jnp.where(lane // 8 == z, moved, total)
            out[c] = total
        lax.fori_loop(block * deep, (block + 1) * deep, load, 0)
        return carry

    lax.fori_loop(0, blocks, step, 0)

    odd = lax.axis_index(axis_cd) % 2 == 1
    outer = lane % 8 < HALO
    needle_copy.wait()
    first[PAIRS] = needle_stage[...]
    second[PAIRS] = needle_stage[...]
    for c in range(PAIRS):
        here, other = out[c], out[min(c + PAIRS, NEEDLES - 1)]
        to_right = jnp.where(outer, here, pltpu.roll(other, HALO, 1))
        to_left = jnp.where(outer, pltpu.roll(other, LANES - HALO, 1), here)
        first[c] = jnp.where(odd, to_left, to_right)
        second[c] = jnp.where(odd, to_right, to_left)


def bulk_kernel(field, coef, base, uy, s1):
    layers = field.shape[1] - 2
    state = Field(field, None)

    def advance(z, carry):
        for tile in range(2):
            at = (z + 1, tile)
            m, damp = coefficients(coef, base, *at)
            wind = (coef[(UX,) + at], uy[at + (OWN,)], coef[(UZ,) + at])
            a = [state.own(c, z, tile) for c in range(5)]
            out = forward(a, m, damp, coef[(SPREAD,) + at], wind, state.around(z, tile))
            for c in range(5):
                s1[c, z + 1, tile, OWN] = out[c]
        return carry

    lax.fori_loop(0, layers, advance, 0)


def split_three(value):
    parts = []
    for _ in range(3):
        part = value.astype(jnp.bfloat16).astype(F32)
        parts.append(part)
        value = value - part
    return parts


def feet_block(ref, block, count):
    place = jnp.clip(block, 0, count - 1) * LANES
    row = ref[:, pl.ds(pl.multiple_of(place, LANES), LANES)]
    return jnp.where((block >= 0) & (block < count), row, 0)


def first_kernel(
    axis_md,
    axis_cd,
    own,
    needle,
    near_first,
    near_second,
    far_first,
    far_second,
    start,
    end,
    column,
    field,
    coef,
    uy,
    s1,
    gain,
    strip_s0,
    strip_coef,
    strip_base,
    strip_uy,
    strip_s1,
    strip_tgt,
    up,
    down,
    spread,
    cover,
    source,
):
    layers = field.shape[1] - 2
    height = own.shape[1]
    md = lax.axis_index(axis_md)
    count = lax.axis_size(axis_md)
    lane = lane_iota((height, LANES))
    outer = lane % 8 < HALO
    odd = lax.axis_index(axis_cd) % 2 == 1

    def from_left(c):
        return jnp.where(odd, near_second[c], near_first[c])

    def from_right(c):
        return jnp.where(odd, near_first[c], near_second[c])

    def half(take, c, turn):
        return take(c) if c < PAIRS else pltpu.roll(take(c - PAIRS), turn, 1)

    near = lane_iota((1, LANES)) < LANES // 2

    def feet(ref):
        far = jnp.where(near, feet_block(ref, md + 2, count), feet_block(ref, md - 2, count))
        blocks = [feet_block(ref, md + d, count) for d in (-1, 0, 1)]
        return jnp.concatenate(blocks + [far], axis=1)

    starts, ends, columns = feet(start), feet(end), feet(column)
    far = jnp.where((lane < LANES // 2) == odd, far_first[...], far_second[...])
    rates = jnp.concatenate(
        [from_left(PAIRS), needle[...], from_right(PAIRS), far], axis=1
    )
    needles = rates.shape[1]
    picked = jnp.where(row_iota((height, needles)) == columns, 1.0, 0.0)
    for part, value in enumerate(split_three(rates)):
        for z in range(layers):
            spread[part, z * height : (z + 1) * height] = (picked * value[z : z + 1]).astype(
                jnp.bfloat16
            )
    length = 2 * LANES
    cells = row_iota((length + LANES, needles))
    beyond = cells - length
    strip = jnp.where(beyond < 8, beyond - HALO, beyond - 8 + length - HALO)
    cells = jnp.where(cells < length, cells, strip) + md * length
    cover[...] = jnp.where((cells >= starts) & (cells < ends), 1.0, 0.0).astype(jnp.bfloat16)
    product = jnp.zeros((layers * height, length + LANES), F32)
    for part in range(3):
        product = product + lax.dot_general(
            spread[part], cover[...], (((1,), (1,)), ((), ())), preferred_element_type=F32
        )
    product = DT * product
    for tile in range(2):
        gain[1 : layers + 1, tile] = product[:, span(tile)].reshape(layers, height, LANES)
    source[...] = product[:, span(2)].reshape(source.shape)

    state = Field(field, strip_s0)
    state.clear_strips()
    has_left, has_right = md > 0, md < count - 1
    for side in range(2):

        def raw(c):
            if side == 0:
                return jnp.where(outer, jnp.where(has_left, half(from_left, c, LANES - HALO), 0.0), own[c])
            return jnp.where(outer, own[c], jnp.where(has_right, half(from_right, c, HALO), 0.0))

        for c in range(5):
            strip_s0[c, side, OWN] = raw(S0 + c)
            strip_tgt[c, side] = raw(TGT + c)
        u = [DT * raw(VEL + d) for d in range(3)]
        turn = DT * raw(ROT)
        for key, value in gradient_parts(lambda i: raw(GRAD + i)).items():
            strip_coef[PLACE[key], side] = value
        strip_coef[SPREAD, side] = 2.0 * turn
        strip_coef[UX, side] = u[0]
        strip_coef[UZ, side] = u[2]
        strip_uy[side, 0:8] = jnp.zeros((8, LANES), F32)
        strip_uy[side, 24:32] = jnp.zeros((8, LANES), F32)
        strip_uy[side, OWN] = u[1]
        damp = 6.0 * turn + (jnp.abs(u[0]) + jnp.abs(u[1]) + jnp.abs(u[2]))
        taken = jnp.zeros((height, LANES), F32)
        for z in range(layers):
            moved = pltpu.roll(source[z], (8 * z - 8 * side) % LANES, 1)
            taken = jnp.where(lane // 8 == z, moved, taken)
        strip_base[side] = damp + taken

    for side in range(2):
        m, damp = coefficients(strip_coef, strip_base, side)
        wind = (strip_coef[UX, side], strip_uy[side, OWN], strip_coef[UZ, side])
        a = [strip_s0[c, side, OWN] for c in range(5)]
        spin = strip_coef[SPREAD, side]
        out = forward(a, m, damp, spin, wind, state.strip_around(side))
        for c in range(5):
            strip_s1[c, side, OWN] = out[c]

    def put(side):
        def at(place):
            return line(None, side * 11 + place, 22, layers)

        for c in range(5):
            first, new = strip_s0.at[c, side], strip_s1.at[c, side]
            up[at(c)], down[at(c)] = first[23:24], first[8:9]
            up[at(5 + c)], down[at(5 + c)] = new[23:24], new[8:9]
        wind = strip_uy.at[side]
        up[at(10)] = -jnp.minimum(wind[23:24], 0.0)
        down[at(10)] = jnp.maximum(wind[8:9], 0.0)

    for message, row in ((up, 15), (down, 0)):
        for tile in range(2):
            u = row_of(coef, UX, tile, row)
            if tile == 0:
                weight, turn = jnp.where(lane == 0, jnp.maximum(u, 0.0), 0.0), 1
            else:
                weight = jnp.where(lane == LANES - 1, -jnp.minimum(u, 0.0), 0.0)
                turn = LANES - 1
            gained = row_of(gain, 0, tile, row)
            for c in range(5):
                left, right = (strip_s0[c, side, 8 + row : 9 + row] for side in (0, 1))
                edge = pltpu.roll(edge_column(left, right, layers), turn, 1)
                old = row_of(field, c, tile, 8 + row)
                new = row_of(s1, c, tile, 8 + row) - gained * old + weight * edge
                message[planes(tile * 11 + c, layers)] = old
                message[planes(tile * 11 + 5 + c, layers)] = new
            speed = row_of(uy, 0, tile, 8 + row)
            outward = -jnp.minimum(speed, 0.0) if row else jnp.maximum(speed, 0.0)
            message[planes(tile * 11 + 10, layers)] = outward
    for side in range(2):
        put(side)


def cd_flags(axis_cd):
    cd = lax.axis_index(axis_cd)
    return cd > 0, cd < lax.axis_size(axis_cd) - 1


def advance_kernel(
    s1_in,
    field,
    gain,
    coef,
    base_in,
    uy,
    tgt,
    strip_s0,
    strip_s1,
    strip_coef,
    strip_base,
    strip_uy,
    strip_tgt,
    s1,
    base,
    s2,
    goal,
    adj1,
    dots,
    adj2,
    strip_adj2,
    joint,
    joint1,
    joint2,
):
    layers, height = tgt.shape[1], tgt.shape[2]
    lane = lane_iota((height, LANES))
    start = Field(field, strip_s0, joint)
    state = Field(s1, strip_s1, joint1)
    delta = Field(adj2, strip_adj2, joint2)
    start.join()
    state.join()
    clear_planes(s1)
    clear_planes(adj2)
    for side in range(2):
        m, damp = coefficients(strip_coef, strip_base, side)
        wind = (strip_coef[UX, side], strip_uy[side, OWN], strip_coef[UZ, side])
        a = [strip_s1[c, side, OWN] for c in range(5)]
        spin = strip_coef[SPREAD, side]
        out = forward(a, m, damp, spin, wind, state.strip_around(side))
        for c in range(5):
            strip_adj2[c, side, OWN] = out[c] - strip_tgt[c, side]
    delta.join()

    def mend(z, carry):
        for tile in range(2):
            gained = gain[z + 1, tile]
            base[z + 1, tile] = base_in[z + 1, tile] + gained
            u = coef[UX, z + 1, tile]
            if tile == 0:
                weight, turn = jnp.where(lane == 0, jnp.maximum(u, 0.0), 0.0), 1
            else:
                weight, turn = jnp.where(lane == LANES - 1, -jnp.minimum(u, 0.0), 0.0), -1
            for c in range(5):
                edge = pltpu.roll(joint[c], (2 * LANES - HALO + turn - 8 * z) % LANES, 1)
                s1[c, z + 1, tile, OWN] = (
                    s1_in[c, z + 1, tile, OWN]
                    - gained * field[c, z + 1, tile, OWN]
                    + weight * edge
                )
        return carry

    lax.fori_loop(0, layers, mend, 0)

    def advance(z, carry):
        for tile in range(2):
            at = (z + 1, tile)
            m, damp = coefficients(coef, base, *at)
            wind = (coef[(UX,) + at], uy[at + (OWN,)], coef[(UZ,) + at])
            a = [state.own(c, z, tile) for c in range(5)]
            out = forward(a, m, damp, coef[(SPREAD,) + at], wind, state.around(z, tile))
            total = 0.0
            for c in range(5):
                wanted = tgt[c, z, :, span(tile)]
                miss = out[c] - wanted
                s2[(c,) + at] = out[c]
                goal[(c,) + at] = wanted
                adj2[(c,) + at + (OWN,)] = miss
                total = total + miss * a[c]
            dots[at] = total
        return carry

    lax.fori_loop(0, layers, advance, 0)
    edge_x = merged(strip_coef, UX, slice(None))

    def retreat(z, carry):
        for tile in range(2):
            m, damp = coefficients(coef, base, z + 1, tile)
            a = [state.own(c, z, tile) for c in range(5)]
            b = [delta.own(c, z, tile) for c in range(5)]
            wind = back_wind(coef, uy, edge_x, z, tile)
            out = backward(b, a, m, damp, wind, delta.around(z, tile))
            for c in range(5):
                adj1[c, z + 1, tile] = out[c]
        return carry

    lax.fori_loop(0, layers, retreat, 0)


def edge_kernel(
    axis_cd,
    s1,
    strip_s1_in,
    coef,
    base,
    uy,
    goal,
    strip_coef,
    strip_base,
    strip_uy,
    strip_tgt,
    own_up,
    own_down,
    from_below,
    from_above,
    s2_edge,
    adj2_edge,
    adj1_edge,
    dots_edge,
    strip_adj2,
    strip_adj1,
    up,
    down,
    strip_s1,
):
    layers = goal.shape[1] - 2
    has_below, has_above = cd_flags(axis_cd)

    state, delta = Field(s1, strip_s1), Field(s1, strip_adj2)
    delta.clear_strips()
    for side in range(2):

        def at(place):
            return line(None, side * 11 + place, 22, layers)

        wind = strip_uy.at[side]
        low_u, high_u = jnp.maximum(wind[8:9], 0.0), -jnp.minimum(wind[23:24], 0.0)
        low_n, high_n = from_below[at(10)], from_above[at(10)]
        for c in range(5):
            old, new = at(c), at(5 + c)
            ref = strip_s1.at[c, side]
            ref[OWN] = strip_s1_in[c, side, OWN]
            low = from_below[new] + low_n * own_down[old]
            high = from_above[new] + high_n * own_up[old]
            ref[7:8] = jnp.where(has_below, low, 0.0)
            ref[24:25] = jnp.where(has_above, high, 0.0)
            ref[8:9] = ref[8:9] + jnp.where(has_below, low_u * from_below[old], 0.0)
            ref[23:24] = ref[23:24] + jnp.where(has_above, high_u * from_above[old], 0.0)
    for side in range(2):
        m, damp = coefficients(strip_coef, strip_base, side)
        wind = (strip_coef[UX, side], strip_uy[side, OWN], strip_coef[UZ, side])
        a = [strip_s1[c, side, OWN] for c in range(5)]
        spin = strip_coef[SPREAD, side]
        out = forward(a, m, damp, spin, wind, state.strip_around(side))
        for c in range(5):
            strip_adj2[c, side, OWN] = out[c] - strip_tgt[c, side]
    for side in range(2):

        def at(place):
            return line(None, side * 10 + place, 20, layers)

        m, damp = coefficients(strip_coef, strip_base, side)
        a = [strip_s1[c, side, OWN] for c in range(5)]
        b = [strip_adj2[c, side, OWN] for c in range(5)]
        wind = strip_back_wind(strip_coef, strip_uy, side)
        out = backward(b, a, m, damp, wind, delta.strip_around(side))
        high = -jnp.minimum(strip_uy[side, 23:24], 0.0)
        low = jnp.maximum(strip_uy[side, 8:9], 0.0)
        for c in range(5):
            strip_adj1[c, side, OWN] = out[c]
            up[at(c)] = high * b[c][-1:]
            down[at(c)] = low * b[c][:1]
            up[at(5 + c)] = high * out[c][-1:]
            down[at(5 + c)] = low * out[c][:1]

    def constants(tile, row):
        m = {key: row_of(coef, place, tile, row) for key, place in PLACE.items()}
        return m, row_of(base, 0, tile, row)

    for number, (message, mine, valid, outgoing) in enumerate(
        ((from_below, own_down, has_below, down), (from_above, own_up, has_above, up))
    ):
        rows = (0, 1, 2) if number == 0 else (15, 14, 13)
        sides = (0, 1)

        def plane(ref, place, tile):
            return ref[planes(tile * 11 + place, layers)]

        lines = [{}, {}, {}, {}]
        for c in range(5):
            for tile in range(2):
                old, new = plane(message, c, tile), plane(message, 5 + c, tile)
                weight = plane(message, 10, tile)
                lines[0][c, tile] = jnp.where(
                    valid, new + weight * plane(mine, c, tile), 0.0
                )
                lines[1][c, tile] = plane(mine, 5 + c, tile) + jnp.where(
                    valid, plane(mine, 10, tile) * old, 0.0
                )
                for k in (1, 2):
                    lines[k + 1][c, tile] = row_of(s1, c, tile, 8 + rows[k])

        def strip_edge(ref, c, row):
            left, right = (ref[c, side, 8 + row : 9 + row] for side in sides)
            return edge_column(left, right, layers)

        def ordered(outer, inner):
            return (outer, inner) if number == 0 else (inner, outer)

        misses = [{}, {}]
        for k in range(2):
            row = rows[k]
            edges = [strip_edge(strip_s1, c, row) for c in range(5)]
            for tile in range(2):
                m, damp = constants(tile, row)
                wind = (
                    row_of(coef, UX, tile, row),
                    row_of(uy, 0, tile, 8 + row),
                    row_of(coef, UZ, tile, row),
                )
                a = [lines[k + 1][c, tile] for c in range(5)]

                def around(c):
                    tiles = [lines[k + 1][c, t] for t in range(2)]
                    return (
                        x_pair(tiles, tile, edges[c]),
                        ordered(lines[k][c, tile], lines[k + 2][c, tile]),
                        layer_pair(a[c]),
                    )

                out = forward(a, m, damp, row_of(coef, SPREAD, tile, row), wind, around)
                total = 0.0
                for c in range(5):
                    miss = out[c] - row_of(goal, c, tile, row)
                    s2_edge[c, 2 * number + k, tile] = out[c]
                    adj2_edge[c, 2 * number + k, tile] = miss
                    misses[k][c, tile] = miss
                    total = total + miss * a[c]
                dots_edge[2 * number + k, tile] = total

        row = rows[0]
        edges = [strip_edge(strip_adj2, c, row) for c in range(5)]
        left, right = (strip_coef[UX, side, row : row + 1] for side in sides)
        edge_x = edge_column(left, right, layers)
        for tile in range(2):
            m, damp = constants(tile, row)
            a = [lines[1][c, tile] for c in range(5)]
            b = [misses[0][c, tile] for c in range(5)]
            zero = jnp.zeros_like(b[0])
            wind = (
                x_pair([row_of(coef, UX, t, row) for t in range(2)], tile, edge_x),
                ordered(zero, row_of(uy, 0, tile, 8 + rows[1])),
                layer_pair(row_of(coef, UZ, tile, row)),
            )

            def around(c):
                tiles = [misses[0][c, t] for t in range(2)]
                return (
                    x_pair(tiles, tile, edges[c]),
                    ordered(zero, misses[1][c, tile]),
                    layer_pair(b[c]),
                )

            out = backward(b, a, m, damp, wind, around)
            weight = plane(mine, 10, tile)
            for c in range(5):
                outgoing[planes(tile * 10 + c, layers)] = weight * b[c]
                outgoing[planes(tile * 10 + 5 + c, layers)] = weight * out[c]
                adj1_edge[c, number, tile] = out[c]


def needle_feet(ref, md, count):
    return jnp.concatenate([feet_block(ref, md + d, count) for d in (-1, 0, 1)], axis=1)


def own_cover(md, length, starts, ends):
    cells = row_iota((length, starts.shape[1])) + md * length
    return jnp.where((cells >= starts) & (cells < ends), 1.0, 0.0).astype(jnp.bfloat16)


def covered_sum(values, cover):
    product = jnp.zeros((values.shape[0], cover.shape[1]), F32)
    for part in split_three(values):
        product = product + jnp.dot(
            part.astype(jnp.bfloat16), cover, preferred_element_type=F32
        )
    return product


def second_kernel(
    axis_md,
    s1,
    s2_in,
    goal,
    adj1_in,
    dots_in,
    s2_edge,
    adj2_edge,
    adj1_edge,
    dots_edge,
    field,
    coef,
    base,
    uy,
    strip_coef,
    strip_adj2,
    strip_adj1,
    start,
    end,
    column,
    s2_out,
    adj0,
    gained,
    adj1,
    dots,
    sens,
    s2,
    joint,
):
    layers, height = goal.shape[1] - 2, goal.shape[3]
    length = 2 * LANES
    md = lax.axis_index(axis_md)
    count = lax.axis_size(axis_md)

    def gather(z, carry):
        for tile in range(2):
            dots[z + 1, tile] = dots_in[z + 1, tile]
            for c in range(5):
                s2[c, z + 1, tile] = s2_in[c, z + 1, tile]
                adj1[c, z + 1, tile, OWN] = adj1_in[c, z + 1, tile]
        return carry

    lax.fori_loop(0, layers, gather, 0)
    for tile in range(2):
        for number, row in enumerate((0, 1, 15, 14)):
            set_row(dots, 0, tile, row, dots_edge[number, tile])
            for c in range(5):
                set_row(s2, c, tile, row, s2_edge[c, number, tile])
        for number, row in enumerate((0, 15)):
            for c in range(5):
                set_row(adj1, c, tile, 8 + row, adj1_edge[c, number, tile])

    for number, rows in enumerate(((0, 1, 2, 3), (15, 14, 13, 12))):
        lines = [{}, {}, {}, {}]
        for c in range(5):
            for tile in range(2):
                for k in (0, 1):
                    lines[k][c, tile] = adj2_edge[c, 2 * number + k, tile]
                for k in (2, 3):
                    state = row_of(s2_in, c, tile, rows[k])
                    lines[k][c, tile] = state - row_of(goal, c, tile, rows[k])

        def ordered(outer, inner):
            return (outer, inner) if number == 0 else (inner, outer)

        for k in (1, 2):
            row = rows[k]
            edges = []
            for c in range(5):
                left, right = (strip_adj2[c, side, 8 + row : 9 + row] for side in (0, 1))
                edges.append(edge_column(left, right, layers))
            left, right = (strip_coef[UX, side, row : row + 1] for side in (0, 1))
            edge = edge_column(left, right, layers)
            for tile in range(2):
                m = {key: row_of(coef, place, tile, row) for key, place in PLACE.items()}
                damp = row_of(base, 0, tile, row)
                a = [row_of(s1, c, tile, 8 + row) for c in range(5)]
                b = [lines[k][c, tile] for c in range(5)]
                wind = (
                    x_pair([row_of(coef, UX, t, row) for t in range(2)], tile, edge),
                    ordered(*(row_of(uy, 0, tile, 8 + rows[i]) for i in (k - 1, k + 1))),
                    layer_pair(row_of(coef, UZ, tile, row)),
                )

                def around(c):
                    return (
                        x_pair([lines[k][c, t] for t in range(2)], tile, edges[c]),
                        ordered(lines[k - 1][c, tile], lines[k + 1][c, tile]),
                        layer_pair(b[c]),
                    )

                out = backward(b, a, m, damp, wind, around)
                for c in range(5):
                    set_row(adj1, c, tile, 8 + row, out[c])

    def write(z, carry):
        for tile in range(2):
            for c in range(5):
                s2_out[c, z, :, span(tile)] = s2[c, z + 1, tile]
        return carry

    lax.fori_loop(0, layers, write, 0)
    edge_x = merged(strip_coef, UX, slice(None))
    last_delta = Field(adj1, strip_adj1, joint)
    last_delta.clear()
    last_delta.join()

    def finish(z, carry):
        for tile in range(2):
            m, damp = coefficients(coef, base, z + 1, tile)
            a = [field[c, z + 1, tile, OWN] for c in range(5)]
            b = [last_delta.own(c, z, tile) for c in range(5)]
            wind = back_wind(coef, uy, edge_x, z, tile)
            out = backward(b, a, m, damp, wind, last_delta.around(z, tile))
            total = dots[z + 1, tile]
            for c in range(5):
                adj0[c, z + 1, tile] = out[c]
                total = total + a[c] * b[c]
            sens[z, :, span(tile)] = -DT * total
        return carry

    lax.fori_loop(0, layers, finish, 0)
    starts, ends, columns = (needle_feet(ref, md, count) for ref in (start, end, column))
    cover = own_cover(md, length, starts, ends)
    product = covered_sum(sens[...].reshape(layers * height, length), cover)
    picked = jnp.where(row_iota((height, starts.shape[1])) == columns, 1.0, 0.0)
    for z in range(layers):
        gained[z : z + 1] = jnp.sum(
            product[z * height : (z + 1) * height] * picked, axis=0, keepdims=True
        )


def third_kernel(
    axis_md,
    axis_cd,
    gained,
    field,
    from_below,
    from_above,
    start,
    end,
    column,
    first,
    kept,
    second,
):
    layers = field.shape[1] - 2
    length = 2 * LANES
    md = lax.axis_index(axis_md)
    count = lax.axis_size(axis_md)
    odd = lax.axis_index(axis_cd) % 2 == 1
    lines = []
    for message, valid, row in zip((from_below, from_above), cd_flags(axis_cd), (8, 23)):
        parts = []
        for tile in range(2):
            total = 0.0
            for c in range(5):
                brought = message[planes(tile * 10 + c, layers)]
                total = total + brought * row_of(field, c, tile, row)
            parts.append(jnp.where(valid, -DT * total, 0.0))
        lines.append(jnp.concatenate(parts, axis=1))
    starts, ends, columns = (needle_feet(ref, md, count) for ref in (start, end, column))
    cover = own_cover(md, length, starts, ends)
    product = covered_sum(jnp.concatenate(lines, axis=0), cover)
    total = gained[...]
    for number, row in enumerate((0, 15)):
        here = product[number * layers : (number + 1) * layers]
        total = total + jnp.where(columns == row, here, 0.0)
    first[...] = jnp.where(odd, total[:, span(0)], total[:, span(2)])
    kept[...] = total[:, span(1)]
    second[...] = jnp.where(odd, total[:, span(2)], total[:, span(0)])


def fourth_kernel(
    axis_cd,
    adj0_in,
    field,
    coef,
    base,
    uy,
    strip_coef,
    weights_below,
    weights_above,
    own_up,
    own_down,
    from_below,
    from_above,
    out_field,
    adj0,
):
    layers = field.shape[1] - 2
    has_below, has_above = cd_flags(axis_cd)

    def gather(z, carry):
        for tile in range(2):
            for c in range(5):
                adj0[c, z + 1, tile] = adj0_in[c, z + 1, tile]
        return carry

    lax.fori_loop(0, layers, gather, 0)

    for number, (weights, message, mine, valid) in enumerate(
        (
            (weights_below, from_below, own_down, has_below),
            (weights_above, from_above, own_up, has_above),
        )
    ):
        row, inner = ((0, 1), (15, 14))[number]
        brought = {}
        for c in range(5):
            for tile in range(2):
                value = message[planes(tile * 10 + c, layers)]
                brought[c, tile] = jnp.where(valid, value, 0.0)
        edges = []
        for c in range(5):
            left, right = (message[line(None, side * 10 + c, 20, layers)] for side in (0, 1))
            edges.append(jnp.where(valid, edge_column(left, right, layers), 0.0))
        left, right = (strip_coef[UX, side, row : row + 1] for side in (0, 1))
        edge_x = edge_column(left, right, layers)
        for tile in range(2):
            m = {key: row_of(coef, place, tile, row) for key, place in PLACE.items()}
            damp = row_of(base, 0, tile, row)
            a = [row_of(field, c, tile, 8 + row) for c in range(5)]
            b = [brought[c, tile] for c in range(5)]
            wind = (
                x_pair([row_of(coef, UX, t, row) for t in range(2)], tile, edge_x),
                layer_pair(row_of(coef, UZ, tile, row)),
            )

            def around(c):
                tiles = [brought[c, t] for t in range(2)]
                return x_pair(tiles, tile, edges[c]), layer_pair(b[c])

            out = backward(b, a, m, damp, wind, around)
            speed = row_of(uy, 0, tile, 8 + row)
            inward = -jnp.minimum(speed, 0.0) if number == 0 else jnp.maximum(speed, 0.0)
            weight = weights[planes(tile * 11 + 10, layers)]
            for c in range(5):
                own = mine[planes(tile * 10 + c, layers)]
                far = message[planes(tile * 10 + 5 + c, layers)] + weight * own
                total = out[c] + jnp.where(valid, far, 0.0)
                set_row(adj0, c, tile, row, row_of(adj0, c, tile, row) + total)
                more = inward * b[c]
                set_row(adj0, c, tile, inner, row_of(adj0, c, tile, inner) + more)

    def scatter(z, carry):
        for tile in range(2):
            for c in range(5):
                out_field[c, z, :, span(tile)] = adj0[c, z + 1, tile]
        return carry

    lax.fori_loop(0, layers, scatter, 0)


def ring(value, axis, steps):
    count = lax.axis_size(axis)
    return lax.ppermute(value, axis, [(i, (i + steps) % count) for i in range(count)])


def winding(value, steps, turn):
    rows, columns = lax.axis_size("md"), lax.axis_size("cd")
    pairs = []
    for column in range(columns):
        for row in range(rows):
            target = row + (steps if column % 2 == turn else -steps)
            if 0 <= target < rows:
                pairs.append((row * columns + column, target * columns + column))
            else:
                pairs.append((row * columns + column, row * columns + (column ^ 1)))
    return lax.ppermute(value, ("md", "cd"), pairs)


def both_ways(value, steps):
    return winding(value, steps, 0), winding(value, steps, 1)


def shape_of(*dims, dtype=F32):
    return jax.ShapeDtypeStruct(dims, dtype)


def scratch(*dims, dtype=F32):
    return pltpu.VMEM(dims, dtype)


def cost(microseconds):
    return pl.CostEstimate(
        flops=int(microseconds * 1e6), bytes_accessed=int(microseconds * 3e6), transcendentals=0
    )


def params(mebibytes):
    return pltpu.CompilerParams(vmem_limit_bytes=mebibytes * 1024 * 1024)


def local(orientation, velocity, velocity_grad, rotary, target, needle_params, *feet):
    _, layers, height, length = orientation.shape
    rotary = rotary[None]
    rates = jnp.transpose(needle_params[:, 0, :])
    feet = [foot.reshape(1, -1) for foot in feet]
    padded = (layers + 2, 2, ROWS, LANES)
    plain = (layers + 2, 2, height, LANES)
    strip_padded, strip = (2, ROWS, LANES), (2, height, LANES)
    message, back_message = shape_of(22 * layers + 24, LANES), shape_of(20 * layers + 24, LANES)
    joint = scratch(5, height, LANES)

    hbm = pl.BlockSpec(memory_space=pltpu.HBM)
    blocks = 4
    packed, first, second, field, coef, base, uy = pl.pallas_call(
        functools.partial(pack_kernel, "cd"),
        in_specs=[hbm] * 6,
        out_shape=[
            shape_of(NEEDLES, height, LANES),
            shape_of(PAIRS + 1, height, LANES),
            shape_of(PAIRS + 1, height, LANES),
            shape_of(5, *padded),
            shape_of(COEFS, *plain),
            shape_of(*plain),
            shape_of(*padded),
        ],
        scratch_shapes=[
            scratch(NEEDLES, layers, height, length),
            scratch(*rates.shape),
            pltpu.SemaphoreType.DMA((blocks, 5)),
            pltpu.SemaphoreType.DMA,
        ],
        compiler_params=params(20),
        cost_estimate=cost(4),
    )(
        *(
            pltpu.with_memory_space_constraint(field, pltpu.HBM)
            for field in (orientation, velocity, velocity_grad, rotary, target, rates)
        )
    )
    far = both_ways(rates, 2)
    near = winding(first, 1, 0), winding(second, 1, 1)

    s1 = pl.pallas_call(
        bulk_kernel,
        out_shape=shape_of(5, *padded),
        compiler_params=params(16),
        cost_estimate=cost(2),
    )(field, coef, base, uy)

    gain, strip_s0, strip_coef, strip_base, strip_uy, strip_s1, strip_tgt, up, down = (
        pl.pallas_call(
            functools.partial(first_kernel, "md", "cd"),
            out_shape=[
                shape_of(*plain),
                shape_of(5, *strip_padded),
                shape_of(COEFS, *strip),
                shape_of(*strip),
                shape_of(*strip_padded),
                shape_of(5, *strip_padded),
                shape_of(5, *strip),
                message,
                message,
            ],
            scratch_shapes=[
                scratch(3, layers * height, 4 * LANES, dtype=jnp.bfloat16),
                scratch(length + LANES, 4 * LANES, dtype=jnp.bfloat16),
                scratch(layers, height, LANES),
            ],
            compiler_params=params(24),
            cost_estimate=cost(3),
        )(packed, rates, *near, *far, *feet, field, coef, uy, s1)
    )
    below = ring(up, "cd", 1)
    above = ring(down, "cd", -1)

    s1, base, s2_part, goal, adj1_part, dots = pl.pallas_call(
        advance_kernel,
        out_shape=[
            shape_of(5, *padded),
            shape_of(*plain),
            shape_of(5, *plain),
            shape_of(5, *plain),
            shape_of(5, *plain),
            shape_of(*plain),
        ],
        scratch_shapes=[scratch(5, *padded), scratch(5, *strip_padded), joint, joint, joint],
        compiler_params=params(16),
        cost_estimate=cost(8),
    )(
        s1,
        field,
        gain,
        coef,
        base,
        uy,
        target,
        strip_s0,
        strip_s1,
        strip_coef,
        strip_base,
        strip_uy,
        strip_tgt,
    )
    edge_row = (2, layers, LANES)
    s2_edge, adj2_edge, adj1_edge, dots_edge, strip_adj2, strip_adj1, back_up, back_down = (
        pl.pallas_call(
            functools.partial(edge_kernel, "cd"),
            out_shape=[
                shape_of(5, 4, *edge_row),
                shape_of(5, 4, *edge_row),
                shape_of(5, 2, *edge_row),
                shape_of(4, *edge_row),
                shape_of(5, *strip_padded),
                shape_of(5, *strip_padded),
                back_message,
                back_message,
            ],
            scratch_shapes=[scratch(5, *strip_padded)],
            compiler_params=params(16),
            cost_estimate=cost(2),
        )(
            s1,
            strip_s1,
            coef,
            base,
            uy,
            goal,
            strip_coef,
            strip_base,
            strip_uy,
            strip_tgt,
            up,
            down,
            below,
            above,
        )
    )
    back_below = ring(back_up, "cd", 1)
    back_above = ring(back_down, "cd", -1)

    part = shape_of(*rates.shape)
    s2, adj0_part, gained = pl.pallas_call(
        functools.partial(second_kernel, "md"),
        out_shape=[
            shape_of(*orientation.shape),
            shape_of(5, *plain),
            shape_of(layers, 3 * LANES),
        ],
        scratch_shapes=[
            scratch(5, *padded),
            scratch(*plain),
            scratch(layers, height, length),
            scratch(5, *plain),
            joint,
        ],
        compiler_params=params(24),
        cost_estimate=cost(6),
    )(
        s1,
        s2_part,
        goal,
        adj1_part,
        dots,
        s2_edge,
        adj2_edge,
        adj1_edge,
        dots_edge,
        field,
        coef,
        base,
        uy,
        strip_coef,
        strip_adj2,
        strip_adj1,
        *feet,
    )

    part_first, part_own, part_second = pl.pallas_call(
        functools.partial(third_kernel, "md", "cd"),
        out_shape=[part, part, part],
        compiler_params=params(16),
        cost_estimate=cost(1),
    )(gained, field, back_below, back_above, *feet)
    part_first = winding(part_first, 1, 0)
    part_second = winding(part_second, 1, 1)

    adj0 = pl.pallas_call(
        functools.partial(fourth_kernel, "cd"),
        out_shape=shape_of(*orientation.shape),
        scratch_shapes=[scratch(5, *plain)],
        compiler_params=params(16),
        cost_estimate=cost(2),
    )(
        adj0_part,
        field,
        coef,
        base,
        uy,
        strip_coef,
        below,
        above,
        back_up,
        back_down,
        back_below,
        back_above,
    )
    gradient = part_own + part_first + part_second
    return s2, adj0, jnp.transpose(gradient)[:, None, :]


def solution(mesh):
    field = P(None, None, "cd", "md")
    feet = P(None, "cd")
    needles = P("md", "cd", None)
    return jax.shard_map(
        local,
        mesh=mesh,
        in_specs=(field, field, field, P(None, "cd", "md"), field, needles, feet, feet, feet),
        out_specs=(field, field, needles),
        check_vma=False,
    )
```

```python
import functools

import jax
import jax.numpy as jnp
from jax import lax
from jax.experimental import pallas as pl
from jax.experimental.pallas import tpu as pltpu
from jax.sharding import PartitionSpec as P

XI = 0.95
DT = 0.1
LANES = 128
F32 = jnp.float32
HALO = 4
S0, VEL, GRAD, ROT, TGT, NEEDLES = 0, 5, 8, 17, 18, 23
PAIRS = 12
PLACE = {(0, 0): 0, (1, 1): 1, (0, 1): 2, (1, 0): 3, (0, 2): 4, (2, 0): 5, (1, 2): 6, (2, 1): 7}
SPREAD, UX, UZ, COEFS = 8, 9, 10, 11
ROWS = 32
OWN, BEHIND, FRONT = slice(8, 24), slice(7, 23), slice(9, 25)


def lane_iota(shape):
    return lax.broadcasted_iota(jnp.int32, shape, len(shape) - 1)


def row_iota(shape):
    return lax.broadcasted_iota(jnp.int32, shape, len(shape) - 2)


def span(tile):
    return slice(tile * LANES, (tile + 1) * LANES)


def gradient_parts(read):
    g = [read(i) for i in range(9)]
    low = 0.5 * (XI - 1.0) * DT
    m = {}
    for i, j in ((0, 1), (0, 2), (1, 2)):
        a, b = g[3 * i + j], g[3 * j + i]
        both = low * (a + b)
        m[i, j] = DT * a + both
        m[j, i] = DT * b + both
    m[0, 0] = (XI * DT) * (g[0] - g[8])
    m[1, 1] = (XI * DT) * (g[4] - g[8])
    return m


def forward(a, m, base, spread, wind, around):
    a11, a22, a12, a13, a23 = a
    a33 = 1.0 - a11 - a22
    n00 = m[0, 0] * a11 + m[0, 1] * a12 + m[0, 2] * a13
    n01 = m[0, 0] * a12 + m[0, 1] * a22 + m[0, 2] * a23
    n02 = m[0, 0] * a13 + m[0, 1] * a23 + m[0, 2] * a33
    n10 = m[1, 0] * a11 + m[1, 1] * a12 + m[1, 2] * a13
    n11 = m[1, 0] * a12 + m[1, 1] * a22 + m[1, 2] * a23
    n12 = m[1, 0] * a13 + m[1, 1] * a23 + m[1, 2] * a33
    n20 = m[2, 0] * a11 + m[2, 1] * a12
    n21 = m[2, 0] * a12 + m[2, 1] * a22
    n22 = m[2, 0] * a13 + m[2, 1] * a23
    keep = 1.0 - (base + 2.0 * (n00 + n11 + n22))
    gain = (2.0 * n00 + spread, 2.0 * n11 + spread, n01 + n10, n02 + n20, n12 + n21)
    out = []
    for c in range(5):
        total = gain[c] + keep * a[c]
        for u, (behind, front) in zip(wind, around(c)):
            total = total + jnp.abs(u) * jnp.where(u > 0.0, behind, front)
        out.append(total)
    return out


def backward(b, a, m, base, wind, around):
    b1, b2, b3, b4, b5 = b
    a11, a22, a12, a13, a23 = a
    g = -2.0 * (b1 * a11 + b2 * a22 + b3 * a12 + b4 * a13 + b5 * a23)
    trace = (
        m[0, 0] * a11
        + m[1, 1] * a22
        + (m[0, 1] + m[1, 0]) * a12
        + (m[0, 2] + m[2, 0]) * a13
        + (m[1, 2] + m[2, 1]) * a23
    )
    s00, s11, s22 = 2.0 * b1 + g, 2.0 * b2 + g, g
    h00 = m[0, 0] * s00 + m[1, 0] * b3 + m[2, 0] * b4
    h01 = m[0, 0] * b3 + m[1, 0] * s11 + m[2, 0] * b5
    h02 = m[0, 0] * b4 + m[1, 0] * b5 + m[2, 0] * s22
    h10 = m[0, 1] * s00 + m[1, 1] * b3 + m[2, 1] * b4
    h11 = m[0, 1] * b3 + m[1, 1] * s11 + m[2, 1] * b5
    h12 = m[0, 1] * b4 + m[1, 1] * b5 + m[2, 1] * s22
    h20 = m[0, 2] * s00 + m[1, 2] * b3
    h21 = m[0, 2] * b3 + m[1, 2] * s11
    h22 = m[0, 2] * b4 + m[1, 2] * b5
    keep = 1.0 - (base + 2.0 * trace)
    gain = (h00 - h22, h11 - h22, h01 + h10, h02 + h20, h12 + h21)
    weights = [(jnp.minimum(w, 0.0), jnp.maximum(f, 0.0)) for w, f in wind]
    out = []
    for c in range(5):
        total = gain[c] + keep * b[c]
        for (low, high), (behind, front) in zip(weights, around(c)):
            total = total + (high * front - low * behind)
        out.append(total)
    return out


def merged(strips, c, rows):
    left, right = strips[c, 0, rows], strips[c, 1, rows]
    return jnp.where(lane_iota(left.shape) % 8 < HALO, left, right)


def edge_tile(joint, z):
    return pltpu.roll(joint, (2 * LANES - HALO - 8 * z) % LANES, 1)


def x_pair(tiles, tile, edge):
    cur = tiles[tile]
    prev, after = (edge, tiles[1]) if tile == 0 else (tiles[0], edge)
    lane = lane_iota(cur.shape)
    behind = pltpu.roll(jnp.where(lane == LANES - 1, prev, cur), 1, 1)
    front = pltpu.roll(jnp.where(lane == 0, after, cur), LANES - 1, 1)
    return behind, front


def strip_x(cur):
    return pltpu.roll(cur, 1, 1), pltpu.roll(cur, LANES - 1, 1)


def strip_z(cur):
    lane = lane_iota(cur.shape)
    behind = jnp.where(lane < 8, 0.0, pltpu.roll(cur, 8, 1))
    front = jnp.where(lane >= LANES - 8, 0.0, pltpu.roll(cur, LANES - 8, 1))
    return behind, front


def coefficients(coef, base, *at):
    m = {key: coef[(place,) + at] for key, place in PLACE.items()}
    return m, base[at]


class Field:
    def __init__(self, ref, strips, joint=None):
        self.ref, self.strips, self.joint = ref, strips, joint

    def join(self):
        for c in range(self.ref.shape[0]):
            self.joint[c] = merged(self.strips, c, OWN)

    def own(self, c, z, tile):
        return self.ref[c, z + 1, tile, OWN]

    def around(self, z, tile):
        def pairs(c):
            ref = self.ref
            tiles = [ref[c, z + 1, t, OWN] for t in range(2)]
            if self.joint is None:
                edge = jnp.zeros_like(tiles[0])
            else:
                edge = edge_tile(self.joint[c], z)
            return (
                x_pair(tiles, tile, edge),
                (ref[c, z + 1, tile, BEHIND], ref[c, z + 1, tile, FRONT]),
                (ref[c, z, tile, OWN], ref[c, z + 2, tile, OWN]),
            )

        return pairs

    def strip_around(self, side):
        def pairs(c):
            cur = self.strips[c, side, OWN]
            return (
                strip_x(cur),
                (self.strips[c, side, BEHIND], self.strips[c, side, FRONT]),
                strip_z(cur),
            )

        return pairs

    def clear(self):
        last = self.ref.shape[1] - 1
        zero = jnp.zeros((8, LANES), F32)
        clear_planes(self.ref)

        def layer(z, carry):
            for c in range(self.ref.shape[0]):
                for tile in range(2):
                    self.ref[c, z, tile, 0:8] = zero
                    self.ref[c, z, tile, 24:32] = zero
            return carry

        lax.fori_loop(1, last, layer, 0)

    def clear_strips(self):
        zero = jnp.zeros((8, LANES), F32)
        for c in range(self.strips.shape[0]):
            for side in range(2):
                self.strips[c, side, 0:8] = zero
                self.strips[c, side, 24:32] = zero


def clear_planes(ref, planes=None):
    last = ref.shape[1] - 1
    for c in planes or range(ref.shape[0]):
        for tile in range(2):
            for z in (0, last):
                ref[c, z, tile] = jnp.zeros(ref.shape[3:], F32)


def line(z, place, count, layers):
    if z is None:
        return slice(count * layers + place, count * layers + place + 1)
    return pl.ds(place * layers + z, 1)


def planes(place, layers):
    return slice(place * layers, (place + 1) * layers)


def row_place(ref, c, tile, row):
    high, rows = ref.shape[-4], ref.shape[-2]
    total = 1
    for size in ref.shape[:-1]:
        total *= size
    at = ((c * high + 1) * 2 + tile) * rows + row
    return ref.reshape(total, LANES), pl.ds(at, high - 2, stride=2 * rows)


def row_of(ref, c, tile, row):
    flat, place = row_place(ref, c, tile, row)
    return flat[place, :]


def set_row(ref, c, tile, row, value):
    flat, place = row_place(ref, c, tile, row)
    flat[place, :] = value


def layer_pair(cur):
    row, last = row_iota(cur.shape), cur.shape[0] - 1
    behind = jnp.where(row == 0, 0.0, pltpu.roll(cur, 1, 0))
    front = jnp.where(row == last, 0.0, pltpu.roll(cur, last, 0))
    return behind, front


def edge_column(left, right, layers):
    shape = (layers, LANES)
    lane, layer = lane_iota(shape), row_iota(shape)
    low = jnp.sum(jnp.where(lane == 8 * layer + HALO - 1, left, 0.0), axis=1, keepdims=True)
    high = jnp.sum(jnp.where(lane == 8 * layer + HALO, right, 0.0), axis=1, keepdims=True)
    return jnp.where(lane == LANES - 1, low, jnp.where(lane == 0, high, 0.0))


def back_wind(coef, uy, edge_x, z, tile):
    tiles = [coef[UX, z + 1, t] for t in range(2)]
    return (
        x_pair(tiles, tile, edge_tile(edge_x, z)),
        (uy[z + 1, tile, BEHIND], uy[z + 1, tile, FRONT]),
        (coef[UZ, z, tile], coef[UZ, z + 2, tile]),
    )


def strip_back_wind(coef, uy, side):
    return (
        strip_x(coef[UX, side]),
        (uy[side, BEHIND], uy[side, FRONT]),
        strip_z(coef[UZ, side]),
    )


def pack_kernel(
    axis_cd,
    s0,
    vel,
    grad,
    rot,
    tgt,
    needle,
    out,
    first,
    second,
    field,
    coef,
    base,
    uy,
    stage,
    needle_stage,
    sems,
    needle_sem,
):
    layers = stage.shape[1]
    blocks = sems.shape[0]
    deep = layers // blocks
    sources = (s0, vel, grad, rot, tgt)

    def copies(block):
        slot, found = 0, []
        for number, ref in enumerate(sources):
            depth = pl.ds(block * deep, deep)
            target = stage.at[pl.ds(slot, ref.shape[0]), depth]
            found.append(
                pltpu.make_async_copy(ref.at[:, depth], target, sems.at[block, number])
            )
            slot += ref.shape[0]
        return found

    for block in range(blocks):
        for copy in copies(block):
            copy.start()
    needle_copy = pltpu.make_async_copy(needle, needle_stage, needle_sem)
    needle_copy.start()
    lane = lane_iota(out.shape[1:])
    Field(field, None).clear()
    clear_planes(coef, [UZ])

    def load(z, carry):
        zero = jnp.zeros((8, LANES), F32)
        for tile in range(2):
            for c in range(5):
                field[c, z + 1, tile, OWN] = stage[c, z, :, span(tile)]
            u = [DT * stage[VEL + d, z, :, span(tile)] for d in range(3)]
            turn = DT * stage[ROT, z, :, span(tile)]
            parts = gradient_parts(lambda i: stage[GRAD + i, z, :, span(tile)])
            for key, value in parts.items():
                coef[PLACE[key], z + 1, tile] = value
            coef[SPREAD, z + 1, tile] = 2.0 * turn
            coef[UX, z + 1, tile] = u[0]
            coef[UZ, z + 1, tile] = u[2]
            uy[z + 1, tile, 0:8] = zero
            uy[z + 1, tile, 24:32] = zero
            uy[z + 1, tile, OWN] = u[1]
            base[z + 1, tile] = 6.0 * turn + (jnp.abs(u[0]) + jnp.abs(u[1]) + jnp.abs(u[2]))
        return carry


    def step(block, carry):
        for copy in copies(block):
            copy.wait()
        for c in range(NEEDLES):
            total = out[c]
            for k in range(deep):
                z = block * deep + k
                low, high = stage[c, z, :, span(0)], stage[c, z, :, span(1)]
                both = jnp.where(lane < HALO, low, high)
                moved = pltpu.roll(both, (8 * z + HALO) % LANES, 1)
                total = jnp.where(lane // 8 == z, moved, total)
            out[c] = total
        lax.fori_loop(block * deep, (block + 1) * deep, load, 0)
        return carry

    lax.fori_loop(0, blocks, step, 0)

    odd = lax.axis_index(axis_cd) % 2 == 1
    outer = lane % 8 < HALO
    needle_copy.wait()
    first[PAIRS] = needle_stage[...]
    second[PAIRS] = needle_stage[...]
    for c in range(PAIRS):
        here, other = out[c], out[min(c + PAIRS, NEEDLES - 1)]
        to_right = jnp.where(outer, here, pltpu.roll(other, HALO, 1))
        to_left = jnp.where(outer, pltpu.roll(other, LANES - HALO, 1), here)
        first[c] = jnp.where(odd, to_left, to_right)
        second[c] = jnp.where(odd, to_right, to_left)


def bulk_kernel(field, coef, base, uy, s1):
    layers = field.shape[1] - 2
    state = Field(field, None)

    def advance(z, carry):
        for tile in range(2):
            at = (z + 1, tile)
            m, damp = coefficients(coef, base, *at)
            wind = (coef[(UX,) + at], uy[at + (OWN,)], coef[(UZ,) + at])
            a = [state.own(c, z, tile) for c in range(5)]
            out = forward(a, m, damp, coef[(SPREAD,) + at], wind, state.around(z, tile))
            for c in range(5):
                s1[c, z + 1, tile, OWN] = out[c]
        return carry

    lax.fori_loop(0, layers, advance, 0, unroll=2)


def split_three(value):
    parts = []
    for _ in range(3):
        part = value.astype(jnp.bfloat16).astype(F32)
        parts.append(part)
        value = value - part
    return parts


def feet_block(ref, block, count):
    place = jnp.clip(block, 0, count - 1) * LANES
    row = ref[:, pl.ds(pl.multiple_of(place, LANES), LANES)]
    return jnp.where((block >= 0) & (block < count), row, 0)


def first_kernel(
    axis_md,
    axis_cd,
    own,
    needle,
    near_first,
    near_second,
    far,
    start,
    end,
    column,
    field,
    coef,
    uy,
    s1,
    gain,
    strip_s0,
    strip_coef,
    strip_base,
    strip_uy,
    strip_s1,
    strip_tgt,
    up,
    down,
    spread,
    cover,
    source,
):
    layers = field.shape[1] - 2
    height = own.shape[1]
    md = lax.axis_index(axis_md)
    count = lax.axis_size(axis_md)
    lane = lane_iota((height, LANES))
    outer = lane % 8 < HALO
    odd = lax.axis_index(axis_cd) % 2 == 1

    def from_left(c):
        return jnp.where(odd, near_second[c], near_first[c])

    def from_right(c):
        return jnp.where(odd, near_first[c], near_second[c])

    def half(take, c, turn):
        return take(c) if c < PAIRS else pltpu.roll(take(c - PAIRS), turn, 1)

    def feet(ref):
        return jnp.concatenate(
            [feet_block(ref, md + d, count) for d in (-1, 0, 1, 2)], axis=1
        )

    starts, ends, columns = feet(start), feet(end), feet(column)
    rates = jnp.concatenate(
        [from_left(PAIRS), needle[...], from_right(PAIRS), far[...]], axis=1
    )
    needles = rates.shape[1]
    picked = jnp.where(row_iota((height, needles)) == columns, 1.0, 0.0)
    for part, value in enumerate(split_three(rates)):
        for z in range(layers):
            spread[part, z * height : (z + 1) * height] = (picked * value[z : z + 1]).astype(
                jnp.bfloat16
            )
    length = 2 * LANES
    cells = row_iota((length + LANES, needles))
    beyond = cells - length
    strip = jnp.where(beyond < 8, beyond - HALO, beyond - 8 + length - HALO)
    cells = jnp.where(cells < length, cells, strip) + md * length
    cover[...] = jnp.where((cells >= starts) & (cells < ends), 1.0, 0.0).astype(jnp.bfloat16)
    product = jnp.zeros((layers * height, length + LANES), F32)
    for part in range(3):
        product = product + lax.dot_general(
            spread[part], cover[...], (((1,), (1,)), ((), ())), preferred_element_type=F32
        )
    product = DT * product
    for tile in range(2):
        gain[1 : layers + 1, tile] = product[:, span(tile)].reshape(layers, height, LANES)
    source[...] = product[:, span(2)].reshape(source.shape)

    state = Field(field, strip_s0)
    state.clear_strips()
    has_left, has_right = md > 0, md < count - 1
    for side in range(2):

        def raw(c):
            if side == 0:
                return jnp.where(outer, jnp.where(has_left, half(from_left, c, LANES - HALO), 0.0), own[c])
            return jnp.where(outer, own[c], jnp.where(has_right, half(from_right, c, HALO), 0.0))

        for c in range(5):
            strip_s0[c, side, OWN] = raw(S0 + c)
            strip_tgt[c, side] = raw(TGT + c)
        u = [DT * raw(VEL + d) for d in range(3)]
        turn = DT * raw(ROT)
        for key, value in gradient_parts(lambda i: raw(GRAD + i)).items():
            strip_coef[PLACE[key], side] = value
        strip_coef[SPREAD, side] = 2.0 * turn
        strip_coef[UX, side] = u[0]
        strip_coef[UZ, side] = u[2]
        strip_uy[side, 0:8] = jnp.zeros((8, LANES), F32)
        strip_uy[side, 24:32] = jnp.zeros((8, LANES), F32)
        strip_uy[side, OWN] = u[1]
        damp = 6.0 * turn + (jnp.abs(u[0]) + jnp.abs(u[1]) + jnp.abs(u[2]))
        taken = jnp.zeros((height, LANES), F32)
        for z in range(layers):
            moved = pltpu.roll(source[z], (8 * z - 8 * side) % LANES, 1)
            taken = jnp.where(lane // 8 == z, moved, taken)
        strip_base[side] = damp + taken

    for side in range(2):
        m, damp = coefficients(strip_coef, strip_base, side)
        wind = (strip_coef[UX, side], strip_uy[side, OWN], strip_coef[UZ, side])
        a = [strip_s0[c, side, OWN] for c in range(5)]
        spin = strip_coef[SPREAD, side]
        out = forward(a, m, damp, spin, wind, state.strip_around(side))
        for c in range(5):
            strip_s1[c, side, OWN] = out[c]

    def put(side):
        def at(place):
            return line(None, side * 11 + place, 22, layers)

        for c in range(5):
            first, new = strip_s0.at[c, side], strip_s1.at[c, side]
            up[at(c)], down[at(c)] = first[23:24], first[8:9]
            up[at(5 + c)], down[at(5 + c)] = new[23:24], new[8:9]
        wind = strip_uy.at[side]
        up[at(10)] = -jnp.minimum(wind[23:24], 0.0)
        down[at(10)] = jnp.maximum(wind[8:9], 0.0)

    for message, row in ((up, 15), (down, 0)):
        for tile in range(2):
            u = row_of(coef, UX, tile, row)
            if tile == 0:
                weight, turn = jnp.where(lane == 0, jnp.maximum(u, 0.0), 0.0), 1
            else:
                weight = jnp.where(lane == LANES - 1, -jnp.minimum(u, 0.0), 0.0)
                turn = LANES - 1
            gained = row_of(gain, 0, tile, row)
            for c in range(5):
                left, right = (strip_s0[c, side, 8 + row : 9 + row] for side in (0, 1))
                edge = pltpu.roll(edge_column(left, right, layers), turn, 1)
                old = row_of(field, c, tile, 8 + row)
                new = row_of(s1, c, tile, 8 + row) - gained * old + weight * edge
                message[planes(tile * 11 + c, layers)] = old
                message[planes(tile * 11 + 5 + c, layers)] = new
            speed = row_of(uy, 0, tile, 8 + row)
            outward = -jnp.minimum(speed, 0.0) if row else jnp.maximum(speed, 0.0)
            message[planes(tile * 11 + 10, layers)] = outward
    for side in range(2):
        put(side)


def cd_flags(axis_cd):
    cd = lax.axis_index(axis_cd)
    return cd > 0, cd < lax.axis_size(axis_cd) - 1


def advance_kernel(
    s1_in,
    field,
    gain,
    coef,
    base_in,
    uy,
    tgt,
    strip_s0,
    strip_s1,
    strip_coef,
    strip_base,
    strip_uy,
    strip_tgt,
    s1,
    base,
    s2,
    goal,
    adj1,
    dots,
    adj2,
    strip_adj2,
    joint,
    joint1,
    joint2,
):
    layers, height = tgt.shape[1], tgt.shape[2]
    lane = lane_iota((height, LANES))
    start = Field(field, strip_s0, joint)
    state = Field(s1, strip_s1, joint1)
    delta = Field(adj2, strip_adj2, joint2)
    start.join()
    state.join()
    clear_planes(s1)
    clear_planes(adj2)
    for side in range(2):
        m, damp = coefficients(strip_coef, strip_base, side)
        wind = (strip_coef[UX, side], strip_uy[side, OWN], strip_coef[UZ, side])
        a = [strip_s1[c, side, OWN] for c in range(5)]
        spin = strip_coef[SPREAD, side]
        out = forward(a, m, damp, spin, wind, state.strip_around(side))
        for c in range(5):
            strip_adj2[c, side, OWN] = out[c] - strip_tgt[c, side]
    delta.join()

    def mend(z, carry):
        for tile in range(2):
            gained = gain[z + 1, tile]
            base[z + 1, tile] = base_in[z + 1, tile] + gained
            u = coef[UX, z + 1, tile]
            if tile == 0:
                weight, turn = jnp.where(lane == 0, jnp.maximum(u, 0.0), 0.0), 1
            else:
                weight, turn = jnp.where(lane == LANES - 1, -jnp.minimum(u, 0.0), 0.0), -1
            for c in range(5):
                edge = pltpu.roll(joint[c], (2 * LANES - HALO + turn - 8 * z) % LANES, 1)
                s1[c, z + 1, tile, OWN] = (
                    s1_in[c, z + 1, tile, OWN]
                    - gained * field[c, z + 1, tile, OWN]
                    + weight * edge
                )
        return carry

    lax.fori_loop(0, layers, mend, 0, unroll=2)

    def advance(z, carry):
        for tile in range(2):
            at = (z + 1, tile)
            m, damp = coefficients(coef, base, *at)
            wind = (coef[(UX,) + at], uy[at + (OWN,)], coef[(UZ,) + at])
            a = [state.own(c, z, tile) for c in range(5)]
            out = forward(a, m, damp, coef[(SPREAD,) + at], wind, state.around(z, tile))
            total = 0.0
            for c in range(5):
                wanted = tgt[c, z, :, span(tile)]
                miss = out[c] - wanted
                s2[(c,) + at] = out[c]
                goal[(c,) + at] = wanted
                adj2[(c,) + at + (OWN,)] = miss
                total = total + miss * a[c]
            dots[at] = total
        return carry

    lax.fori_loop(0, layers, advance, 0, unroll=2)
    edge_x = merged(strip_coef, UX, slice(None))

    def retreat(z, carry):
        for tile in range(2):
            m, damp = coefficients(coef, base, z + 1, tile)
            a = [state.own(c, z, tile) for c in range(5)]
            b = [delta.own(c, z, tile) for c in range(5)]
            wind = back_wind(coef, uy, edge_x, z, tile)
            out = backward(b, a, m, damp, wind, delta.around(z, tile))
            for c in range(5):
                adj1[c, z + 1, tile] = out[c]
        return carry

    lax.fori_loop(0, layers, retreat, 0, unroll=2)


def edge_kernel(
    axis_cd,
    s1,
    strip_s1_in,
    coef,
    base,
    uy,
    goal,
    strip_coef,
    strip_base,
    strip_uy,
    strip_tgt,
    own_up,
    own_down,
    from_below,
    from_above,
    s2_edge,
    adj2_edge,
    adj1_edge,
    dots_edge,
    strip_adj2,
    strip_adj1,
    up,
    down,
    strip_s1,
):
    layers = goal.shape[1] - 2
    has_below, has_above = cd_flags(axis_cd)

    state, delta = Field(s1, strip_s1), Field(s1, strip_adj2)
    delta.clear_strips()
    for side in range(2):

        def at(place):
            return line(None, side * 11 + place, 22, layers)

        wind = strip_uy.at[side]
        low_u, high_u = jnp.maximum(wind[8:9], 0.0), -jnp.minimum(wind[23:24], 0.0)
        low_n, high_n = from_below[at(10)], from_above[at(10)]
        for c in range(5):
            old, new = at(c), at(5 + c)
            ref = strip_s1.at[c, side]
            ref[OWN] = strip_s1_in[c, side, OWN]
            low = from_below[new] + low_n * own_down[old]
            high = from_above[new] + high_n * own_up[old]
            ref[7:8] = jnp.where(has_below, low, 0.0)
            ref[24:25] = jnp.where(has_above, high, 0.0)
            ref[8:9] = ref[8:9] + jnp.where(has_below, low_u * from_below[old], 0.0)
            ref[23:24] = ref[23:24] + jnp.where(has_above, high_u * from_above[old], 0.0)
    for side in range(2):
        m, damp = coefficients(strip_coef, strip_base, side)
        wind = (strip_coef[UX, side], strip_uy[side, OWN], strip_coef[UZ, side])
        a = [strip_s1[c, side, OWN] for c in range(5)]
        spin = strip_coef[SPREAD, side]
        out = forward(a, m, damp, spin, wind, state.strip_around(side))
        for c in range(5):
            strip_adj2[c, side, OWN] = out[c] - strip_tgt[c, side]
    for side in range(2):

        def at(place):
            return line(None, side * 10 + place, 20, layers)

        m, damp = coefficients(strip_coef, strip_base, side)
        a = [strip_s1[c, side, OWN] for c in range(5)]
        b = [strip_adj2[c, side, OWN] for c in range(5)]
        wind = strip_back_wind(strip_coef, strip_uy, side)
        out = backward(b, a, m, damp, wind, delta.strip_around(side))
        high = -jnp.minimum(strip_uy[side, 23:24], 0.0)
        low = jnp.maximum(strip_uy[side, 8:9], 0.0)
        for c in range(5):
            strip_adj1[c, side, OWN] = out[c]
            up[at(c)] = high * b[c][-1:]
            down[at(c)] = low * b[c][:1]
            up[at(5 + c)] = high * out[c][-1:]
            down[at(5 + c)] = low * out[c][:1]

    def constants(tile, row):
        m = {key: row_of(coef, place, tile, row) for key, place in PLACE.items()}
        return m, row_of(base, 0, tile, row)

    for number, (message, mine, valid, outgoing) in enumerate(
        ((from_below, own_down, has_below, down), (from_above, own_up, has_above, up))
    ):
        rows = (0, 1, 2) if number == 0 else (15, 14, 13)
        sides = (0, 1)

        def plane(ref, place, tile):
            return ref[planes(tile * 11 + place, layers)]

        lines = [{}, {}, {}, {}]
        for c in range(5):
            for tile in range(2):
                old, new = plane(message, c, tile), plane(message, 5 + c, tile)
                weight = plane(message, 10, tile)
                lines[0][c, tile] = jnp.where(
                    valid, new + weight * plane(mine, c, tile), 0.0
                )
                lines[1][c, tile] = plane(mine, 5 + c, tile) + jnp.where(
                    valid, plane(mine, 10, tile) * old, 0.0
                )
                for k in (1, 2):
                    lines[k + 1][c, tile] = row_of(s1, c, tile, 8 + rows[k])

        def strip_edge(ref, c, row):
            left, right = (ref[c, side, 8 + row : 9 + row] for side in sides)
            return edge_column(left, right, layers)

        def ordered(outer, inner):
            return (outer, inner) if number == 0 else (inner, outer)

        misses = [{}, {}]
        for k in range(2):
            row = rows[k]
            edges = [strip_edge(strip_s1, c, row) for c in range(5)]
            for tile in range(2):
                m, damp = constants(tile, row)
                wind = (
                    row_of(coef, UX, tile, row),
                    row_of(uy, 0, tile, 8 + row),
                    row_of(coef, UZ, tile, row),
                )
                a = [lines[k + 1][c, tile] for c in range(5)]

                def around(c):
                    tiles = [lines[k + 1][c, t] for t in range(2)]
                    return (
                        x_pair(tiles, tile, edges[c]),
                        ordered(lines[k][c, tile], lines[k + 2][c, tile]),
                        layer_pair(a[c]),
                    )

                out = forward(a, m, damp, row_of(coef, SPREAD, tile, row), wind, around)
                total = 0.0
                for c in range(5):
                    miss = out[c] - row_of(goal, c, tile, row)
                    s2_edge[c, 2 * number + k, tile] = out[c]
                    adj2_edge[c, 2 * number + k, tile] = miss
                    misses[k][c, tile] = miss
                    total = total + miss * a[c]
                dots_edge[2 * number + k, tile] = total

        row = rows[0]
        edges = [strip_edge(strip_adj2, c, row) for c in range(5)]
        left, right = (strip_coef[UX, side, row : row + 1] for side in sides)
        edge_x = edge_column(left, right, layers)
        for tile in range(2):
            m, damp = constants(tile, row)
            a = [lines[1][c, tile] for c in range(5)]
            b = [misses[0][c, tile] for c in range(5)]
            zero = jnp.zeros_like(b[0])
            wind = (
                x_pair([row_of(coef, UX, t, row) for t in range(2)], tile, edge_x),
                ordered(zero, row_of(uy, 0, tile, 8 + rows[1])),
                layer_pair(row_of(coef, UZ, tile, row)),
            )

            def around(c):
                tiles = [misses[0][c, t] for t in range(2)]
                return (
                    x_pair(tiles, tile, edges[c]),
                    ordered(zero, misses[1][c, tile]),
                    layer_pair(b[c]),
                )

            out = backward(b, a, m, damp, wind, around)
            weight = plane(mine, 10, tile)
            for c in range(5):
                outgoing[planes(tile * 10 + c, layers)] = weight * b[c]
                outgoing[planes(tile * 10 + 5 + c, layers)] = weight * out[c]
                adj1_edge[c, number, tile] = out[c]


def needle_feet(ref, md, count):
    return jnp.concatenate([feet_block(ref, md + d, count) for d in (-1, 0, 1)], axis=1)


def own_cover(md, length, starts, ends):
    cells = row_iota((length, starts.shape[1])) + md * length
    return jnp.where((cells >= starts) & (cells < ends), 1.0, 0.0).astype(jnp.bfloat16)


def covered_sum(values, cover):
    product = jnp.zeros((values.shape[0], cover.shape[1]), F32)
    for part in split_three(values):
        product = product + jnp.dot(
            part.astype(jnp.bfloat16), cover, preferred_element_type=F32
        )
    return product


def second_kernel(
    axis_md,
    s1,
    s2_in,
    goal,
    adj1_in,
    dots_in,
    s2_edge,
    adj2_edge,
    adj1_edge,
    dots_edge,
    field,
    coef,
    base,
    uy,
    strip_coef,
    strip_adj2,
    strip_adj1,
    start,
    end,
    column,
    s2_out,
    adj0,
    gained,
    adj1,
    dots,
    sens,
    s2,
    joint,
):
    layers, height = goal.shape[1] - 2, goal.shape[3]
    length = 2 * LANES
    md = lax.axis_index(axis_md)
    count = lax.axis_size(axis_md)

    def gather(z, carry):
        for tile in range(2):
            dots[z + 1, tile] = dots_in[z + 1, tile]
            for c in range(5):
                s2[c, z + 1, tile] = s2_in[c, z + 1, tile]
                adj1[c, z + 1, tile, OWN] = adj1_in[c, z + 1, tile]
        return carry

    lax.fori_loop(0, layers, gather, 0, unroll=2)
    for tile in range(2):
        for number, row in enumerate((0, 1, 15, 14)):
            set_row(dots, 0, tile, row, dots_edge[number, tile])
            for c in range(5):
                set_row(s2, c, tile, row, s2_edge[c, number, tile])
        for number, row in enumerate((0, 15)):
            for c in range(5):
                set_row(adj1, c, tile, 8 + row, adj1_edge[c, number, tile])

    for number, rows in enumerate(((0, 1, 2, 3), (15, 14, 13, 12))):
        lines = [{}, {}, {}, {}]
        for c in range(5):
            for tile in range(2):
                for k in (0, 1):
                    lines[k][c, tile] = adj2_edge[c, 2 * number + k, tile]
                for k in (2, 3):
                    state = row_of(s2_in, c, tile, rows[k])
                    lines[k][c, tile] = state - row_of(goal, c, tile, rows[k])

        def ordered(outer, inner):
            return (outer, inner) if number == 0 else (inner, outer)

        for k in (1, 2):
            row = rows[k]
            edges = []
            for c in range(5):
                left, right = (strip_adj2[c, side, 8 + row : 9 + row] for side in (0, 1))
                edges.append(edge_column(left, right, layers))
            left, right = (strip_coef[UX, side, row : row + 1] for side in (0, 1))
            edge = edge_column(left, right, layers)
            for tile in range(2):
                m = {key: row_of(coef, place, tile, row) for key, place in PLACE.items()}
                damp = row_of(base, 0, tile, row)
                a = [row_of(s1, c, tile, 8 + row) for c in range(5)]
                b = [lines[k][c, tile] for c in range(5)]
                wind = (
                    x_pair([row_of(coef, UX, t, row) for t in range(2)], tile, edge),
                    ordered(*(row_of(uy, 0, tile, 8 + rows[i]) for i in (k - 1, k + 1))),
                    layer_pair(row_of(coef, UZ, tile, row)),
                )

                def around(c):
                    return (
                        x_pair([lines[k][c, t] for t in range(2)], tile, edges[c]),
                        ordered(lines[k - 1][c, tile], lines[k + 1][c, tile]),
                        layer_pair(b[c]),
                    )

                out = backward(b, a, m, damp, wind, around)
                for c in range(5):
                    set_row(adj1, c, tile, 8 + row, out[c])

    def write(z, carry):
        for tile in range(2):
            for c in range(5):
                s2_out[c, z, :, span(tile)] = s2[c, z + 1, tile]
        return carry

    lax.fori_loop(0, layers, write, 0, unroll=2)
    edge_x = merged(strip_coef, UX, slice(None))
    last_delta = Field(adj1, strip_adj1, joint)
    last_delta.clear()
    last_delta.join()

    def finish(z, carry):
        for tile in range(2):
            m, damp = coefficients(coef, base, z + 1, tile)
            a = [field[c, z + 1, tile, OWN] for c in range(5)]
            b = [last_delta.own(c, z, tile) for c in range(5)]
            wind = back_wind(coef, uy, edge_x, z, tile)
            out = backward(b, a, m, damp, wind, last_delta.around(z, tile))
            total = dots[z + 1, tile]
            for c in range(5):
                adj0[c, z + 1, tile] = out[c]
                total = total + a[c] * b[c]
            sens[z, :, span(tile)] = -DT * total
        return carry

    lax.fori_loop(0, layers, finish, 0, unroll=2)
    starts, ends, columns = (needle_feet(ref, md, count) for ref in (start, end, column))
    cover = own_cover(md, length, starts, ends)
    product = covered_sum(sens[...].reshape(layers * height, length), cover)
    picked = jnp.where(row_iota((height, starts.shape[1])) == columns, 1.0, 0.0)
    for z in range(layers):
        gained[z : z + 1] = jnp.sum(
            product[z * height : (z + 1) * height] * picked, axis=0, keepdims=True
        )


def third_kernel(
    axis_md,
    axis_cd,
    gained,
    field,
    from_below,
    from_above,
    start,
    end,
    column,
    first,
    kept,
    second,
):
    layers = field.shape[1] - 2
    length = 2 * LANES
    md = lax.axis_index(axis_md)
    count = lax.axis_size(axis_md)
    odd = lax.axis_index(axis_cd) % 2 == 1
    lines = []
    for message, valid, row in zip((from_below, from_above), cd_flags(axis_cd), (8, 23)):
        parts = []
        for tile in range(2):
            total = 0.0
            for c in range(5):
                brought = message[planes(tile * 10 + c, layers)]
                total = total + brought * row_of(field, c, tile, row)
            parts.append(jnp.where(valid, -DT * total, 0.0))
        lines.append(jnp.concatenate(parts, axis=1))
    starts, ends, columns = (needle_feet(ref, md, count) for ref in (start, end, column))
    cover = own_cover(md, length, starts, ends)
    product = covered_sum(jnp.concatenate(lines, axis=0), cover)
    total = gained[...]
    for number, row in enumerate((0, 15)):
        here = product[number * layers : (number + 1) * layers]
        total = total + jnp.where(columns == row, here, 0.0)
    first[...] = jnp.where(odd, total[:, span(0)], total[:, span(2)])
    kept[...] = total[:, span(1)]
    second[...] = jnp.where(odd, total[:, span(2)], total[:, span(0)])


def fourth_kernel(
    axis_cd,
    adj0_in,
    field,
    coef,
    base,
    uy,
    strip_coef,
    weights_below,
    weights_above,
    own_up,
    own_down,
    from_below,
    from_above,
    out_field,
    adj0,
):
    layers = field.shape[1] - 2
    has_below, has_above = cd_flags(axis_cd)

    def gather(z, carry):
        for tile in range(2):
            for c in range(5):
                adj0[c, z + 1, tile] = adj0_in[c, z + 1, tile]
        return carry

    lax.fori_loop(0, layers, gather, 0, unroll=2)

    for number, (weights, message, mine, valid) in enumerate(
        (
            (weights_below, from_below, own_down, has_below),
            (weights_above, from_above, own_up, has_above),
        )
    ):
        row, inner = ((0, 1), (15, 14))[number]
        brought = {}
        for c in range(5):
            for tile in range(2):
                value = message[planes(tile * 10 + c, layers)]
                brought[c, tile] = jnp.where(valid, value, 0.0)
        edges = []
        for c in range(5):
            left, right = (message[line(None, side * 10 + c, 20, layers)] for side in (0, 1))
            edges.append(jnp.where(valid, edge_column(left, right, layers), 0.0))
        left, right = (strip_coef[UX, side, row : row + 1] for side in (0, 1))
        edge_x = edge_column(left, right, layers)
        for tile in range(2):
            m = {key: row_of(coef, place, tile, row) for key, place in PLACE.items()}
            damp = row_of(base, 0, tile, row)
            a = [row_of(field, c, tile, 8 + row) for c in range(5)]
            b = [brought[c, tile] for c in range(5)]
            wind = (
                x_pair([row_of(coef, UX, t, row) for t in range(2)], tile, edge_x),
                layer_pair(row_of(coef, UZ, tile, row)),
            )

            def around(c):
                tiles = [brought[c, t] for t in range(2)]
                return x_pair(tiles, tile, edges[c]), layer_pair(b[c])

            out = backward(b, a, m, damp, wind, around)
            speed = row_of(uy, 0, tile, 8 + row)
            inward = -jnp.minimum(speed, 0.0) if number == 0 else jnp.maximum(speed, 0.0)
            weight = weights[planes(tile * 11 + 10, layers)]
            for c in range(5):
                own = mine[planes(tile * 10 + c, layers)]
                far = message[planes(tile * 10 + 5 + c, layers)] + weight * own
                total = out[c] + jnp.where(valid, far, 0.0)
                set_row(adj0, c, tile, row, row_of(adj0, c, tile, row) + total)
                more = inward * b[c]
                set_row(adj0, c, tile, inner, row_of(adj0, c, tile, inner) + more)

    def scatter(z, carry):
        for tile in range(2):
            for c in range(5):
                out_field[c, z, :, span(tile)] = adj0[c, z + 1, tile]
        return carry

    lax.fori_loop(0, layers, scatter, 0, unroll=2)


def ring(value, axis, steps):
    count = lax.axis_size(axis)
    return lax.ppermute(value, axis, [(i, (i + steps) % count) for i in range(count)])


def winding(value, steps, turn):
    rows, columns = lax.axis_size("md"), lax.axis_size("cd")
    pairs = []
    for column in range(columns):
        for row in range(rows):
            target = row + (steps if column % 2 == turn else -steps)
            if 0 <= target < rows:
                pairs.append((row * columns + column, target * columns + column))
            else:
                pairs.append((row * columns + column, row * columns + (column ^ 1)))
    return lax.ppermute(value, ("md", "cd"), pairs)


def shape_of(*dims, dtype=F32):
    return jax.ShapeDtypeStruct(dims, dtype)


def scratch(*dims, dtype=F32):
    return pltpu.VMEM(dims, dtype)


def cost(microseconds):
    return pl.CostEstimate(
        flops=int(microseconds * 1e6), bytes_accessed=int(microseconds * 3e6), transcendentals=0
    )


def params(mebibytes):
    return pltpu.CompilerParams(vmem_limit_bytes=mebibytes * 1024 * 1024)


def local(orientation, velocity, velocity_grad, rotary, target, needle_params, *feet):
    _, layers, height, length = orientation.shape
    rotary = rotary[None]
    rates = jnp.transpose(needle_params[:, 0, :])
    feet = [foot.reshape(1, -1) for foot in feet]
    padded = (layers + 2, 2, ROWS, LANES)
    plain = (layers + 2, 2, height, LANES)
    strip_padded, strip = (2, ROWS, LANES), (2, height, LANES)
    message, back_message = shape_of(22 * layers + 24, LANES), shape_of(20 * layers + 24, LANES)
    joint = scratch(5, height, LANES)

    hbm = pl.BlockSpec(memory_space=pltpu.HBM)
    blocks = 4
    packed, first, second, field, coef, base, uy = pl.pallas_call(
        functools.partial(pack_kernel, "cd"),
        in_specs=[hbm] * 6,
        out_shape=[
            shape_of(NEEDLES, height, LANES),
            shape_of(PAIRS + 1, height, LANES),
            shape_of(PAIRS + 1, height, LANES),
            shape_of(5, *padded),
            shape_of(COEFS, *plain),
            shape_of(*plain),
            shape_of(*padded),
        ],
        scratch_shapes=[
            scratch(NEEDLES, layers, height, length),
            scratch(*rates.shape),
            pltpu.SemaphoreType.DMA((blocks, 5)),
            pltpu.SemaphoreType.DMA,
        ],
        compiler_params=params(20),
        cost_estimate=cost(4),
    )(
        *(
            pltpu.with_memory_space_constraint(field, pltpu.HBM)
            for field in (orientation, velocity, velocity_grad, rotary, target, rates)
        )
    )
    far = ring(rates, "md", -2)
    near = winding(first, 1, 0), winding(second, 1, 1)

    s1 = pl.pallas_call(
        bulk_kernel,
        out_shape=shape_of(5, *padded),
        compiler_params=params(16),
        cost_estimate=cost(2),
    )(field, coef, base, uy)

    gain, strip_s0, strip_coef, strip_base, strip_uy, strip_s1, strip_tgt, up, down = (
        pl.pallas_call(
            functools.partial(first_kernel, "md", "cd"),
            out_shape=[
                shape_of(*plain),
                shape_of(5, *strip_padded),
                shape_of(COEFS, *strip),
                shape_of(*strip),
                shape_of(*strip_padded),
                shape_of(5, *strip_padded),
                shape_of(5, *strip),
                message,
                message,
            ],
            scratch_shapes=[
                scratch(3, layers * height, 4 * LANES, dtype=jnp.bfloat16),
                scratch(length + LANES, 4 * LANES, dtype=jnp.bfloat16),
                scratch(layers, height, LANES),
            ],
            compiler_params=params(24),
            cost_estimate=cost(3),
        )(packed, rates, *near, far, *feet, field, coef, uy, s1)
    )
    below = ring(up, "cd", 1)
    above = ring(down, "cd", -1)

    s1, base, s2_part, goal, adj1_part, dots = pl.pallas_call(
        advance_kernel,
        out_shape=[
            shape_of(5, *padded),
            shape_of(*plain),
            shape_of(5, *plain),
            shape_of(5, *plain),
            shape_of(5, *plain),
            shape_of(*plain),
        ],
        scratch_shapes=[scratch(5, *padded), scratch(5, *strip_padded), joint, joint, joint],
        compiler_params=params(16),
        cost_estimate=cost(8),
    )(
        s1,
        field,
        gain,
        coef,
        base,
        uy,
        target,
        strip_s0,
        strip_s1,
        strip_coef,
        strip_base,
        strip_uy,
        strip_tgt,
    )
    edge_row = (2, layers, LANES)
    s2_edge, adj2_edge, adj1_edge, dots_edge, strip_adj2, strip_adj1, back_up, back_down = (
        pl.pallas_call(
            functools.partial(edge_kernel, "cd"),
            out_shape=[
                shape_of(5, 4, *edge_row),
                shape_of(5, 4, *edge_row),
                shape_of(5, 2, *edge_row),
                shape_of(4, *edge_row),
                shape_of(5, *strip_padded),
                shape_of(5, *strip_padded),
                back_message,
                back_message,
            ],
            scratch_shapes=[scratch(5, *strip_padded)],
            compiler_params=params(16),
            cost_estimate=cost(2),
        )(
            s1,
            strip_s1,
            coef,
            base,
            uy,
            goal,
            strip_coef,
            strip_base,
            strip_uy,
            strip_tgt,
            up,
            down,
            below,
            above,
        )
    )
    back_below = ring(back_up, "cd", 1)
    back_above = ring(back_down, "cd", -1)

    part = shape_of(*rates.shape)
    s2, adj0_part, gained = pl.pallas_call(
        functools.partial(second_kernel, "md"),
        out_shape=[
            shape_of(*orientation.shape),
            shape_of(5, *plain),
            shape_of(layers, 3 * LANES),
        ],
        scratch_shapes=[
            scratch(5, *padded),
            scratch(*plain),
            scratch(layers, height, length),
            scratch(5, *plain),
            joint,
        ],
        compiler_params=params(24),
        cost_estimate=cost(6),
    )(
        s1,
        s2_part,
        goal,
        adj1_part,
        dots,
        s2_edge,
        adj2_edge,
        adj1_edge,
        dots_edge,
        field,
        coef,
        base,
        uy,
        strip_coef,
        strip_adj2,
        strip_adj1,
        *feet,
    )

    part_first, part_own, part_second = pl.pallas_call(
        functools.partial(third_kernel, "md", "cd"),
        out_shape=[part, part, part],
        compiler_params=params(16),
        cost_estimate=cost(1),
    )(gained, field, back_below, back_above, *feet)
    part_first = winding(part_first, 1, 0)
    part_second = winding(part_second, 1, 1)

    adj0 = pl.pallas_call(
        functools.partial(fourth_kernel, "cd"),
        out_shape=shape_of(*orientation.shape),
        scratch_shapes=[scratch(5, *plain)],
        compiler_params=params(16),
        cost_estimate=cost(2),
    )(
        adj0_part,
        field,
        coef,
        base,
        uy,
        strip_coef,
        below,
        above,
        back_up,
        back_down,
        back_below,
        back_above,
    )
    gradient = part_own + part_first + part_second
    return s2, adj0, jnp.transpose(gradient)[:, None, :]


def solution(mesh):
    field = P(None, None, "cd", "md")
    feet = P(None, "cd")
    needles = P("md", "cd", None)
    return jax.shard_map(
        local,
        mesh=mesh,
        in_specs=(field, field, field, P(None, "cd", "md"), field, needles, feet, feet, feet),
        out_specs=(field, field, needles),
        check_vma=False,
    )
```

```python
import functools

import jax
import jax.numpy as jnp
from jax import lax
from jax.experimental import pallas as pl
from jax.experimental.pallas import tpu as pltpu
from jax.sharding import PartitionSpec as P

XI = 0.95
DT = 0.1
LANES = 128
F32 = jnp.float32
HALO = 4
S0, VEL, GRAD, ROT, TGT, NEEDLES = 0, 5, 8, 17, 18, 23
PAIRS = 12
PLACE = {(0, 0): 0, (1, 1): 1, (0, 1): 2, (1, 0): 3, (0, 2): 4, (2, 0): 5, (1, 2): 6, (2, 1): 7}
SPREAD, UX, UZ, COEFS = 8, 9, 10, 11
ROWS = 32
OWN, BEHIND, FRONT = slice(8, 24), slice(7, 23), slice(9, 25)


def lane_iota(shape):
    return lax.broadcasted_iota(jnp.int32, shape, len(shape) - 1)


def row_iota(shape):
    return lax.broadcasted_iota(jnp.int32, shape, len(shape) - 2)


def span(tile):
    return slice(tile * LANES, (tile + 1) * LANES)


def gradient_parts(read):
    g = [read(i) for i in range(9)]
    low = 0.5 * (XI - 1.0) * DT
    m = {}
    for i, j in ((0, 1), (0, 2), (1, 2)):
        a, b = g[3 * i + j], g[3 * j + i]
        both = low * (a + b)
        m[i, j] = DT * a + both
        m[j, i] = DT * b + both
    m[0, 0] = (XI * DT) * (g[0] - g[8])
    m[1, 1] = (XI * DT) * (g[4] - g[8])
    return m


def forward(a, m, base, spread, wind, around):
    a11, a22, a12, a13, a23 = a
    a33 = 1.0 - a11 - a22
    n00 = m[0, 0] * a11 + m[0, 1] * a12 + m[0, 2] * a13
    n01 = m[0, 0] * a12 + m[0, 1] * a22 + m[0, 2] * a23
    n02 = m[0, 0] * a13 + m[0, 1] * a23 + m[0, 2] * a33
    n10 = m[1, 0] * a11 + m[1, 1] * a12 + m[1, 2] * a13
    n11 = m[1, 0] * a12 + m[1, 1] * a22 + m[1, 2] * a23
    n12 = m[1, 0] * a13 + m[1, 1] * a23 + m[1, 2] * a33
    n20 = m[2, 0] * a11 + m[2, 1] * a12
    n21 = m[2, 0] * a12 + m[2, 1] * a22
    n22 = m[2, 0] * a13 + m[2, 1] * a23
    keep = 1.0 - (base + 2.0 * (n00 + n11 + n22))
    gain = (2.0 * n00 + spread, 2.0 * n11 + spread, n01 + n10, n02 + n20, n12 + n21)
    out = []
    for c in range(5):
        total = gain[c] + keep * a[c]
        for u, (behind, front) in zip(wind, around(c)):
            total = total + jnp.abs(u) * jnp.where(u > 0.0, behind, front)
        out.append(total)
    return out


def backward(b, a, m, base, wind, around):
    b1, b2, b3, b4, b5 = b
    a11, a22, a12, a13, a23 = a
    g = -2.0 * (b1 * a11 + b2 * a22 + b3 * a12 + b4 * a13 + b5 * a23)
    trace = (
        m[0, 0] * a11
        + m[1, 1] * a22
        + (m[0, 1] + m[1, 0]) * a12
        + (m[0, 2] + m[2, 0]) * a13
        + (m[1, 2] + m[2, 1]) * a23
    )
    s00, s11, s22 = 2.0 * b1 + g, 2.0 * b2 + g, g
    h00 = m[0, 0] * s00 + m[1, 0] * b3 + m[2, 0] * b4
    h01 = m[0, 0] * b3 + m[1, 0] * s11 + m[2, 0] * b5
    h02 = m[0, 0] * b4 + m[1, 0] * b5 + m[2, 0] * s22
    h10 = m[0, 1] * s00 + m[1, 1] * b3 + m[2, 1] * b4
    h11 = m[0, 1] * b3 + m[1, 1] * s11 + m[2, 1] * b5
    h12 = m[0, 1] * b4 + m[1, 1] * b5 + m[2, 1] * s22
    h20 = m[0, 2] * s00 + m[1, 2] * b3
    h21 = m[0, 2] * b3 + m[1, 2] * s11
    h22 = m[0, 2] * b4 + m[1, 2] * b5
    keep = 1.0 - (base + 2.0 * trace)
    gain = (h00 - h22, h11 - h22, h01 + h10, h02 + h20, h12 + h21)
    weights = [(jnp.minimum(w, 0.0), jnp.maximum(f, 0.0)) for w, f in wind]
    out = []
    for c in range(5):
        total = gain[c] + keep * b[c]
        for (low, high), (behind, front) in zip(weights, around(c)):
            total = total + (high * front - low * behind)
        out.append(total)
    return out


def merged(strips, c, rows):
    left, right = strips[c, 0, rows], strips[c, 1, rows]
    return jnp.where(lane_iota(left.shape) % 8 < HALO, left, right)


def edge_tile(joint, z):
    return pltpu.roll(joint, (2 * LANES - HALO - 8 * z) % LANES, 1)


def x_pair(tiles, tile, edge):
    cur = tiles[tile]
    prev, after = (edge, tiles[1]) if tile == 0 else (tiles[0], edge)
    lane = lane_iota(cur.shape)
    behind = pltpu.roll(jnp.where(lane == LANES - 1, prev, cur), 1, 1)
    front = pltpu.roll(jnp.where(lane == 0, after, cur), LANES - 1, 1)
    return behind, front


def strip_x(cur):
    return pltpu.roll(cur, 1, 1), pltpu.roll(cur, LANES - 1, 1)


def strip_z(cur):
    lane = lane_iota(cur.shape)
    behind = jnp.where(lane < 8, 0.0, pltpu.roll(cur, 8, 1))
    front = jnp.where(lane >= LANES - 8, 0.0, pltpu.roll(cur, LANES - 8, 1))
    return behind, front


def coefficients(coef, base, *at):
    m = {key: coef[(place,) + at] for key, place in PLACE.items()}
    return m, base[at]


class Field:
    def __init__(self, ref, strips, joint=None):
        self.ref, self.strips, self.joint = ref, strips, joint

    def join(self):
        for c in range(self.ref.shape[0]):
            self.joint[c] = merged(self.strips, c, OWN)

    def own(self, c, z, tile):
        return self.ref[c, z + 1, tile, OWN]

    def around(self, z, tile):
        def pairs(c):
            ref = self.ref
            tiles = [ref[c, z + 1, t, OWN] for t in range(2)]
            if self.joint is None:
                edge = jnp.zeros_like(tiles[0])
            else:
                edge = edge_tile(self.joint[c], z)
            return (
                x_pair(tiles, tile, edge),
                (ref[c, z + 1, tile, BEHIND], ref[c, z + 1, tile, FRONT]),
                (ref[c, z, tile, OWN], ref[c, z + 2, tile, OWN]),
            )

        return pairs

    def strip_around(self, side):
        def pairs(c):
            cur = self.strips[c, side, OWN]
            return (
                strip_x(cur),
                (self.strips[c, side, BEHIND], self.strips[c, side, FRONT]),
                strip_z(cur),
            )

        return pairs

    def clear(self):
        last = self.ref.shape[1] - 1
        zero = jnp.zeros((8, LANES), F32)
        clear_planes(self.ref)

        def layer(z, carry):
            for c in range(self.ref.shape[0]):
                for tile in range(2):
                    self.ref[c, z, tile, 0:8] = zero
                    self.ref[c, z, tile, 24:32] = zero
            return carry

        lax.fori_loop(1, last, layer, 0)

    def clear_strips(self):
        zero = jnp.zeros((8, LANES), F32)
        for c in range(self.strips.shape[0]):
            for side in range(2):
                self.strips[c, side, 0:8] = zero
                self.strips[c, side, 24:32] = zero


def clear_planes(ref, planes=None):
    last = ref.shape[1] - 1
    for c in planes or range(ref.shape[0]):
        for tile in range(2):
            for z in (0, last):
                ref[c, z, tile] = jnp.zeros(ref.shape[3:], F32)


def line(z, place, count, layers):
    if z is None:
        return slice(count * layers + place, count * layers + place + 1)
    return pl.ds(place * layers + z, 1)


def planes(place, layers):
    return slice(place * layers, (place + 1) * layers)


def row_place(ref, c, tile, row):
    high, rows = ref.shape[-4], ref.shape[-2]
    total = 1
    for size in ref.shape[:-1]:
        total *= size
    at = ((c * high + 1) * 2 + tile) * rows + row
    return ref.reshape(total, LANES), pl.ds(at, high - 2, stride=2 * rows)


def row_of(ref, c, tile, row):
    flat, place = row_place(ref, c, tile, row)
    return flat[place, :]


def set_row(ref, c, tile, row, value):
    flat, place = row_place(ref, c, tile, row)
    flat[place, :] = value


def layer_pair(cur):
    row, last = row_iota(cur.shape), cur.shape[0] - 1
    behind = jnp.where(row == 0, 0.0, pltpu.roll(cur, 1, 0))
    front = jnp.where(row == last, 0.0, pltpu.roll(cur, last, 0))
    return behind, front


def edge_column(left, right, layers):
    shape = (layers, LANES)
    lane, layer = lane_iota(shape), row_iota(shape)
    low = jnp.sum(jnp.where(lane == 8 * layer + HALO - 1, left, 0.0), axis=1, keepdims=True)
    high = jnp.sum(jnp.where(lane == 8 * layer + HALO, right, 0.0), axis=1, keepdims=True)
    return jnp.where(lane == LANES - 1, low, jnp.where(lane == 0, high, 0.0))


def back_wind(coef, uy, edge_x, z, tile):
    tiles = [coef[UX, z + 1, t] for t in range(2)]
    return (
        x_pair(tiles, tile, edge_tile(edge_x, z)),
        (uy[z + 1, tile, BEHIND], uy[z + 1, tile, FRONT]),
        (coef[UZ, z, tile], coef[UZ, z + 2, tile]),
    )


def strip_back_wind(coef, uy, side):
    return (
        strip_x(coef[UX, side]),
        (uy[side, BEHIND], uy[side, FRONT]),
        strip_z(coef[UZ, side]),
    )


def pack_kernel(
    axis_cd,
    s0,
    vel,
    grad,
    rot,
    tgt,
    needle,
    out,
    first,
    second,
    field,
    coef,
    base,
    uy,
    stage,
    needle_stage,
    sems,
    needle_sem,
):
    layers = stage.shape[1]
    blocks = sems.shape[0]
    deep = layers // blocks
    sources = (s0, vel, grad, rot, tgt)

    def copies(block):
        slot, found = 0, []
        for number, ref in enumerate(sources):
            depth = pl.ds(block * deep, deep)
            target = stage.at[pl.ds(slot, ref.shape[0]), depth]
            found.append(
                pltpu.make_async_copy(ref.at[:, depth], target, sems.at[block, number])
            )
            slot += ref.shape[0]
        return found

    for block in range(blocks):
        for copy in copies(block):
            copy.start()
    needle_copy = pltpu.make_async_copy(needle, needle_stage, needle_sem)
    needle_copy.start()
    lane = lane_iota(out.shape[1:])
    Field(field, None).clear()
    clear_planes(coef, [UZ])

    def load(z, carry):
        zero = jnp.zeros((8, LANES), F32)
        for tile in range(2):
            for c in range(5):
                field[c, z + 1, tile, OWN] = stage[c, z, :, span(tile)]
            u = [DT * stage[VEL + d, z, :, span(tile)] for d in range(3)]
            turn = DT * stage[ROT, z, :, span(tile)]
            parts = gradient_parts(lambda i: stage[GRAD + i, z, :, span(tile)])
            for key, value in parts.items():
                coef[PLACE[key], z + 1, tile] = value
            coef[SPREAD, z + 1, tile] = 2.0 * turn
            coef[UX, z + 1, tile] = u[0]
            coef[UZ, z + 1, tile] = u[2]
            uy[z + 1, tile, 0:8] = zero
            uy[z + 1, tile, 24:32] = zero
            uy[z + 1, tile, OWN] = u[1]
            base[z + 1, tile] = 6.0 * turn + (jnp.abs(u[0]) + jnp.abs(u[1]) + jnp.abs(u[2]))
        return carry


    def step(block, carry):
        for copy in copies(block):
            copy.wait()
        for c in range(NEEDLES):
            total = out[c]
            for k in range(deep):
                z = block * deep + k
                low, high = stage[c, z, :, span(0)], stage[c, z, :, span(1)]
                both = jnp.where(lane < HALO, low, high)
                moved = pltpu.roll(both, (8 * z + HALO) % LANES, 1)
                total = jnp.where(lane // 8 == z, moved, total)
            out[c] = total
        lax.fori_loop(block * deep, (block + 1) * deep, load, 0)
        return carry

    lax.fori_loop(0, blocks, step, 0)

    odd = lax.axis_index(axis_cd) % 2 == 1
    outer = lane % 8 < HALO
    needle_copy.wait()
    first[PAIRS] = needle_stage[...]
    second[PAIRS] = needle_stage[...]
    for c in range(PAIRS):
        here, other = out[c], out[min(c + PAIRS, NEEDLES - 1)]
        to_right = jnp.where(outer, here, pltpu.roll(other, HALO, 1))
        to_left = jnp.where(outer, pltpu.roll(other, LANES - HALO, 1), here)
        first[c] = jnp.where(odd, to_left, to_right)
        second[c] = jnp.where(odd, to_right, to_left)


def bulk_kernel(field, coef, base, uy, s1):
    layers = field.shape[1] - 2
    state = Field(field, None)

    def advance(z, carry):
        for tile in range(2):
            at = (z + 1, tile)
            m, damp = coefficients(coef, base, *at)
            wind = (coef[(UX,) + at], uy[at + (OWN,)], coef[(UZ,) + at])
            a = [state.own(c, z, tile) for c in range(5)]
            out = forward(a, m, damp, coef[(SPREAD,) + at], wind, state.around(z, tile))
            for c in range(5):
                s1[c, z + 1, tile, OWN] = out[c]
        return carry

    lax.fori_loop(0, layers, advance, 0, unroll=2)


def choose(axis_md, low, high, first, second):
    odd = lax.axis_index(axis_md) % 2 == 1
    first[...] = jnp.where(odd, high[...], low[...])
    second[...] = jnp.where(odd, low[...], high[...])


def split_three(value):
    parts = []
    for _ in range(3):
        part = value.astype(jnp.bfloat16).astype(F32)
        parts.append(part)
        value = value - part
    return parts


def feet_block(ref, block, count):
    place = jnp.clip(block, 0, count - 1) * LANES
    row = ref[:, pl.ds(pl.multiple_of(place, LANES), LANES)]
    return jnp.where((block >= 0) & (block < count), row, 0)


def first_kernel(
    axis_md,
    axis_cd,
    own,
    needle,
    near_first,
    near_second,
    far,
    start,
    end,
    column,
    field,
    coef,
    uy,
    s1,
    gain,
    strip_s0,
    strip_coef,
    strip_base,
    strip_uy,
    strip_s1,
    strip_tgt,
    up,
    down,
    sent_first,
    sent_second,
    spread,
    cover,
    source,
):
    layers = field.shape[1] - 2
    height = own.shape[1]
    md = lax.axis_index(axis_md)
    count = lax.axis_size(axis_md)
    lane = lane_iota((height, LANES))
    outer = lane % 8 < HALO
    odd = lax.axis_index(axis_cd) % 2 == 1

    def from_left(c):
        return jnp.where(odd, near_second[c], near_first[c])

    def from_right(c):
        return jnp.where(odd, near_first[c], near_second[c])

    def half(take, c, turn):
        return take(c) if c < PAIRS else pltpu.roll(take(c - PAIRS), turn, 1)

    def feet(ref):
        return jnp.concatenate(
            [feet_block(ref, md + d, count) for d in (-1, 0, 1, 2)], axis=1
        )

    starts, ends, columns = feet(start), feet(end), feet(column)
    rates = jnp.concatenate(
        [from_left(PAIRS), needle[...], from_right(PAIRS), far[...]], axis=1
    )
    needles = rates.shape[1]
    picked = jnp.where(row_iota((height, needles)) == columns, 1.0, 0.0)
    for part, value in enumerate(split_three(rates)):
        for z in range(layers):
            spread[part, z * height : (z + 1) * height] = (picked * value[z : z + 1]).astype(
                jnp.bfloat16
            )
    length = 2 * LANES
    cells = row_iota((length + LANES, needles))
    beyond = cells - length
    strip = jnp.where(beyond < 8, beyond - HALO, beyond - 8 + length - HALO)
    cells = jnp.where(cells < length, cells, strip) + md * length
    cover[...] = jnp.where((cells >= starts) & (cells < ends), 1.0, 0.0).astype(jnp.bfloat16)
    product = jnp.zeros((layers * height, length + LANES), F32)
    for part in range(3):
        product = product + lax.dot_general(
            spread[part], cover[...], (((1,), (1,)), ((), ())), preferred_element_type=F32
        )
    product = DT * product
    for tile in range(2):
        gain[1 : layers + 1, tile] = product[:, span(tile)].reshape(layers, height, LANES)
    source[...] = product[:, span(2)].reshape(source.shape)

    state = Field(field, strip_s0)
    state.clear_strips()
    has_left, has_right = md > 0, md < count - 1
    for side in range(2):

        def raw(c):
            if side == 0:
                return jnp.where(outer, jnp.where(has_left, half(from_left, c, LANES - HALO), 0.0), own[c])
            return jnp.where(outer, own[c], jnp.where(has_right, half(from_right, c, HALO), 0.0))

        for c in range(5):
            strip_s0[c, side, OWN] = raw(S0 + c)
            strip_tgt[c, side] = raw(TGT + c)
        u = [DT * raw(VEL + d) for d in range(3)]
        turn = DT * raw(ROT)
        for key, value in gradient_parts(lambda i: raw(GRAD + i)).items():
            strip_coef[PLACE[key], side] = value
        strip_coef[SPREAD, side] = 2.0 * turn
        strip_coef[UX, side] = u[0]
        strip_coef[UZ, side] = u[2]
        strip_uy[side, 0:8] = jnp.zeros((8, LANES), F32)
        strip_uy[side, 24:32] = jnp.zeros((8, LANES), F32)
        strip_uy[side, OWN] = u[1]
        damp = 6.0 * turn + (jnp.abs(u[0]) + jnp.abs(u[1]) + jnp.abs(u[2]))
        taken = jnp.zeros((height, LANES), F32)
        for z in range(layers):
            moved = pltpu.roll(source[z], (8 * z - 8 * side) % LANES, 1)
            taken = jnp.where(lane // 8 == z, moved, taken)
        strip_base[side] = damp + taken

    for side in range(2):
        m, damp = coefficients(strip_coef, strip_base, side)
        wind = (strip_coef[UX, side], strip_uy[side, OWN], strip_coef[UZ, side])
        a = [strip_s0[c, side, OWN] for c in range(5)]
        spin = strip_coef[SPREAD, side]
        out = forward(a, m, damp, spin, wind, state.strip_around(side))
        for c in range(5):
            strip_s1[c, side, OWN] = out[c]

    def put(side):
        def at(place):
            return line(None, side * 11 + place, 22, layers)

        for c in range(5):
            first, new = strip_s0.at[c, side], strip_s1.at[c, side]
            up[at(c)], down[at(c)] = first[23:24], first[8:9]
            up[at(5 + c)], down[at(5 + c)] = new[23:24], new[8:9]
        wind = strip_uy.at[side]
        up[at(10)] = -jnp.minimum(wind[23:24], 0.0)
        down[at(10)] = jnp.maximum(wind[8:9], 0.0)

    for message, row in ((up, 15), (down, 0)):
        for tile in range(2):
            u = row_of(coef, UX, tile, row)
            if tile == 0:
                weight, turn = jnp.where(lane == 0, jnp.maximum(u, 0.0), 0.0), 1
            else:
                weight = jnp.where(lane == LANES - 1, -jnp.minimum(u, 0.0), 0.0)
                turn = LANES - 1
            gained = row_of(gain, 0, tile, row)
            for c in range(5):
                left, right = (strip_s0[c, side, 8 + row : 9 + row] for side in (0, 1))
                edge = pltpu.roll(edge_column(left, right, layers), turn, 1)
                old = row_of(field, c, tile, 8 + row)
                new = row_of(s1, c, tile, 8 + row) - gained * old + weight * edge
                message[planes(tile * 11 + c, layers)] = old
                message[planes(tile * 11 + 5 + c, layers)] = new
            speed = row_of(uy, 0, tile, 8 + row)
            outward = -jnp.minimum(speed, 0.0) if row else jnp.maximum(speed, 0.0)
            message[planes(tile * 11 + 10, layers)] = outward
    for side in range(2):
        put(side)
    choose(axis_md, up, down, sent_first, sent_second)


def cd_flags(axis_cd):
    cd = lax.axis_index(axis_cd)
    return cd > 0, cd < lax.axis_size(axis_cd) - 1


def advance_kernel(
    s1_in,
    field,
    gain,
    coef,
    base_in,
    uy,
    tgt,
    strip_s0,
    strip_s1,
    strip_coef,
    strip_base,
    strip_uy,
    strip_tgt,
    s1,
    base,
    s2,
    goal,
    adj1,
    dots,
    adj2,
    strip_adj2,
    joint,
    joint1,
    joint2,
):
    layers, height = tgt.shape[1], tgt.shape[2]
    lane = lane_iota((height, LANES))
    start = Field(field, strip_s0, joint)
    state = Field(s1, strip_s1, joint1)
    delta = Field(adj2, strip_adj2, joint2)
    start.join()
    state.join()
    clear_planes(s1)
    clear_planes(adj2)
    for side in range(2):
        m, damp = coefficients(strip_coef, strip_base, side)
        wind = (strip_coef[UX, side], strip_uy[side, OWN], strip_coef[UZ, side])
        a = [strip_s1[c, side, OWN] for c in range(5)]
        spin = strip_coef[SPREAD, side]
        out = forward(a, m, damp, spin, wind, state.strip_around(side))
        for c in range(5):
            strip_adj2[c, side, OWN] = out[c] - strip_tgt[c, side]
    delta.join()

    def mend(z, carry):
        for tile in range(2):
            gained = gain[z + 1, tile]
            base[z + 1, tile] = base_in[z + 1, tile] + gained
            u = coef[UX, z + 1, tile]
            if tile == 0:
                weight, turn = jnp.where(lane == 0, jnp.maximum(u, 0.0), 0.0), 1
            else:
                weight, turn = jnp.where(lane == LANES - 1, -jnp.minimum(u, 0.0), 0.0), -1
            for c in range(5):
                edge = pltpu.roll(joint[c], (2 * LANES - HALO + turn - 8 * z) % LANES, 1)
                s1[c, z + 1, tile, OWN] = (
                    s1_in[c, z + 1, tile, OWN]
                    - gained * field[c, z + 1, tile, OWN]
                    + weight * edge
                )
        return carry

    lax.fori_loop(0, layers, mend, 0, unroll=2)

    def advance(z, carry):
        for tile in range(2):
            at = (z + 1, tile)
            m, damp = coefficients(coef, base, *at)
            wind = (coef[(UX,) + at], uy[at + (OWN,)], coef[(UZ,) + at])
            a = [state.own(c, z, tile) for c in range(5)]
            out = forward(a, m, damp, coef[(SPREAD,) + at], wind, state.around(z, tile))
            total = 0.0
            for c in range(5):
                wanted = tgt[c, z, :, span(tile)]
                miss = out[c] - wanted
                s2[(c,) + at] = out[c]
                goal[(c,) + at] = wanted
                adj2[(c,) + at + (OWN,)] = miss
                total = total + miss * a[c]
            dots[at] = total
        return carry

    lax.fori_loop(0, layers, advance, 0, unroll=2)
    edge_x = merged(strip_coef, UX, slice(None))

    def retreat(z, carry):
        for tile in range(2):
            m, damp = coefficients(coef, base, z + 1, tile)
            a = [state.own(c, z, tile) for c in range(5)]
            b = [delta.own(c, z, tile) for c in range(5)]
            wind = back_wind(coef, uy, edge_x, z, tile)
            out = backward(b, a, m, damp, wind, delta.around(z, tile))
            for c in range(5):
                adj1[c, z + 1, tile] = out[c]
        return carry

    lax.fori_loop(0, layers, retreat, 0, unroll=2)


def edge_kernel(
    axis_md,
    axis_cd,
    s1,
    strip_s1_in,
    coef,
    base,
    uy,
    goal,
    strip_coef,
    strip_base,
    strip_uy,
    strip_tgt,
    own_up,
    own_down,
    got_first,
    got_second,
    s2_edge,
    adj2_edge,
    adj1_edge,
    dots_edge,
    strip_adj2,
    strip_adj1,
    up,
    down,
    sent_first,
    sent_second,
    from_below,
    from_above,
    strip_s1,
):
    layers = goal.shape[1] - 2
    has_below, has_above = cd_flags(axis_cd)
    choose(axis_md, got_first, got_second, from_below, from_above)

    state, delta = Field(s1, strip_s1), Field(s1, strip_adj2)
    delta.clear_strips()
    for side in range(2):

        def at(place):
            return line(None, side * 11 + place, 22, layers)

        wind = strip_uy.at[side]
        low_u, high_u = jnp.maximum(wind[8:9], 0.0), -jnp.minimum(wind[23:24], 0.0)
        low_n, high_n = from_below[at(10)], from_above[at(10)]
        for c in range(5):
            old, new = at(c), at(5 + c)
            ref = strip_s1.at[c, side]
            ref[OWN] = strip_s1_in[c, side, OWN]
            low = from_below[new] + low_n * own_down[old]
            high = from_above[new] + high_n * own_up[old]
            ref[7:8] = jnp.where(has_below, low, 0.0)
            ref[24:25] = jnp.where(has_above, high, 0.0)
            ref[8:9] = ref[8:9] + jnp.where(has_below, low_u * from_below[old], 0.0)
            ref[23:24] = ref[23:24] + jnp.where(has_above, high_u * from_above[old], 0.0)
    for side in range(2):
        m, damp = coefficients(strip_coef, strip_base, side)
        wind = (strip_coef[UX, side], strip_uy[side, OWN], strip_coef[UZ, side])
        a = [strip_s1[c, side, OWN] for c in range(5)]
        spin = strip_coef[SPREAD, side]
        out = forward(a, m, damp, spin, wind, state.strip_around(side))
        for c in range(5):
            strip_adj2[c, side, OWN] = out[c] - strip_tgt[c, side]
    for side in range(2):

        def at(place):
            return line(None, side * 10 + place, 20, layers)

        m, damp = coefficients(strip_coef, strip_base, side)
        a = [strip_s1[c, side, OWN] for c in range(5)]
        b = [strip_adj2[c, side, OWN] for c in range(5)]
        wind = strip_back_wind(strip_coef, strip_uy, side)
        out = backward(b, a, m, damp, wind, delta.strip_around(side))
        high = -jnp.minimum(strip_uy[side, 23:24], 0.0)
        low = jnp.maximum(strip_uy[side, 8:9], 0.0)
        for c in range(5):
            strip_adj1[c, side, OWN] = out[c]
            up[at(c)] = high * b[c][-1:]
            down[at(c)] = low * b[c][:1]
            up[at(5 + c)] = high * out[c][-1:]
            down[at(5 + c)] = low * out[c][:1]

    def constants(tile, row):
        m = {key: row_of(coef, place, tile, row) for key, place in PLACE.items()}
        return m, row_of(base, 0, tile, row)

    for number, (message, mine, valid, outgoing) in enumerate(
        ((from_below, own_down, has_below, down), (from_above, own_up, has_above, up))
    ):
        rows = (0, 1, 2) if number == 0 else (15, 14, 13)
        sides = (0, 1)

        def plane(ref, place, tile):
            return ref[planes(tile * 11 + place, layers)]

        lines = [{}, {}, {}, {}]
        for c in range(5):
            for tile in range(2):
                old, new = plane(message, c, tile), plane(message, 5 + c, tile)
                weight = plane(message, 10, tile)
                lines[0][c, tile] = jnp.where(
                    valid, new + weight * plane(mine, c, tile), 0.0
                )
                lines[1][c, tile] = plane(mine, 5 + c, tile) + jnp.where(
                    valid, plane(mine, 10, tile) * old, 0.0
                )
                for k in (1, 2):
                    lines[k + 1][c, tile] = row_of(s1, c, tile, 8 + rows[k])

        def strip_edge(ref, c, row):
            left, right = (ref[c, side, 8 + row : 9 + row] for side in sides)
            return edge_column(left, right, layers)

        def ordered(outer, inner):
            return (outer, inner) if number == 0 else (inner, outer)

        misses = [{}, {}]
        for k in range(2):
            row = rows[k]
            edges = [strip_edge(strip_s1, c, row) for c in range(5)]
            for tile in range(2):
                m, damp = constants(tile, row)
                wind = (
                    row_of(coef, UX, tile, row),
                    row_of(uy, 0, tile, 8 + row),
                    row_of(coef, UZ, tile, row),
                )
                a = [lines[k + 1][c, tile] for c in range(5)]

                def around(c):
                    tiles = [lines[k + 1][c, t] for t in range(2)]
                    return (
                        x_pair(tiles, tile, edges[c]),
                        ordered(lines[k][c, tile], lines[k + 2][c, tile]),
                        layer_pair(a[c]),
                    )

                out = forward(a, m, damp, row_of(coef, SPREAD, tile, row), wind, around)
                total = 0.0
                for c in range(5):
                    miss = out[c] - row_of(goal, c, tile, row)
                    s2_edge[c, 2 * number + k, tile] = out[c]
                    adj2_edge[c, 2 * number + k, tile] = miss
                    misses[k][c, tile] = miss
                    total = total + miss * a[c]
                dots_edge[2 * number + k, tile] = total

        row = rows[0]
        edges = [strip_edge(strip_adj2, c, row) for c in range(5)]
        left, right = (strip_coef[UX, side, row : row + 1] for side in sides)
        edge_x = edge_column(left, right, layers)
        for tile in range(2):
            m, damp = constants(tile, row)
            a = [lines[1][c, tile] for c in range(5)]
            b = [misses[0][c, tile] for c in range(5)]
            zero = jnp.zeros_like(b[0])
            wind = (
                x_pair([row_of(coef, UX, t, row) for t in range(2)], tile, edge_x),
                ordered(zero, row_of(uy, 0, tile, 8 + rows[1])),
                layer_pair(row_of(coef, UZ, tile, row)),
            )

            def around(c):
                tiles = [misses[0][c, t] for t in range(2)]
                return (
                    x_pair(tiles, tile, edges[c]),
                    ordered(zero, misses[1][c, tile]),
                    layer_pair(b[c]),
                )

            out = backward(b, a, m, damp, wind, around)
            weight = plane(mine, 10, tile)
            for c in range(5):
                outgoing[planes(tile * 10 + c, layers)] = weight * b[c]
                outgoing[planes(tile * 10 + 5 + c, layers)] = weight * out[c]
                adj1_edge[c, number, tile] = out[c]
    choose(axis_md, up, down, sent_first, sent_second)


def needle_feet(ref, md, count):
    return jnp.concatenate([feet_block(ref, md + d, count) for d in (-1, 0, 1)], axis=1)


def own_cover(md, length, starts, ends):
    cells = row_iota((length, starts.shape[1])) + md * length
    return jnp.where((cells >= starts) & (cells < ends), 1.0, 0.0).astype(jnp.bfloat16)


def covered_sum(values, cover):
    product = jnp.zeros((values.shape[0], cover.shape[1]), F32)
    for part in split_three(values):
        product = product + jnp.dot(
            part.astype(jnp.bfloat16), cover, preferred_element_type=F32
        )
    return product


def second_kernel(
    axis_md,
    s1,
    s2_in,
    goal,
    adj1_in,
    dots_in,
    s2_edge,
    adj2_edge,
    adj1_edge,
    dots_edge,
    field,
    coef,
    base,
    uy,
    strip_coef,
    strip_adj2,
    strip_adj1,
    start,
    end,
    column,
    s2_out,
    adj0,
    gained,
    adj1,
    dots,
    sens,
    s2,
    joint,
):
    layers, height = goal.shape[1] - 2, goal.shape[3]
    length = 2 * LANES
    md = lax.axis_index(axis_md)
    count = lax.axis_size(axis_md)

    def gather(z, carry):
        for tile in range(2):
            dots[z + 1, tile] = dots_in[z + 1, tile]
            for c in range(5):
                s2[c, z + 1, tile] = s2_in[c, z + 1, tile]
                adj1[c, z + 1, tile, OWN] = adj1_in[c, z + 1, tile]
        return carry

    lax.fori_loop(0, layers, gather, 0, unroll=2)
    for tile in range(2):
        for number, row in enumerate((0, 1, 15, 14)):
            set_row(dots, 0, tile, row, dots_edge[number, tile])
            for c in range(5):
                set_row(s2, c, tile, row, s2_edge[c, number, tile])
        for number, row in enumerate((0, 15)):
            for c in range(5):
                set_row(adj1, c, tile, 8 + row, adj1_edge[c, number, tile])

    for number, rows in enumerate(((0, 1, 2, 3), (15, 14, 13, 12))):
        lines = [{}, {}, {}, {}]
        for c in range(5):
            for tile in range(2):
                for k in (0, 1):
                    lines[k][c, tile] = adj2_edge[c, 2 * number + k, tile]
                for k in (2, 3):
                    state = row_of(s2_in, c, tile, rows[k])
                    lines[k][c, tile] = state - row_of(goal, c, tile, rows[k])

        def ordered(outer, inner):
            return (outer, inner) if number == 0 else (inner, outer)

        for k in (1, 2):
            row = rows[k]
            edges = []
            for c in range(5):
                left, right = (strip_adj2[c, side, 8 + row : 9 + row] for side in (0, 1))
                edges.append(edge_column(left, right, layers))
            left, right = (strip_coef[UX, side, row : row + 1] for side in (0, 1))
            edge = edge_column(left, right, layers)
            for tile in range(2):
                m = {key: row_of(coef, place, tile, row) for key, place in PLACE.items()}
                damp = row_of(base, 0, tile, row)
                a = [row_of(s1, c, tile, 8 + row) for c in range(5)]
                b = [lines[k][c, tile] for c in range(5)]
                wind = (
                    x_pair([row_of(coef, UX, t, row) for t in range(2)], tile, edge),
                    ordered(*(row_of(uy, 0, tile, 8 + rows[i]) for i in (k - 1, k + 1))),
                    layer_pair(row_of(coef, UZ, tile, row)),
                )

                def around(c):
                    return (
                        x_pair([lines[k][c, t] for t in range(2)], tile, edges[c]),
                        ordered(lines[k - 1][c, tile], lines[k + 1][c, tile]),
                        layer_pair(b[c]),
                    )

                out = backward(b, a, m, damp, wind, around)
                for c in range(5):
                    set_row(adj1, c, tile, 8 + row, out[c])

    def write(z, carry):
        for tile in range(2):
            for c in range(5):
                s2_out[c, z, :, span(tile)] = s2[c, z + 1, tile]
        return carry

    lax.fori_loop(0, layers, write, 0, unroll=2)
    edge_x = merged(strip_coef, UX, slice(None))
    last_delta = Field(adj1, strip_adj1, joint)
    last_delta.clear()
    last_delta.join()

    def finish(z, carry):
        for tile in range(2):
            m, damp = coefficients(coef, base, z + 1, tile)
            a = [field[c, z + 1, tile, OWN] for c in range(5)]
            b = [last_delta.own(c, z, tile) for c in range(5)]
            wind = back_wind(coef, uy, edge_x, z, tile)
            out = backward(b, a, m, damp, wind, last_delta.around(z, tile))
            total = dots[z + 1, tile]
            for c in range(5):
                adj0[c, z + 1, tile] = out[c]
                total = total + a[c] * b[c]
            sens[z, :, span(tile)] = -DT * total
        return carry

    lax.fori_loop(0, layers, finish, 0, unroll=2)
    starts, ends, columns = (needle_feet(ref, md, count) for ref in (start, end, column))
    cover = own_cover(md, length, starts, ends)
    product = covered_sum(sens[...].reshape(layers * height, length), cover)
    picked = jnp.where(row_iota((height, starts.shape[1])) == columns, 1.0, 0.0)
    for z in range(layers):
        gained[z : z + 1] = jnp.sum(
            product[z * height : (z + 1) * height] * picked, axis=0, keepdims=True
        )


def third_kernel(
    axis_md,
    axis_cd,
    gained,
    field,
    got_first,
    got_second,
    start,
    end,
    column,
    first,
    kept,
    second,
    from_below,
    from_above,
):
    choose(axis_md, got_first, got_second, from_below, from_above)
    layers = field.shape[1] - 2
    length = 2 * LANES
    md = lax.axis_index(axis_md)
    count = lax.axis_size(axis_md)
    odd = lax.axis_index(axis_cd) % 2 == 1
    lines = []
    for message, valid, row in zip((from_below, from_above), cd_flags(axis_cd), (8, 23)):
        parts = []
        for tile in range(2):
            total = 0.0
            for c in range(5):
                brought = message[planes(tile * 10 + c, layers)]
                total = total + brought * row_of(field, c, tile, row)
            parts.append(jnp.where(valid, -DT * total, 0.0))
        lines.append(jnp.concatenate(parts, axis=1))
    starts, ends, columns = (needle_feet(ref, md, count) for ref in (start, end, column))
    cover = own_cover(md, length, starts, ends)
    product = covered_sum(jnp.concatenate(lines, axis=0), cover)
    total = gained[...]
    for number, row in enumerate((0, 15)):
        here = product[number * layers : (number + 1) * layers]
        total = total + jnp.where(columns == row, here, 0.0)
    first[...] = jnp.where(odd, total[:, span(0)], total[:, span(2)])
    kept[...] = total[:, span(1)]
    second[...] = jnp.where(odd, total[:, span(2)], total[:, span(0)])


def fourth_kernel(
    axis_cd,
    adj0_in,
    field,
    coef,
    base,
    uy,
    strip_coef,
    weights_below,
    weights_above,
    own_up,
    own_down,
    from_below,
    from_above,
    out_field,
    adj0,
):
    layers = field.shape[1] - 2
    has_below, has_above = cd_flags(axis_cd)

    def gather(z, carry):
        for tile in range(2):
            for c in range(5):
                adj0[c, z + 1, tile] = adj0_in[c, z + 1, tile]
        return carry

    lax.fori_loop(0, layers, gather, 0, unroll=2)

    for number, (weights, message, mine, valid) in enumerate(
        (
            (weights_below, from_below, own_down, has_below),
            (weights_above, from_above, own_up, has_above),
        )
    ):
        row, inner = ((0, 1), (15, 14))[number]
        brought = {}
        for c in range(5):
            for tile in range(2):
                value = message[planes(tile * 10 + c, layers)]
                brought[c, tile] = jnp.where(valid, value, 0.0)
        edges = []
        for c in range(5):
            left, right = (message[line(None, side * 10 + c, 20, layers)] for side in (0, 1))
            edges.append(jnp.where(valid, edge_column(left, right, layers), 0.0))
        left, right = (strip_coef[UX, side, row : row + 1] for side in (0, 1))
        edge_x = edge_column(left, right, layers)
        for tile in range(2):
            m = {key: row_of(coef, place, tile, row) for key, place in PLACE.items()}
            damp = row_of(base, 0, tile, row)
            a = [row_of(field, c, tile, 8 + row) for c in range(5)]
            b = [brought[c, tile] for c in range(5)]
            wind = (
                x_pair([row_of(coef, UX, t, row) for t in range(2)], tile, edge_x),
                layer_pair(row_of(coef, UZ, tile, row)),
            )

            def around(c):
                tiles = [brought[c, t] for t in range(2)]
                return x_pair(tiles, tile, edges[c]), layer_pair(b[c])

            out = backward(b, a, m, damp, wind, around)
            speed = row_of(uy, 0, tile, 8 + row)
            inward = -jnp.minimum(speed, 0.0) if number == 0 else jnp.maximum(speed, 0.0)
            weight = weights[planes(tile * 11 + 10, layers)]
            for c in range(5):
                own = mine[planes(tile * 10 + c, layers)]
                far = message[planes(tile * 10 + 5 + c, layers)] + weight * own
                total = out[c] + jnp.where(valid, far, 0.0)
                set_row(adj0, c, tile, row, row_of(adj0, c, tile, row) + total)
                more = inward * b[c]
                set_row(adj0, c, tile, inner, row_of(adj0, c, tile, inner) + more)

    def scatter(z, carry):
        for tile in range(2):
            for c in range(5):
                out_field[c, z, :, span(tile)] = adj0[c, z + 1, tile]
        return carry

    lax.fori_loop(0, layers, scatter, 0, unroll=2)


def ring(value, axis, steps):
    count = lax.axis_size(axis)
    return lax.ppermute(value, axis, [(i, (i + steps) % count) for i in range(count)])


def winding(value, steps, turn):
    rows, columns = lax.axis_size("md"), lax.axis_size("cd")
    pairs = []
    for column in range(columns):
        for row in range(rows):
            target = row + (steps if column % 2 == turn else -steps)
            if 0 <= target < rows:
                pairs.append((row * columns + column, target * columns + column))
            else:
                pairs.append((row * columns + column, row * columns + (column ^ 1)))
    return lax.ppermute(value, ("md", "cd"), pairs)


def weaving(value, turn):
    rows, columns = lax.axis_size("md"), lax.axis_size("cd")
    pairs = []
    for row in range(rows):
        for column in range(columns):
            target = column + (1 if row % 2 == turn else -1)
            if 0 <= target < columns:
                pairs.append((row * columns + column, row * columns + target))
            else:
                pairs.append((row * columns + column, (row ^ 1) * columns + column))
    return lax.ppermute(value, ("md", "cd"), pairs)


def shape_of(*dims, dtype=F32):
    return jax.ShapeDtypeStruct(dims, dtype)


def scratch(*dims, dtype=F32):
    return pltpu.VMEM(dims, dtype)


def cost(microseconds):
    return pl.CostEstimate(
        flops=int(microseconds * 1e6), bytes_accessed=int(microseconds * 3e6), transcendentals=0
    )


def params(mebibytes):
    return pltpu.CompilerParams(vmem_limit_bytes=mebibytes * 1024 * 1024)


def local(orientation, velocity, velocity_grad, rotary, target, needle_params, *feet):
    _, layers, height, length = orientation.shape
    rotary = rotary[None]
    rates = jnp.transpose(needle_params[:, 0, :])
    feet = [foot.reshape(1, -1) for foot in feet]
    padded = (layers + 2, 2, ROWS, LANES)
    plain = (layers + 2, 2, height, LANES)
    strip_padded, strip = (2, ROWS, LANES), (2, height, LANES)
    message, back_message = shape_of(22 * layers + 24, LANES), shape_of(20 * layers + 24, LANES)
    joint = scratch(5, height, LANES)

    hbm = pl.BlockSpec(memory_space=pltpu.HBM)
    blocks = 4
    packed, first, second, field, coef, base, uy = pl.pallas_call(
        functools.partial(pack_kernel, "cd"),
        in_specs=[hbm] * 6,
        out_shape=[
            shape_of(NEEDLES, height, LANES),
            shape_of(PAIRS + 1, height, LANES),
            shape_of(PAIRS + 1, height, LANES),
            shape_of(5, *padded),
            shape_of(COEFS, *plain),
            shape_of(*plain),
            shape_of(*padded),
        ],
        scratch_shapes=[
            scratch(NEEDLES, layers, height, length),
            scratch(*rates.shape),
            pltpu.SemaphoreType.DMA((blocks, 5)),
            pltpu.SemaphoreType.DMA,
        ],
        compiler_params=params(20),
        cost_estimate=cost(4),
    )(
        *(
            pltpu.with_memory_space_constraint(field, pltpu.HBM)
            for field in (orientation, velocity, velocity_grad, rotary, target, rates)
        )
    )
    far = lax.ppermute(rates, "md", [(i + 2, i) for i in range(lax.axis_size("md") - 2)])
    near = winding(first, 1, 0), winding(second, 1, 1)

    s1 = pl.pallas_call(
        bulk_kernel,
        out_shape=shape_of(5, *padded),
        compiler_params=params(16),
        cost_estimate=cost(2),
    )(field, coef, base, uy)

    gain, strip_s0, strip_coef, strip_base, strip_uy, strip_s1, strip_tgt, up, down, *sent = (
        pl.pallas_call(
            functools.partial(first_kernel, "md", "cd"),
            out_shape=[
                shape_of(*plain),
                shape_of(5, *strip_padded),
                shape_of(COEFS, *strip),
                shape_of(*strip),
                shape_of(*strip_padded),
                shape_of(5, *strip_padded),
                shape_of(5, *strip),
                *[message] * 4,
            ],
            scratch_shapes=[
                scratch(3, layers * height, 4 * LANES, dtype=jnp.bfloat16),
                scratch(length + LANES, 4 * LANES, dtype=jnp.bfloat16),
                scratch(layers, height, LANES),
            ],
            compiler_params=params(24),
            cost_estimate=cost(3),
        )(packed, rates, *near, far, *feet, field, coef, uy, s1)
    )
    got = weaving(sent[0], 0), weaving(sent[1], 1)

    s1, base, s2_part, goal, adj1_part, dots = pl.pallas_call(
        advance_kernel,
        out_shape=[
            shape_of(5, *padded),
            shape_of(*plain),
            shape_of(5, *plain),
            shape_of(5, *plain),
            shape_of(5, *plain),
            shape_of(*plain),
        ],
        scratch_shapes=[scratch(5, *padded), scratch(5, *strip_padded), joint, joint, joint],
        compiler_params=params(16),
        cost_estimate=cost(8),
    )(
        s1,
        field,
        gain,
        coef,
        base,
        uy,
        target,
        strip_s0,
        strip_s1,
        strip_coef,
        strip_base,
        strip_uy,
        strip_tgt,
    )
    edge_row = (2, layers, LANES)
    s2_edge, adj2_edge, adj1_edge, dots_edge, strip_adj2, strip_adj1, back_up, back_down, *more = (
        pl.pallas_call(
            functools.partial(edge_kernel, "md", "cd"),
            out_shape=[
                shape_of(5, 4, *edge_row),
                shape_of(5, 4, *edge_row),
                shape_of(5, 2, *edge_row),
                shape_of(4, *edge_row),
                shape_of(5, *strip_padded),
                shape_of(5, *strip_padded),
                *[back_message] * 4,
                message,
                message,
            ],
            scratch_shapes=[scratch(5, *strip_padded)],
            compiler_params=params(16),
            cost_estimate=cost(2),
        )(
            s1,
            strip_s1,
            coef,
            base,
            uy,
            goal,
            strip_coef,
            strip_base,
            strip_uy,
            strip_tgt,
            up,
            down,
            *got,
        )
    )
    back_sent, (below, above) = more[:2], more[2:]
    back_got = weaving(back_sent[0], 0), weaving(back_sent[1], 1)

    part = shape_of(*rates.shape)
    s2, adj0_part, gained = pl.pallas_call(
        functools.partial(second_kernel, "md"),
        out_shape=[
            shape_of(*orientation.shape),
            shape_of(5, *plain),
            shape_of(layers, 3 * LANES),
        ],
        scratch_shapes=[
            scratch(5, *padded),
            scratch(*plain),
            scratch(layers, height, length),
            scratch(5, *plain),
            joint,
        ],
        compiler_params=params(24),
        cost_estimate=cost(6),
    )(
        s1,
        s2_part,
        goal,
        adj1_part,
        dots,
        s2_edge,
        adj2_edge,
        adj1_edge,
        dots_edge,
        field,
        coef,
        base,
        uy,
        strip_coef,
        strip_adj2,
        strip_adj1,
        *feet,
    )

    part_first, part_own, part_second, back_below, back_above = pl.pallas_call(
        functools.partial(third_kernel, "md", "cd"),
        out_shape=[part, part, part, back_message, back_message],
        compiler_params=params(16),
        cost_estimate=cost(1),
    )(gained, field, *back_got, *feet)
    part_first = winding(part_first, 1, 0)
    part_second = winding(part_second, 1, 1)

    adj0 = pl.pallas_call(
        functools.partial(fourth_kernel, "cd"),
        out_shape=shape_of(*orientation.shape),
        scratch_shapes=[scratch(5, *plain)],
        compiler_params=params(16),
        cost_estimate=cost(2),
    )(
        adj0_part,
        field,
        coef,
        base,
        uy,
        strip_coef,
        below,
        above,
        back_up,
        back_down,
        back_below,
        back_above,
    )
    gradient = part_own + part_first + part_second
    return s2, adj0, jnp.transpose(gradient)[:, None, :]


def solution(mesh):
    field = P(None, None, "cd", "md")
    feet = P(None, "cd")
    needles = P("md", "cd", None)
    return jax.shard_map(
        local,
        mesh=mesh,
        in_specs=(field, field, field, P(None, "cd", "md"), field, needles, feet, feet, feet),
        out_specs=(field, field, needles),
        check_vma=False,
    )
```
